128 devices in a mesh: dp: 4 (over x_hi, core), seq: 32 (over y, z, x_lo).
Axes of the slice: x: 4 (x_hi: 2, x_lo: 2; x = x_hi * 2 + x_lo), y: 4, z: 4, core: 2. Of those that a mesh axis runs over, the one named last changes fastest.
Arguments:
- tokens: bfloat16 [4, 32768, 1024], P('dp', 'seq'), may hold values from -16 to 16
- out_grad: bfloat16 [4, 32768, 1024], P('dp', 'seq'), may hold values from -6 to 6
- w_query: bfloat16 [1024, 1024], replicated, may hold values from -0.1875 to 0.1875
- w_key: bfloat16 [1024, 1024], replicated, may hold values from -0.1875 to 0.1875
- w_value: bfloat16 [1024, 1024], replicated, may hold values from -0.1875 to 0.1875
- w_output: bfloat16 [1024, 1024], replicated, may hold values from -0.1875 to 0.1875
- grad_accum: float32 [1024, 4096], P(('dp', 'seq')), may hold values from -4 to 4
Outputs:
- in_grad: bfloat16 [4, 32768, 1024], P('dp', 'seq')
- new_accum: float32 [1024, 4096], P(('dp', 'seq'))
The draws below stay inside these ranges and needn't reach their ends.
All inputs are finite; a program needn't handle non-finite values.
Results may differ from the reference program's by a relative error of at most 0.015.
The reference program's roundings to bfloat16 on the way (of `probs_b`, `attended`, `att_grad`, `score_grad` and `query_grad`) count: a program that leaves them out, or rounds other values in their place, can miss the bound.
Values may be sent and summed in bfloat16 or wider, within the bound.
No kernel may reach another device: no remote copies, remote signals or barrier semaphores. Data moves between devices by JAX's collectives and lax.ppermute only.
A program may use at most 128 MiB of HBM per device.

```python
import math
import jax
import jax.numpy as jnp
from jax import lax

D = 1024
HD = 128
WIN = 256
RECS = 4
LEN = 32768


def draw_tokens(key, part):
    key = jax.random.fold_in(key, 7)
    first, second = jax.random.split(key)
    base = jax.random.normal(first, (RECS, LEN, D), jnp.float32)
    scales = jnp.exp(jax.random.uniform(second, (RECS, LEN, 1), jnp.float32, math.log(0.5), math.log(2.0)))
    return jnp.clip(base * scales, -16.0, 16.0).astype(jnp.bfloat16)


def block_levels(key, dims, cuts, low, largest):
    def one(dim, blocks):
        draws = jax.random.uniform(jax.random.fold_in(jax.random.fold_in(key, 6), dim), (blocks,), jnp.float32, low / len(cuts), largest / len(cuts))
        return jnp.repeat(jnp.exp(draws), dims[dim] // blocks).reshape((-1,) + (1,) * (len(dims) - dim - 1))

    loudness = one(*cuts[0])
    for cut in cuts[1:]:
        loudness = loudness * one(*cut)
    return loudness


def bell_draw(stream_key, dims, scale, most, cuts=(), kind=jnp.bfloat16):
    loudness = block_levels(stream_key, dims, cuts, -0.22, 0.18) if cuts else 1.0
    array = jax.random.normal(stream_key, dims, jnp.float32) * scale * loudness
    return jnp.minimum(jnp.maximum(array, -most), most).astype(kind)


def setup_inputs(seed: int = 0) -> dict:
    key_of = jax.random.split(jax.random.key(seed), 8)
    return {
        "tokens": draw_tokens(jax.random.fold_in(key_of[7], 71), 0),
        "out_grad": bell_draw(key_of[1], (RECS, LEN, D), 1.0, 6.0, ((0, 4), (1, 32))),
        "w_query": bell_draw(key_of[2], (D, D), D ** -0.5, 0.1875),
        "w_key": bell_draw(key_of[3], (D, D), D ** -0.5, 0.1875),
        "w_value": bell_draw(key_of[4], (D, D), D ** -0.5, 0.1875),
        "w_output": bell_draw(key_of[5], (D, D), D ** -0.5, 0.1875),
        "grad_accum": bell_draw(key_of[6], (D, 4 * D), 0.5, 4.0, ((0, 128),), jnp.float32),
    }


def attend(query_blk, key_win, value_win, grad_blk, allowed):
    qcount = query_blk.shape[0]
    kcount = key_win.shape[0]
    heads = query_blk.shape[1] // HD
    scale = 1.0 / (HD ** 0.5)
    query3 = query_blk.reshape(qcount, heads, HD).astype(jnp.float32)
    key3 = key_win.reshape(kcount, heads, HD).astype(jnp.float32)
    value3 = value_win.reshape(kcount, heads, HD).astype(jnp.float32)
    grad3 = grad_blk.reshape(qcount, heads, HD).astype(jnp.float32)
    scores = jnp.einsum("qhd,khd->hqk", query3, key3) * scale
    scores = jnp.where(allowed[None], scores, -1e30)
    top = jnp.max(scores, axis=-1, keepdims=True)
    lse = top + jnp.log(jnp.sum(jnp.exp(scores - top), axis=-1, keepdims=True))
    probs = jnp.exp(scores - lse)
    probs_b = probs.astype(jnp.bfloat16)
    attended = jnp.einsum("hqk,khd->qhd", probs_b.astype(jnp.float32), value3).astype(jnp.bfloat16)
    delta = jnp.einsum("qhd,qhd->hq", grad3, attended.astype(jnp.float32))[..., None]
    prob_grad = jnp.einsum("qhd,khd->hqk", grad3, value3)
    score_grad = (probs * (prob_grad - delta) * scale).astype(jnp.bfloat16).astype(jnp.float32)
    query_grad = jnp.einsum("hqk,khd->qhd", score_grad, key3).astype(jnp.bfloat16)
    key_part = jnp.einsum("hqk,qhd->khd", score_grad, query3)
    value_part = jnp.einsum("hqk,qhd->khd", probs_b.astype(jnp.float32), grad3)
    return (attended.reshape(qcount, -1), query_grad.reshape(qcount, -1),
            key_part.reshape(kcount, -1), value_part.reshape(kcount, -1))


def record_pass(tokens_rec, grad_rec, w_query, w_key, w_value, w_output):
    queries = jnp.dot(tokens_rec, w_query, preferred_element_type=jnp.float32).astype(jnp.bfloat16)
    keys_rec = jnp.dot(tokens_rec, w_key, preferred_element_type=jnp.float32).astype(jnp.bfloat16)
    values_rec = jnp.dot(tokens_rec, w_value, preferred_element_type=jnp.float32).astype(jnp.bfloat16)
    att_grad = jnp.dot(grad_rec, w_output.T, preferred_element_type=jnp.float32).astype(jnp.bfloat16)
    block = min(512, LEN)
    width = tokens_rec.shape[1]
    front = jnp.zeros((WIN, width), jnp.bfloat16)
    keys_pad = jnp.concatenate([front, keys_rec], axis=0)
    values_pad = jnp.concatenate([front, values_rec], axis=0)
    rows_idx = jnp.arange(block, dtype=jnp.int32)[:, None]
    cols_idx = jnp.arange(block + WIN, dtype=jnp.int32)[None, :]

    def step(carry, block_index):
        key_acc, value_acc = carry
        start = (block_index * block).astype(jnp.int32)
        query_blk = lax.dynamic_slice_in_dim(queries, start, block, 0)
        grad_blk = lax.dynamic_slice_in_dim(att_grad, start, block, 0)
        key_win = lax.dynamic_slice_in_dim(keys_pad, start, block + WIN, 0)
        value_win = lax.dynamic_slice_in_dim(values_pad, start, block + WIN, 0)
        allowed = (cols_idx > rows_idx) & (cols_idx <= rows_idx + WIN) & (start + cols_idx >= WIN)
        attended, query_grad, key_part, value_part = attend(query_blk, key_win, value_win, grad_blk, allowed)
        key_old = lax.dynamic_slice_in_dim(key_acc, start, block + WIN, 0)
        value_old = lax.dynamic_slice_in_dim(value_acc, start, block + WIN, 0)
        key_acc = lax.dynamic_update_slice_in_dim(key_acc, key_old + key_part, start, 0)
        value_acc = lax.dynamic_update_slice_in_dim(value_acc, value_old + value_part, start, 0)
        return (key_acc, value_acc), (attended, query_grad)

    init = (jnp.zeros((LEN + WIN, width), jnp.float32), jnp.zeros((LEN + WIN, width), jnp.float32))
    (key_acc, value_acc), (attended, query_grad) = lax.scan(step, init, jnp.arange(LEN // block, dtype=jnp.int32))
    attended = attended.reshape(LEN, width)
    query_grad = query_grad.reshape(LEN, width)
    key_grad = key_acc[WIN:].astype(jnp.bfloat16)
    value_grad = value_acc[WIN:].astype(jnp.bfloat16)
    in_grad = (jnp.dot(query_grad, w_query.T, preferred_element_type=jnp.float32)
               + jnp.dot(key_grad, w_key.T, preferred_element_type=jnp.float32)
               + jnp.dot(value_grad, w_value.T, preferred_element_type=jnp.float32)).astype(jnp.bfloat16)
    weight_term = jnp.concatenate([
        jnp.dot(tokens_rec.T, query_grad, preferred_element_type=jnp.float32),
        jnp.dot(tokens_rec.T, key_grad, preferred_element_type=jnp.float32),
        jnp.dot(tokens_rec.T, value_grad, preferred_element_type=jnp.float32),
        jnp.dot(attended.T, grad_rec, preferred_element_type=jnp.float32)], axis=1)
    return in_grad, weight_term


def reference(tokens, out_grad, w_query, w_key, w_value, w_output, grad_accum):
    grads_list = []
    weight_sum = jnp.zeros(grad_accum.shape, jnp.float32)
    for record in range(RECS):
        in_grad, weight_term = record_pass(tokens[record], out_grad[record], w_query, w_key, w_value, w_output)
        grads_list.append(in_grad)
        weight_sum = weight_sum + weight_term
    factor = 1.0 / ((RECS * LEN) ** 0.5)
    return jnp.stack(grads_list), grad_accum + weight_sum * factor
```

```python
import functools

import jax
import jax.numpy as jnp
from jax import lax
from jax.experimental import pallas as pl
from jax.experimental.pallas import tpu as pltpu
from jax.sharding import Mesh
from jax.sharding import PartitionSpec as P

HD = 128
WIN = 256
LOG2E = 1.4426950408889634
SCALE = 1.0 / HD**0.5
AXES = ("xh", "co", "y", "z", "xl")
SEQ = ("y", "z", "xl")
CHIPS = ("xh", "y", "z", "xl")
F32 = jnp.float32
BF16 = jnp.bfloat16


def dot(a, b, ca, cb):
    return lax.dot_general(a, b, (((ca,), (cb,)), ((), ())), preferred_element_type=F32)


def triangles():
    rows = lax.broadcasted_iota(jnp.int32, (WIN, WIN), 0)
    cols = lax.broadcasted_iota(jnp.int32, (WIN, WIN), 1)
    return cols > rows


def block_pass(query, grad, key_l, value_l, key_r, value_r, upper, bias=None):
    c = SCALE * LOG2E
    s_l = jnp.where(upper, dot(query, key_l, 1, 1), -1e30)
    s_r = jnp.where(upper, -1e30, dot(query, key_r, 1, 1))
    if bias is not None:
        s_l = s_l + bias
    top = jnp.max(jnp.maximum(s_l, s_r), axis=1, keepdims=True) * c
    e_l = jnp.exp2(s_l * c - top)
    e_r = jnp.exp2(s_r * c - top)
    inv = 1.0 / jnp.sum(e_l + e_r, axis=1, keepdims=True)
    p_l = e_l * inv
    p_r = e_r * inv
    pb_l = p_l.astype(BF16)
    pb_r = p_r.astype(BF16)
    attended = (dot(pb_l, value_l, 1, 0) + dot(pb_r, value_r, 1, 0)).astype(BF16)
    delta = jnp.sum(grad.astype(F32) * attended.astype(F32), axis=1, keepdims=True)
    ds_l = (p_l * (dot(grad, value_l, 1, 1) - delta)).astype(BF16)
    return attended, delta, p_r, pb_l, pb_r, ds_l


def main_kernel(
    bias_ref, q_ref, k_ref, v_ref, g_ref, kl_ref, vl_ref, att_ref, dq_ref, dk_ref, dv_ref, pk_ref, pv_ref
):
    upper = triangles()
    blocks = q_ref.shape[0] // WIN
    dk_open = None
    dv_open = None
    for b in range(blocks):
        own = pl.ds(b * WIN, WIN)
        query = q_ref[own, :]
        grad = g_ref[own, :]
        key_r = k_ref[own, :]
        value_r = v_ref[own, :]
        if b == 0:
            key_l = kl_ref[...]
            value_l = vl_ref[...]
            bias = bias_ref[0]
        else:
            key_l = k_ref[pl.ds((b - 1) * WIN, WIN), :]
            value_l = v_ref[pl.ds((b - 1) * WIN, WIN), :]
            bias = None
        attended, delta, p_r, pb_l, pb_r, ds_l = block_pass(
            query, grad, key_l, value_l, key_r, value_r, upper, bias
        )
        att_ref[own, :] = attended
        ds_r = (p_r * (dot(grad, value_r, 1, 1) - delta)).astype(BF16)
        dq_ref[own, :] = ((dot(ds_l, key_l, 1, 0) + dot(ds_r, key_r, 1, 0)) * SCALE).astype(BF16)
        if b > 0:
            before = pl.ds((b - 1) * WIN, WIN)
            dk_ref[before, :] = ((dk_open + dot(ds_l, query, 0, 0)) * SCALE).astype(BF16)
            dv_ref[before, :] = (dv_open + dot(pb_l, grad, 0, 0)).astype(BF16)
        dk_open = dot(ds_r, query, 0, 0)
        dv_open = dot(pb_r, grad, 0, 0)
    last = pl.ds((blocks - 1) * WIN, WIN)
    dk_ref[last, :] = (dk_open * SCALE).astype(BF16)
    dv_ref[last, :] = dv_open.astype(BF16)
    pk_ref[...] = dk_open
    pv_ref[...] = dv_open


def main_attention(bias, queries, keys, values, att_grad, keys_l, values_l):
    count, width = queries.shape
    heads = width // HD
    own = pl.BlockSpec((count, HD), lambda h: (0, h))
    rim = pl.BlockSpec((WIN, HD), lambda h: (0, h))
    full = jax.ShapeDtypeStruct((count, width), BF16)
    part = jax.ShapeDtypeStruct((WIN, width), F32)
    return pl.pallas_call(
        main_kernel,
        grid=(heads,),
        in_specs=[pl.BlockSpec(memory_space=pltpu.SMEM), own, own, own, own, rim, rim],
        out_specs=[own, own, own, own, rim, rim],
        out_shape=[full, full, full, full, part, part],
        compiler_params=pltpu.CompilerParams(vmem_limit_bytes=24 * 2**20),
        cost_estimate=pl.CostEstimate(
            flops=20 * count * 2 * WIN * width, bytes_accessed=20 * 2**20, transcendentals=count * 2 * WIN * heads
        ),
        name="attention_main",
    )(bias, queries, keys, values, att_grad, keys_l, values_l)


def rim_kernel(q_ref, k_ref, v_ref, g_ref, kr_ref, vr_ref, pk_ref, pv_ref, dk_in, dv_in, dk_ref, dv_ref):
    query = q_ref[...]
    grad = g_ref[...]
    _, _, _, pb_l, _, ds_l = block_pass(
        query, grad, k_ref[...], v_ref[...], kr_ref[...], vr_ref[...], triangles()
    )
    dk_ref[...] = ((pk_ref[...] + dot(ds_l, query, 0, 0)) * SCALE).astype(BF16)
    dv_ref[...] = (pv_ref[...] + dot(pb_l, grad, 0, 0)).astype(BF16)


def rim_attention(queries_n, keys, values, grad_n, keys_n, values_n, part_k, part_v, key_grad, value_grad):
    count, width = keys.shape
    heads = width // HD
    rim = pl.BlockSpec((WIN, HD), lambda h: (0, h))
    last = pl.BlockSpec((WIN, HD), lambda h: (count // WIN - 1, h))
    anywhere = pl.BlockSpec(memory_space=pl.ANY)
    full = jax.ShapeDtypeStruct((count, width), BF16)
    return pl.pallas_call(
        rim_kernel,
        grid=(heads,),
        in_specs=[rim, last, last, rim, rim, rim, rim, rim, anywhere, anywhere],
        out_specs=[last, last],
        out_shape=[full, full],
        input_output_aliases={8: 0, 9: 1},
        compiler_params=pltpu.CompilerParams(vmem_limit_bytes=16 * 2**20),
        cost_estimate=pl.CostEstimate(
            flops=14 * WIN * 2 * WIN * width, bytes_accessed=6 * 2**20, transcendentals=2 * WIN * WIN * heads
        ),
        name="attention_rim",
    )(queries_n, keys, values, grad_n, keys_n, values_n, part_k, part_v, key_grad, value_grad)


def project(rows, weight):
    return dot(rows, weight, 1, 0).astype(BF16)


def passed_along(block, distance):
    size = 1
    for axis in SEQ:
        size *= lax.axis_size(axis)
    route = [(i - distance, i) for i in range(size) if 0 <= i - distance < size]
    return lax.ppermute(block, SEQ, route)


def by_core(array, core):
    count, width = array.shape
    parts = array.reshape(count, lax.axis_size("xh"), 2, -1)
    keep = lax.dynamic_index_in_dim(parts, core, 2, keepdims=False).reshape(count, width // 2)
    send = lax.dynamic_index_in_dim(parts, 1 - core, 2, keepdims=False).reshape(count, width // 2)
    return keep, send


def chunk_sum(pairs, core):
    split = [by_core(left, core) for left, _ in pairs]
    rights = [right for _, right in pairs]
    sent = jnp.concatenate(
        [dot(send, right, 0, 0).astype(BF16) for (_, send), right in zip(split, rights)], axis=1
    )
    got = lax.ppermute(sent, "co", [(0, 1), (1, 0)])
    width = rights[0].shape[1]
    both = jnp.concatenate(
        [
            (dot(keep, right, 0, 0) + got[:, i * width : (i + 1) * width].astype(F32)).astype(BF16)
            for i, ((keep, _), right) in enumerate(zip(split, rights))
        ],
        axis=1,
    )
    pieces = lax.all_to_all(both, CHIPS, 0, 0, tiled=True)
    return jnp.sum(pieces.reshape(-1, 8, both.shape[1]).astype(F32), axis=0)


def on_device(tokens, out_grad, w_query, w_key, w_value, w_output, grad_accum):
    tokens = tokens[0]
    out_grad = out_grad[0]
    count, width = tokens.shape
    core = lax.axis_index("co")
    tokens_l = passed_along(tokens[count - WIN :], 1)
    after = passed_along(jnp.stack([tokens[:WIN], out_grad[:WIN]]), -1)
    tokens_n = after[0]
    grads_n = after[1]
    queries = project(tokens, w_query)
    keys = project(tokens, w_key)
    values = project(tokens, w_value)
    att_grad = dot(out_grad, w_output, 1, 1).astype(BF16)
    keys_l = project(tokens_l, w_key)
    values_l = project(tokens_l, w_value)
    first = (lax.axis_index("y") + lax.axis_index("z") + lax.axis_index("xl")) == 0
    bias = jnp.where(first, -1e30, 0.0).astype(F32).reshape(1)
    attended, query_grad, key_grad, value_grad, part_k, part_v = main_attention(
        bias, queries, keys, values, att_grad, keys_l, values_l
    )
    sum_qo = chunk_sum([(tokens, query_grad), (attended, out_grad)], core)
    queries_n = project(tokens_n, w_query)
    keys_n = project(tokens_n, w_key)
    values_n = project(tokens_n, w_value)
    att_grad_n = dot(grads_n, w_output, 1, 1).astype(BF16)
    key_grad, value_grad = rim_attention(
        queries_n, keys, values, att_grad_n, keys_n, values_n, part_k, part_v, key_grad, value_grad
    )
    sum_kv = chunk_sum([(tokens, key_grad), (tokens, value_grad)], core)
    in_grad = (
        dot(query_grad, w_query, 1, 1) + dot(key_grad, w_key, 1, 1) + dot(value_grad, w_value, 1, 1)
    ).astype(BF16)
    total = count
    for axis in AXES:
        total *= lax.axis_size(axis)
    factor = 1.0 / total**0.5
    summed = jnp.concatenate([sum_qo[:, :width], sum_kv, sum_qo[:, width:]], axis=1)
    return in_grad[None], grad_accum + summed * factor


def solution(mesh):
    fine = Mesh(mesh.devices.reshape(2, 2, 4, 4, 2), AXES)
    rows = P(("xh", "co"), SEQ, None)
    accum = P(AXES, None)
    return jax.shard_map(
        on_device,
        mesh=fine,
        in_specs=(rows, rows, P(), P(), P(), P(), accum),
        out_specs=(rows, accum),
        check_vma=False,
    )
```

```python
import functools

import jax
import jax.numpy as jnp
from jax import lax
from jax.experimental import pallas as pl
from jax.experimental.pallas import tpu as pltpu
from jax.sharding import Mesh
from jax.sharding import PartitionSpec as P

HD = 128
WIN = 256
LOG2E = 1.4426950408889634
SCALE = 1.0 / HD**0.5
AXES = ("xh", "co", "y", "z", "xl")
SEQ = ("y", "z", "xl")
CHIPS = ("xh", "y", "z", "xl")
F32 = jnp.float32
BF16 = jnp.bfloat16


def dot(a, b, ca, cb):
    return lax.dot_general(a, b, (((ca,), (cb,)), ((), ())), preferred_element_type=F32)


HALF = WIN // 2
NEG = -1e30


def bf(value):
    return value.astype(BF16)


def quads(a, b, c, d):
    return jnp.concatenate([jnp.concatenate([a, b], axis=1), jnp.concatenate([c, d], axis=1)], axis=0)


def upper_triangle():
    rows = lax.broadcasted_iota(jnp.int32, (HALF, HALF), 0)
    cols = lax.broadcasted_iota(jnp.int32, (HALF, HALF), 1)
    return cols > rows


def scores_of(block, bias):
    query, grad, key_l, value_l, key_r, value_r = block
    s_l = dot(query, key_l, 1, 1)
    if bias is not None:
        s_l = s_l + bias
    return s_l, dot(query, key_r, 1, 1), dot(grad, value_l, 1, 1), dot(grad, value_r, 1, 1)


def probs_of(scores, upper):
    s_l, s_r = scores[:2]
    low = slice(0, HALF)
    high = slice(HALF, WIN)
    runs = (
        (jnp.where(upper, s_l[low, low], NEG), s_l[low, high], jnp.where(upper, NEG, s_r[low, low])),
        (jnp.where(upper, s_l[high, high], NEG), s_r[high, low], jnp.where(upper, NEG, s_r[high, high])),
    )
    probs = []
    for run in runs:
        top = jnp.max(jnp.maximum(jnp.maximum(run[0], run[1]), run[2]), axis=1, keepdims=True)
        shift = top * (SCALE * LOG2E)
        e = [jnp.exp2(part * (SCALE * LOG2E) - shift) for part in run]
        inv = 1.0 / jnp.sum(e[0] + e[1] + e[2], axis=1, keepdims=True)
        probs.append([part * inv for part in e])
    zero = jnp.zeros((HALF, HALF), BF16)
    (t0, t1, t2), (b0, b1, b2) = probs
    return probs, quads(bf(t0), bf(t1), zero, bf(b0)), quads(bf(t2), zero, bf(b1), bf(b2))


def delta_of(block, weights):
    grad, value_l, value_r = block[1], block[3], block[5]
    attended = bf(dot(weights[1], value_l, 1, 0) + dot(weights[2], value_r, 1, 0))
    return attended, jnp.sum(grad.astype(F32) * attended.astype(F32), axis=1, keepdims=True)


def score_grads(scores, weights, delta):
    d_l, d_r = scores[2:]
    low = slice(0, HALF)
    high = slice(HALF, WIN)
    (t0, t1, t2), (b0, b1, b2) = weights[0]
    dt = delta[low]
    db = delta[high]
    zero = jnp.zeros((HALF, HALF), BF16)
    left = quads(
        bf(t0 * (d_l[low, low] - dt)), bf(t1 * (d_l[low, high] - dt)), zero, bf(b0 * (d_l[high, high] - db))
    )
    right = quads(
        bf(t2 * (d_r[low, low] - dt)), zero, bf(b1 * (d_r[high, low] - db)), bf(b2 * (d_r[high, high] - db))
    )
    return left, right


def project_kernel(x_ref, g_ref, wq_ref, wk_ref, wv_ref, wo_ref, q_ref, k_ref, v_ref, a_ref):
    tokens = x_ref[...]
    k_ref[...] = bf(dot(tokens, wk_ref[...], 1, 0))
    v_ref[...] = bf(dot(tokens, wv_ref[...], 1, 0))
    q_ref[...] = bf(dot(tokens, wq_ref[...], 1, 0))
    a_ref[...] = bf(dot(g_ref[...], wo_ref[...], 1, 1))


def projections(tokens, out_grad, w_query, w_key, w_value, w_output):
    count, width = tokens.shape
    step = 256
    whole = pl.BlockSpec((count, width), lambda j: (0, 0))
    column = pl.BlockSpec((width, step), lambda j: (0, j))
    row = pl.BlockSpec((step, width), lambda j: (j, 0))
    out = pl.BlockSpec((count, step), lambda j: (0, j))
    return pl.pallas_call(
        project_kernel,
        grid=(width // step,),
        in_specs=[whole, whole, column, column, column, row],
        out_specs=[out] * 4,
        out_shape=[jax.ShapeDtypeStruct((count, width), BF16)] * 4,
        compiler_params=pltpu.CompilerParams(vmem_limit_bytes=40 * 2**20),
        cost_estimate=pl.CostEstimate(
            flops=8 * count * width * width, bytes_accessed=20 * 2**20, transcendentals=0
        ),
        name="projections",
    )(tokens, out_grad, w_query, w_key, w_value, w_output)


def main_kernel(
    bias_ref, q_ref, k_ref, v_ref, g_ref, xl_ref, wk_ref, wv_ref,
    att_ref, dq_ref, dk_ref, dv_ref, pk_ref, pv_ref,
):
    upper = upper_triangle()
    blocks = q_ref.shape[0] // WIN
    span = [slice(b * WIN, (b + 1) * WIN) for b in range(blocks)]
    keys = [bf(dot(xl_ref[...], wk_ref[...], 1, 0))] + [k_ref[s, :] for s in span]
    values = [bf(dot(xl_ref[...], wv_ref[...], 1, 0))] + [v_ref[s, :] for s in span]
    block = [
        (q_ref[span[b], :], g_ref[span[b], :], keys[b], values[b], keys[b + 1], values[b + 1])
        for b in range(blocks)
    ]
    order = list(range(1, blocks)) + [0]
    scores = {b: scores_of(block[b], bias_ref[0] if b == 0 else None) for b in order}
    weights = {b: probs_of(scores[b], upper) for b in order}
    deltas = {}
    for b in order:
        attended, deltas[b] = delta_of(block[b], weights[b])
        att_ref[span[b], :] = attended
    sgrads = {b: score_grads(scores[b], weights[b], deltas[b]) for b in order}
    dk_open = None
    dv_open = None
    for b in range(blocks):
        query, grad, key_l, _, key_r, _ = block[b]
        ds_l, ds_r = sgrads[b]
        _, pb_l, pb_r = weights[b]
        dq_ref[span[b], :] = bf((dot(ds_l, key_l, 1, 0) + dot(ds_r, key_r, 1, 0)) * SCALE)
        if b > 0:
            dk_ref[span[b - 1], :] = bf((dk_open + dot(ds_l, query, 0, 0)) * SCALE)
            dv_ref[span[b - 1], :] = bf(dv_open + dot(pb_l, grad, 0, 0))
        dk_open = dot(ds_r, query, 0, 0)
        dv_open = dot(pb_r, grad, 0, 0)
    dk_ref[span[-1], :] = bf(dk_open * SCALE)
    dv_ref[span[-1], :] = bf(dv_open)
    pk_ref[...] = dk_open
    pv_ref[...] = dv_open


def main_attention(bias, queries, keys, values, att_grad, tokens_l, w_key, w_value):
    count, width = queries.shape
    heads = width // HD
    own = pl.BlockSpec((count, HD), lambda h: (0, h))
    rim = pl.BlockSpec((WIN, HD), lambda h: (0, h))
    left = pl.BlockSpec((WIN, width), lambda h: (0, 0))
    column = pl.BlockSpec((width, HD), lambda h: (0, h))
    full = jax.ShapeDtypeStruct((count, width), BF16)
    part = jax.ShapeDtypeStruct((WIN, width), F32)
    return pl.pallas_call(
        main_kernel,
        grid=(heads,),
        in_specs=[pl.BlockSpec(memory_space=pltpu.SMEM), own, own, own, own, left, column, column],
        out_specs=[own, own, own, own, rim, rim],
        out_shape=[full, full, full, full, part, part],
        compiler_params=pltpu.CompilerParams(vmem_limit_bytes=40 * 2**20),
        cost_estimate=pl.CostEstimate(
            flops=20 * count * 2 * WIN * width,
            bytes_accessed=22 * 2**20,
            transcendentals=count * 2 * WIN * heads,
        ),
        name="attention_main",
    )(bias, queries, keys, values, att_grad, tokens_l, w_key, w_value)


def rim_kernel(
    n_ref, wq_ref, wk_ref, wv_ref, wo_ref, k_ref, v_ref, pk_ref, pv_ref, dk_in, dv_in, dk_ref, dv_ref
):
    upper = upper_triangle()
    tokens = n_ref[0]
    queries = bf(dot(tokens, wq_ref[...], 1, 0))
    keys = bf(dot(tokens, wk_ref[...], 1, 0))
    values = bf(dot(tokens, wv_ref[...], 1, 0))
    grads = bf(dot(n_ref[1], wo_ref[...], 1, 1))
    columns = [slice(h * HD, (h + 1) * HD) for h in range(k_ref.shape[1] // HD)]
    block = [
        (queries[:, c], grads[:, c], k_ref[:, c], v_ref[:, c], keys[:, c], values[:, c]) for c in columns
    ]
    scores = [scores_of(entry, None) for entry in block]
    weights = [probs_of(entry, upper) for entry in scores]
    deltas = [delta_of(*entry)[1] for entry in zip(block, weights)]
    for h, c in enumerate(columns):
        ds_l = score_grads(scores[h], weights[h], deltas[h])[0]
        dk_ref[:, c] = bf((pk_ref[:, c] + dot(ds_l, block[h][0], 0, 0)) * SCALE)
        dv_ref[:, c] = bf(pv_ref[:, c] + dot(weights[h][1], block[h][1], 0, 0))


def rim_attention(after, w_query, w_key, w_value, w_output, keys, values, part_k, part_v, key_grad, value_grad):
    count, width = keys.shape
    step = 4 * HD
    column = pl.BlockSpec((width, step), lambda j: (0, j))
    row = pl.BlockSpec((step, width), lambda j: (j, 0))
    rim = pl.BlockSpec((WIN, step), lambda j: (0, j))
    last = pl.BlockSpec((WIN, step), lambda j: (count // WIN - 1, j))
    whole = pl.BlockSpec((2, WIN, width), lambda j: (0, 0, 0))
    anywhere = pl.BlockSpec(memory_space=pl.ANY)
    full = jax.ShapeDtypeStruct((count, width), BF16)
    return pl.pallas_call(
        rim_kernel,
        grid=(width // step,),
        in_specs=[whole, column, column, column, row, last, last, rim, rim, anywhere, anywhere],
        out_specs=[last, last],
        out_shape=[full, full],
        input_output_aliases={9: 0, 10: 1},
        compiler_params=pltpu.CompilerParams(vmem_limit_bytes=40 * 2**20),
        cost_estimate=pl.CostEstimate(
            flops=8 * WIN * width * width + 14 * WIN * 2 * WIN * width,
            bytes_accessed=14 * 2**20,
            transcendentals=2 * WIN * WIN * width // HD,
        ),
        name="attention_rim",
    )(after, w_query, w_key, w_value, w_output, keys, values, part_k, part_v, key_grad, value_grad)


def weight_kernel(core_ref, *refs, added):
    if added:
        a0, a1, b0, b1, r0, r1, got, out = refs
    else:
        a0, a1, b0, b1, r0, r1, out = refs
    pair = pl.program_id(0)

    def product(low, high, right):
        left = jnp.concatenate([low[...], high[...]], axis=1)
        total = dot(left, right[...], 0, 0)
        if added:
            total = total + got[...].astype(F32)
        out[...] = bf(total)

    @pl.when(pair == 0)
    def _():
        product(a0, a1, r0)

    @pl.when(pair == 1)
    def _():
        product(b0, b1, r1)


def weight_pair(core, lefts, rights, got=None):
    count, width = rights[0].shape
    step = 512
    steps = width // step
    rows = width // 4

    def left_spec(x):
        return pl.BlockSpec((count, rows), lambda p, j, c: (0, 2 * x + c[0]))

    right0 = pl.BlockSpec((count, step), lambda p, j, c: (0, jnp.where(p == 0, j, steps - 1)))
    right1 = pl.BlockSpec((count, step), lambda p, j, c: (0, jnp.where(p == 1, j, 0)))
    out = pl.BlockSpec((2 * rows, step), lambda p, j, c: (0, p * steps + j))
    operands = [lefts[0], lefts[0], lefts[1], lefts[1], rights[0], rights[1]]
    specs = [left_spec(0), left_spec(1), left_spec(0), left_spec(1), right0, right1]
    if got is not None:
        operands.append(got)
        specs.append(out)
    return pl.pallas_call(
        functools.partial(weight_kernel, added=got is not None),
        grid_spec=pltpu.PrefetchScalarGridSpec(
            num_scalar_prefetch=1, grid=(2, steps), in_specs=specs, out_specs=out
        ),
        out_shape=jax.ShapeDtypeStruct((2 * rows, 2 * width), BF16),
        compiler_params=pltpu.CompilerParams(vmem_limit_bytes=40 * 2**20),
        cost_estimate=pl.CostEstimate(
            flops=4 * count * 2 * rows * width, bytes_accessed=8 * 2**20, transcendentals=0
        ),
        name="weight_send" if got is None else "weight_keep",
    )(core.reshape(1), *operands)


def passed_along(block, distance):
    size = 1
    for axis in SEQ:
        size *= lax.axis_size(axis)
    route = [(i - distance, i) for i in range(size) if 0 <= i - distance < size]
    return lax.ppermute(block, SEQ, route)


def on_device(tokens, out_grad, w_query, w_key, w_value, w_output, grad_accum):
    tokens = tokens[0]
    out_grad = out_grad[0]
    count, width = tokens.shape
    core = lax.axis_index("co")
    swap = [(0, 1), (1, 0)]
    tokens_l = passed_along(tokens[count - WIN :], 1)
    ahead, tokens_l = lax.optimization_barrier((jnp.stack([tokens[:WIN], out_grad[:WIN]]), tokens_l))
    after = passed_along(ahead, -1)
    queries, keys, values, att_grad = projections(tokens, out_grad, w_query, w_key, w_value, w_output)
    first = (lax.axis_index("y") + lax.axis_index("z") + lax.axis_index("xl")) == 0
    bias = jnp.where(first, NEG, 0.0).astype(F32).reshape(1)
    attended, query_grad, key_grad, value_grad, part_k, part_v = main_attention(
        bias, queries, keys, values, att_grad, tokens_l, w_key, w_value
    )
    sent = weight_pair(1 - core, (tokens, attended), (query_grad, out_grad))
    got = lax.ppermute(sent, "co", swap)
    both = weight_pair(core, (tokens, attended), (query_grad, out_grad), got)
    pieces_qo = lax.all_to_all(both, CHIPS, 0, 0, tiled=True)
    part_k, part_v, _ = lax.optimization_barrier((part_k, part_v, both))
    key_grad, value_grad = rim_attention(
        after, w_query, w_key, w_value, w_output, keys, values, part_k, part_v, key_grad, value_grad
    )
    sent = weight_pair(1 - core, (tokens, tokens), (key_grad, value_grad))
    got = lax.ppermute(sent, "co", swap)
    both = weight_pair(core, (tokens, tokens), (key_grad, value_grad), got)
    pieces_kv = lax.all_to_all(both, CHIPS, 0, 0, tiled=True)
    in_grad = bf(
        dot(query_grad, w_query, 1, 1) + dot(key_grad, w_key, 1, 1) + dot(value_grad, w_value, 1, 1)
    )
    sum_qo, sum_kv = [
        jnp.sum(pieces.reshape(-1, 8, 2 * width).astype(F32), axis=0) for pieces in (pieces_qo, pieces_kv)
    ]
    total = count
    for axis in AXES:
        total *= lax.axis_size(axis)
    factor = 1.0 / total**0.5
    summed = jnp.concatenate([sum_qo[:, :width], sum_kv, sum_qo[:, width:]], axis=1)
    return in_grad[None], grad_accum + summed * factor


def solution(mesh):
    fine = Mesh(mesh.devices.reshape(2, 2, 4, 4, 2), AXES)
    rows = P(("xh", "co"), SEQ, None)
    accum = P(AXES, None)
    return jax.shard_map(
        on_device,
        mesh=fine,
        in_specs=(rows, rows, P(), P(), P(), P(), accum),
        out_specs=(rows, accum),
        check_vma=False,
    )
```

```python
import functools

import jax
import jax.numpy as jnp
from jax import lax
from jax.experimental import pallas as pl
from jax.experimental.pallas import tpu as pltpu
from jax.sharding import Mesh
from jax.sharding import PartitionSpec as P

HD = 128
WIN = 256
LOG2E = 1.4426950408889634
SCALE = 1.0 / HD**0.5
AXES = ("xh", "co", "y", "z", "xl")
SEQ = ("y", "z", "xl")
CHIPS = ("xh", "y", "z", "xl")
F32 = jnp.float32
BF16 = jnp.bfloat16


def dot(a, b, ca, cb):
    return lax.dot_general(a, b, (((ca,), (cb,)), ((), ())), preferred_element_type=F32)


SMALL = pl.CostEstimate(flops=10**8, bytes_accessed=10**5, transcendentals=0)
VMEM = 60 * 2**20
HALF = WIN // 2
NEG = -1e30


def bf(value):
    return value.astype(BF16)


def quads(a, b, c, d):
    return jnp.concatenate([jnp.concatenate([a, b], axis=1), jnp.concatenate([c, d], axis=1)], axis=0)


def upper_triangle():
    rows = lax.broadcasted_iota(jnp.int32, (HALF, HALF), 0)
    cols = lax.broadcasted_iota(jnp.int32, (HALF, HALF), 1)
    return cols > rows


def scores_of(block, bias):
    query, grad, key_l, value_l, key_r, value_r = block
    s_l = dot(query, key_l, 1, 1)
    if bias is not None:
        s_l = s_l + bias
    return s_l, dot(query, key_r, 1, 1), dot(grad, value_l, 1, 1), dot(grad, value_r, 1, 1)


def probs_of(scores, upper):
    s_l, s_r = scores[:2]
    low = slice(0, HALF)
    high = slice(HALF, WIN)
    runs = (
        (jnp.where(upper, s_l[low, low], NEG), s_l[low, high], jnp.where(upper, NEG, s_r[low, low])),
        (jnp.where(upper, s_l[high, high], NEG), s_r[high, low], jnp.where(upper, NEG, s_r[high, high])),
    )
    probs = []
    for run in runs:
        top = jnp.max(jnp.maximum(jnp.maximum(run[0], run[1]), run[2]), axis=1, keepdims=True)
        shift = top * (SCALE * LOG2E)
        e = [jnp.exp2(part * (SCALE * LOG2E) - shift) for part in run]
        inv = 1.0 / jnp.sum(e[0] + e[1] + e[2], axis=1, keepdims=True)
        probs.append([part * inv for part in e])
    zero = jnp.zeros((HALF, HALF), BF16)
    (t0, t1, t2), (b0, b1, b2) = probs
    return probs, quads(bf(t0), bf(t1), zero, bf(b0)), quads(bf(t2), zero, bf(b1), bf(b2))


def delta_of(block, weights):
    grad, value_l, value_r = block[1], block[3], block[5]
    attended = bf(dot(weights[1], value_l, 1, 0) + dot(weights[2], value_r, 1, 0))
    return attended, jnp.sum(grad.astype(F32) * attended.astype(F32), axis=1, keepdims=True)


def score_grads(scores, weights, delta):
    d_l, d_r = scores[2:]
    low = slice(0, HALF)
    high = slice(HALF, WIN)
    (t0, t1, t2), (b0, b1, b2) = weights[0]
    dt = delta[low]
    db = delta[high]
    zero = jnp.zeros((HALF, HALF), BF16)
    left = quads(
        bf(t0 * (d_l[low, low] - dt)), bf(t1 * (d_l[low, high] - dt)), zero, bf(b0 * (d_l[high, high] - db))
    )
    right = quads(
        bf(t2 * (d_r[low, low] - dt)), zero, bf(b1 * (d_r[high, low] - db)), bf(b2 * (d_r[high, high] - db))
    )
    return left, right


def project_kernel(x_ref, wq_ref, wk_ref, wv_ref, q_ref, k_ref, v_ref):
    tokens = x_ref[...]
    q_ref[...] = bf(dot(tokens, wq_ref[...], 1, 0))
    k_ref[...] = bf(dot(tokens, wk_ref[...], 1, 0))
    v_ref[...] = bf(dot(tokens, wv_ref[...], 1, 0))


def back_kernel(g_ref, wo_ref, a_ref):
    a_ref[...] = bf(dot(g_ref[...], wo_ref[...], 1, 1))


def projections(rows, weights, back):
    count, width = rows.shape
    step = 256
    whole = pl.BlockSpec((count, width), lambda j: (0, 0))
    side = (
        pl.BlockSpec((step, width), lambda j: (j, 0)) if back else pl.BlockSpec((width, step), lambda j: (0, j))
    )
    out = pl.BlockSpec((count, step), lambda j: (0, j))
    return pl.pallas_call(
        back_kernel if back else project_kernel,
        grid=(width // step,),
        in_specs=[whole] + [side] * len(weights),
        out_specs=[out] * len(weights),
        out_shape=[jax.ShapeDtypeStruct((count, width), BF16)] * len(weights),
        compiler_params=pltpu.CompilerParams(vmem_limit_bytes=VMEM),
        cost_estimate=SMALL,
        name="project_back" if back else "projections",
    )(rows, *weights)


def main_kernel(
    bias_ref, q_ref, k_ref, v_ref, g_ref, xl_ref, wk_ref, wv_ref,
    att_ref, dq_ref, dk_ref, dv_ref, pk_ref, pv_ref,
):
    upper = upper_triangle()
    blocks = q_ref.shape[0] // WIN
    span = [slice(b * WIN, (b + 1) * WIN) for b in range(blocks)]
    keys = [bf(dot(xl_ref[...], wk_ref[...], 1, 0))] + [k_ref[s, :] for s in span]
    values = [bf(dot(xl_ref[...], wv_ref[...], 1, 0))] + [v_ref[s, :] for s in span]
    block = [
        (q_ref[span[b], :], g_ref[span[b], :], keys[b], values[b], keys[b + 1], values[b + 1])
        for b in range(blocks)
    ]
    order = list(range(1, blocks)) + [0]
    scores = {b: scores_of(block[b], bias_ref[0] if b == 0 else None) for b in order}
    weights = {b: probs_of(scores[b], upper) for b in order}
    deltas = {}
    for b in order:
        attended, deltas[b] = delta_of(block[b], weights[b])
        att_ref[span[b], :] = attended
    sgrads = {b: score_grads(scores[b], weights[b], deltas[b]) for b in order}
    dk_open = None
    dv_open = None
    for b in range(blocks):
        query, grad, key_l, _, key_r, _ = block[b]
        ds_l, ds_r = sgrads[b]
        _, pb_l, pb_r = weights[b]
        dq_ref[span[b], :] = bf((dot(ds_l, key_l, 1, 0) + dot(ds_r, key_r, 1, 0)) * SCALE)
        if b > 0:
            dk_ref[span[b - 1], :] = bf((dk_open + dot(ds_l, query, 0, 0)) * SCALE)
            dv_ref[span[b - 1], :] = bf(dv_open + dot(pb_l, grad, 0, 0))
        dk_open = dot(ds_r, query, 0, 0)
        dv_open = dot(pb_r, grad, 0, 0)
    dk_ref[span[-1], :] = bf(dk_open * SCALE)
    dv_ref[span[-1], :] = bf(dv_open)
    pk_ref[...] = dk_open
    pv_ref[...] = dv_open


def main_attention(bias, queries, keys, values, att_grad, tokens_l, w_key, w_value):
    count, width = queries.shape
    heads = width // HD
    own = pl.BlockSpec((count, HD), lambda h: (0, h))
    rim = pl.BlockSpec((WIN, HD), lambda h: (0, h))
    left = pl.BlockSpec((WIN, width), lambda h: (0, 0))
    column = pl.BlockSpec((width, HD), lambda h: (0, h))
    full = jax.ShapeDtypeStruct((count, width), BF16)
    part = jax.ShapeDtypeStruct((WIN, width), F32)
    return pl.pallas_call(
        main_kernel,
        grid=(heads,),
        in_specs=[pl.BlockSpec(memory_space=pltpu.SMEM), own, own, own, own, left, column, column],
        out_specs=[own, own, own, own, rim, rim],
        out_shape=[full, full, full, full, part, part],
        compiler_params=pltpu.CompilerParams(vmem_limit_bytes=VMEM),
        cost_estimate=SMALL,
        name="attention_main",
    )(bias, queries, keys, values, att_grad, tokens_l, w_key, w_value)


def rim_kernel(
    xn_ref, gn_ref, wq_ref, wk_ref, wv_ref, wo_ref, k_ref, v_ref, pk_ref, pv_ref, dk_in, dv_in, dk_ref, dv_ref
):
    upper = upper_triangle()
    tokens = xn_ref[...]
    queries = bf(dot(tokens, wq_ref[...], 1, 0))
    keys = bf(dot(tokens, wk_ref[...], 1, 0))
    values = bf(dot(tokens, wv_ref[...], 1, 0))
    grads = bf(dot(gn_ref[...], wo_ref[...], 1, 1))
    columns = [slice(h * HD, (h + 1) * HD) for h in range(k_ref.shape[1] // HD)]
    block = [
        (queries[:, c], grads[:, c], k_ref[:, c], v_ref[:, c], keys[:, c], values[:, c]) for c in columns
    ]
    scores = [scores_of(entry, None) for entry in block]
    weights = [probs_of(entry, upper) for entry in scores]
    deltas = [delta_of(*entry)[1] for entry in zip(block, weights)]
    for h, c in enumerate(columns):
        ds_l = score_grads(scores[h], weights[h], deltas[h])[0]
        dk_ref[:, c] = bf((pk_ref[:, c] + dot(ds_l, block[h][0], 0, 0)) * SCALE)
        dv_ref[:, c] = bf(pv_ref[:, c] + dot(weights[h][1], block[h][1], 0, 0))


def rim_attention(tokens_n, grads_n, w_query, w_key, w_value, w_output, keys, values, part_k, part_v, key_grad, value_grad):
    count, width = keys.shape
    step = 4 * HD
    column = pl.BlockSpec((width, step), lambda j: (0, j))
    row = pl.BlockSpec((step, width), lambda j: (j, 0))
    rim = pl.BlockSpec((WIN, step), lambda j: (0, j))
    last = pl.BlockSpec((WIN, step), lambda j: (count // WIN - 1, j))
    whole = pl.BlockSpec((WIN, width), lambda j: (0, 0))
    anywhere = pl.BlockSpec(memory_space=pl.ANY)
    full = jax.ShapeDtypeStruct((count, width), BF16)
    return pl.pallas_call(
        rim_kernel,
        grid=(width // step,),
        in_specs=[whole, whole, column, column, column, row, last, last, rim, rim, anywhere, anywhere],
        out_specs=[last, last],
        out_shape=[full, full],
        input_output_aliases={10: 0, 11: 1},
        compiler_params=pltpu.CompilerParams(vmem_limit_bytes=VMEM),
        cost_estimate=SMALL,
        name="attention_rim",
    )(tokens_n, grads_n, w_query, w_key, w_value, w_output, keys, values, part_k, part_v, key_grad, value_grad)


def weight_kernel(core_ref, low_ref, high_ref, right_ref, *refs, added):
    left = jnp.concatenate([low_ref[...], high_ref[...]], axis=1)
    total = dot(left, right_ref[...], 0, 0)
    if added:
        total = total + refs[0][...].astype(F32)
    refs[-1][...] = bf(total)


def weight_part(core, left, right, got=None, slot=0, into=None):
    count, width = right.shape
    step = 512
    steps = width // step
    rows = width // 4
    added = got is not None

    def left_spec(x):
        return pl.BlockSpec((count, rows), lambda j, c: (0, 2 * x + c[0]))

    column = pl.BlockSpec((2 * rows, step), lambda j, c: (0, j))
    operands = [core.reshape(1), left, left, right]
    specs = [left_spec(0), left_spec(1), pl.BlockSpec((count, step), lambda j, c: (0, j))]
    alias = {}
    if added:
        operands.append(got)
        specs.append(column)
    if into is not None:
        alias = {len(operands): 0}
        operands.append(into)
        specs.append(pl.BlockSpec(memory_space=pl.ANY))
    return pl.pallas_call(
        functools.partial(weight_kernel, added=added),
        grid_spec=pltpu.PrefetchScalarGridSpec(
            num_scalar_prefetch=1,
            grid=(steps,),
            in_specs=specs,
            out_specs=pl.BlockSpec((2 * rows, step), lambda j, c: (0, slot * steps + j)),
        ),
        out_shape=jax.ShapeDtypeStruct((2 * rows, 2 * width if added else width), BF16),
        input_output_aliases=alias,
        compiler_params=pltpu.CompilerParams(vmem_limit_bytes=VMEM),
        cost_estimate=SMALL,
        name="weight_keep" if added else "weight_send",
    )(*operands)


def weight_pair(core, pairs):
    swap = [(0, 1), (1, 0)]
    got = [lax.ppermute(weight_part(1 - core, left, right), "co", swap) for left, right in pairs]
    both = None
    for slot, (left, right) in enumerate(pairs):
        both = weight_part(core, left, right, got[slot], slot, both)
    return both


def passed_along(block, distance):
    size = 1
    for axis in SEQ:
        size *= lax.axis_size(axis)
    route = [(i - distance, i) for i in range(size) if 0 <= i - distance < size]
    return lax.ppermute(block, SEQ, route)


def on_device(tokens, out_grad, w_query, w_key, w_value, w_output, grad_accum):
    tokens = tokens[0]
    out_grad = out_grad[0]
    count, width = tokens.shape
    core = lax.axis_index("co")
    tokens_l = passed_along(tokens[count - WIN :], 1)
    queries, keys, values = projections(tokens, (w_query, w_key, w_value), False)
    head_x, head_g, behind, tokens_l, keys = lax.optimization_barrier(
        (tokens[:WIN], out_grad[:WIN], out_grad, tokens_l, keys)
    )
    tokens_n = passed_along(head_x, -1)
    grads_n = passed_along(head_g, -1)
    (att_grad,) = projections(behind, (w_output,), True)
    first = (lax.axis_index("y") + lax.axis_index("z") + lax.axis_index("xl")) == 0
    bias = jnp.where(first, NEG, 0.0).astype(F32).reshape(1)
    attended, query_grad, key_grad, value_grad, part_k, part_v = main_attention(
        bias, queries, keys, values, att_grad, tokens_l, w_key, w_value
    )
    query_grad, tokens_n, grads_n = lax.optimization_barrier((query_grad, tokens_n, grads_n))
    both = weight_pair(core, ((tokens, query_grad), (attended, out_grad)))
    pieces_qo = lax.all_to_all(both, CHIPS, 0, 0, tiled=True)
    part_k, part_v, _ = lax.optimization_barrier((part_k, part_v, both))
    key_grad, value_grad = rim_attention(
        tokens_n, grads_n, w_query, w_key, w_value, w_output,
        keys, values, part_k, part_v, key_grad, value_grad,
    )
    both = weight_pair(core, ((tokens, key_grad), (tokens, value_grad)))
    pieces_kv = lax.all_to_all(both, CHIPS, 0, 0, tiled=True)
    in_grad = bf(
        dot(query_grad, w_query, 1, 1) + dot(key_grad, w_key, 1, 1) + dot(value_grad, w_value, 1, 1)
    )
    sum_qo, sum_kv = [
        jnp.sum(pieces.reshape(-1, 8, 2 * width).astype(F32), axis=0) for pieces in (pieces_qo, pieces_kv)
    ]
    total = count
    for axis in AXES:
        total *= lax.axis_size(axis)
    factor = 1.0 / total**0.5
    summed = jnp.concatenate([sum_qo[:, :width], sum_kv, sum_qo[:, width:]], axis=1)
    return in_grad[None], grad_accum + summed * factor


def solution(mesh):
    fine = Mesh(mesh.devices.reshape(2, 2, 4, 4, 2), AXES)
    rows = P(("xh", "co"), SEQ, None)
    accum = P(AXES, None)
    return jax.shard_map(
        on_device,
        mesh=fine,
        in_specs=(rows, rows, P(), P(), P(), P(), accum),
        out_specs=(rows, accum),
        check_vma=False,
    )
```

```python
import jax
import jax.numpy as jnp
from jax import lax
from jax.experimental import pallas as pl
from jax.experimental.pallas import tpu as pltpu
from jax.sharding import Mesh
from jax.sharding import PartitionSpec as P

HD = 128
WIN = 256
LOG2E = 1.4426950408889634
SCALE = 1.0 / HD**0.5
AXES = ("xh", "co", "y", "z", "xl")
SEQ = ("y", "z", "xl")
CHIPS = ("xh", "y", "z", "xl")
F32 = jnp.float32
BF16 = jnp.bfloat16


def dot(a, b, ca, cb):
    return lax.dot_general(a, b, (((ca,), (cb,)), ((), ())), preferred_element_type=F32)


SMALL = pl.CostEstimate(flops=10**8, bytes_accessed=10**5, transcendentals=0)
VMEM = 60 * 2**20
PAIR = 2 * HD
HALF = WIN // 2
NEG = -1e30


def bf(value):
    return value.astype(BF16)


def quads(a, b, c, d):
    return jnp.concatenate([jnp.concatenate([a, b], axis=1), jnp.concatenate([c, d], axis=1)], axis=0)


def upper_triangle():
    rows = lax.broadcasted_iota(jnp.int32, (HALF, HALF), 0)
    cols = lax.broadcasted_iota(jnp.int32, (HALF, HALF), 1)
    return cols > rows


def scores_of(block, bias):
    query, grad, key_l, value_l, key_r, value_r = block
    s_l = dot(query, key_l, 1, 1)
    if bias is not None:
        s_l = s_l + bias
    return s_l, dot(query, key_r, 1, 1), dot(grad, value_l, 1, 1), dot(grad, value_r, 1, 1)


def probs_of(scores, upper):
    s_l, s_r = scores[:2]
    low = slice(0, HALF)
    high = slice(HALF, WIN)
    runs = (
        (jnp.where(upper, s_l[low, low], NEG), s_l[low, high], jnp.where(upper, NEG, s_r[low, low])),
        (jnp.where(upper, s_l[high, high], NEG), s_r[high, low], jnp.where(upper, NEG, s_r[high, high])),
    )
    probs = []
    for run in runs:
        top = jnp.max(jnp.maximum(jnp.maximum(run[0], run[1]), run[2]), axis=1, keepdims=True)
        shift = top * (SCALE * LOG2E)
        e = [jnp.exp2(part * (SCALE * LOG2E) - shift) for part in run]
        inv = 1.0 / jnp.sum(e[0] + e[1] + e[2], axis=1, keepdims=True)
        probs.append([part * inv for part in e])
    zero = jnp.zeros((HALF, HALF), BF16)
    (t0, t1, t2), (b0, b1, b2) = probs
    return probs, quads(bf(t0), bf(t1), zero, bf(b0)), quads(bf(t2), zero, bf(b1), bf(b2))


def delta_of(block, weights):
    grad, value_l, value_r = block[1], block[3], block[5]
    attended = bf(dot(weights[1], value_l, 1, 0) + dot(weights[2], value_r, 1, 0))
    return attended, jnp.sum(grad.astype(F32) * attended.astype(F32), axis=1, keepdims=True)


def score_grads(scores, weights, delta):
    d_l, d_r = scores[2:]
    low = slice(0, HALF)
    high = slice(HALF, WIN)
    (t0, t1, t2), (b0, b1, b2) = weights[0]
    dt = delta[low]
    db = delta[high]
    zero = jnp.zeros((HALF, HALF), BF16)
    left = quads(
        bf(t0 * (d_l[low, low] - dt)), bf(t1 * (d_l[low, high] - dt)), zero, bf(b0 * (d_l[high, high] - db))
    )
    right = quads(
        bf(t2 * (d_r[low, low] - dt)), zero, bf(b1 * (d_r[high, low] - db)), bf(b2 * (d_r[high, high] - db))
    )
    return left, right


def project_kernel(x_ref, g_ref, wq_ref, wk_ref, wv_ref, wo_ref, q_ref, k_ref, v_ref, a_ref):
    tokens = x_ref[...]
    q_ref[...] = bf(dot(tokens, wq_ref[...], 1, 0))
    k_ref[...] = bf(dot(tokens, wk_ref[...], 1, 0))
    v_ref[...] = bf(dot(tokens, wv_ref[...], 1, 0))
    a_ref[...] = bf(dot(g_ref[...], wo_ref[...], 1, 1))


def projections(tokens, out_grad, w_query, w_key, w_value, w_output):
    count, width = tokens.shape
    whole = pl.BlockSpec((count, width), lambda j: (0, 0))
    column = pl.BlockSpec((width, PAIR), lambda j: (0, j))
    row = pl.BlockSpec((PAIR, width), lambda j: (j, 0))
    out = pl.BlockSpec((count, PAIR), lambda j: (0, j))
    return pl.pallas_call(
        project_kernel,
        grid=(width // PAIR,),
        in_specs=[whole, whole, column, column, column, row],
        out_specs=[out] * 4,
        out_shape=[jax.ShapeDtypeStruct((count, width), BF16)] * 4,
        compiler_params=pltpu.CompilerParams(vmem_limit_bytes=VMEM),
        cost_estimate=SMALL,
        name="projections",
    )(tokens, out_grad, w_query, w_key, w_value, w_output)


def keep_transposed(parts, turned_ref):
    @pl.when(pl.program_id(0) == 0)
    def _():
        for i, part in enumerate(parts):
            turned_ref[i * part.shape[1] : (i + 1) * part.shape[1], :] = part[...].T


def main_kernel(
    core_ref, bias_ref, q_ref, k_ref, v_ref, a_ref, g_ref, xl_ref, wk_ref, wv_ref, x0, x1, x2, x3,
    dq_ref, dk_ref, dv_ref, pk_ref, pv_ref, sq_ref, kq_ref, so_ref, ko_ref, turned_ref, att_ref,
):
    keep_transposed((x0, x1, x2, x3), turned_ref)
    upper = upper_triangle()
    blocks = q_ref.shape[0] // WIN
    span = [slice(b * WIN, (b + 1) * WIN) for b in range(blocks)]
    keys_l = bf(dot(xl_ref[...], wk_ref[...], 1, 0))
    values_l = bf(dot(xl_ref[...], wv_ref[...], 1, 0))
    for h in range(PAIR // HD):
        c = slice(h * HD, (h + 1) * HD)
        keys = [keys_l[:, c]] + [k_ref[s, c] for s in span]
        values = [values_l[:, c]] + [v_ref[s, c] for s in span]
        block = [
            (q_ref[span[b], c], a_ref[span[b], c], keys[b], values[b], keys[b + 1], values[b + 1])
            for b in range(blocks)
        ]
        scores = [scores_of(block[b], bias_ref[0] if b == 0 else None) for b in range(blocks)]
        weights = [probs_of(scores[b], upper) for b in range(blocks)]
        deltas = []
        for b in range(blocks):
            attended, delta = delta_of(block[b], weights[b])
            att_ref[span[b], c] = attended
            deltas.append(delta)
        sgrads = [score_grads(scores[b], weights[b], deltas[b]) for b in range(blocks)]
        for b in range(blocks):
            query, grad, key_l, _, key_r, _ = block[b]
            ds_l, ds_r = sgrads[b]
            _, pb_l, pb_r = weights[b]
            dq_ref[span[b], c] = bf((dot(ds_l, key_l, 1, 0) + dot(ds_r, key_r, 1, 0)) * SCALE)
            if b > 0:
                dk_ref[span[b - 1], c] = bf((dk_open + dot(ds_l, query, 0, 0)) * SCALE)
                dv_ref[span[b - 1], c] = bf(dv_open + dot(pb_l, grad, 0, 0))
            dk_open = dot(ds_r, query, 0, 0)
            dv_open = dot(pb_r, grad, 0, 0)
        pk_ref[:, c] = dk_open
        pv_ref[:, c] = dv_open
    part = dot(turned_ref[...], dq_ref[...], 1, 0)
    half = part.shape[0] // 2
    sq_ref[...] = bf(part[:half])
    kq_ref[...] = bf(part[half:])
    part = bf(dot(att_ref[...], g_ref[...], 0, 0))
    own = lax.rem(pl.program_id(0), 2) == core_ref[0]

    @pl.when(own)
    def _():
        ko_ref[...] = part

    @pl.when(jnp.logical_not(own))
    def _():
        so_ref[...] = part


def token_specs(count):
    def pick(half, other):
        return pl.BlockSpec((count, PAIR), lambda j, c: (0, 2 * half + (1 - c[0] if other else c[0])))

    return [pick(0, True), pick(1, True), pick(0, False), pick(1, False)]


def main_attention(core, bias, queries, keys, values, att_grad, out_grad, tokens_l, w_key, w_value, tokens):
    count, width = queries.shape
    own = pl.BlockSpec((count, PAIR), lambda j, c: (0, j))
    done = pl.BlockSpec((count - WIN, PAIR), lambda j, c: (0, j))
    rim = pl.BlockSpec((WIN, PAIR), lambda j, c: (0, j))
    left = pl.BlockSpec((WIN, width), lambda j, c: (0, 0))
    whole = pl.BlockSpec((count, width), lambda j, c: (0, 0))
    column = pl.BlockSpec((width, PAIR), lambda j, c: (0, j))
    half = pl.BlockSpec((width // 2, PAIR), lambda j, c: (0, j))
    band = pl.BlockSpec((PAIR, width), lambda j, c: (j // 2, 0))
    sums = jax.ShapeDtypeStruct((width // 2, width), BF16)
    part = jax.ShapeDtypeStruct((WIN, width), F32)
    return pl.pallas_call(
        main_kernel,
        grid_spec=pltpu.PrefetchScalarGridSpec(
            num_scalar_prefetch=1,
            grid=(width // PAIR,),
            in_specs=[pl.BlockSpec(memory_space=pltpu.SMEM), own, own, own, own, whole, left, column, column]
            + token_specs(count),
            out_specs=[own, done, done, rim, rim, half, half, band, band],
            scratch_shapes=[pltpu.VMEM((width, count), BF16), pltpu.VMEM((count, PAIR), BF16)],
        ),
        out_shape=[
            jax.ShapeDtypeStruct((count, width), BF16),
            jax.ShapeDtypeStruct((count - WIN, width), BF16),
            jax.ShapeDtypeStruct((count - WIN, width), BF16),
            part, part, sums, sums, sums, sums,
        ],
        compiler_params=pltpu.CompilerParams(vmem_limit_bytes=VMEM),
        cost_estimate=SMALL,
        name="attention_main",
    )(core, bias, queries, keys, values, att_grad, out_grad, tokens_l, w_key, w_value, *[tokens] * 4)


def rim_kernel(
    core_ref, xn_ref, gn_ref, wq_ref, wk_ref, wv_ref, wo_ref, k_ref, v_ref, pk_ref, pv_ref, dkm_ref, dvm_ref,
    x0, x1, x2, x3, dk_ref, dv_ref, sk_ref, kk_ref, sv_ref, kv_ref, turned_ref,
):
    keep_transposed((x0, x1, x2, x3), turned_ref)
    upper = upper_triangle()
    tokens = xn_ref[...]
    queries = bf(dot(tokens, wq_ref[...], 1, 0))
    keys = bf(dot(tokens, wk_ref[...], 1, 0))
    values = bf(dot(tokens, wv_ref[...], 1, 0))
    grads = bf(dot(gn_ref[...], wo_ref[...], 1, 1))
    columns = [slice(h * HD, (h + 1) * HD) for h in range(PAIR // HD)]
    block = [
        (queries[:, c], grads[:, c], k_ref[:, c], v_ref[:, c], keys[:, c], values[:, c]) for c in columns
    ]
    scores = [scores_of(entry, None) for entry in block]
    weights = [probs_of(entry, upper) for entry in scores]
    deltas = [delta_of(*entry)[1] for entry in zip(block, weights)]
    early = dkm_ref.shape[0]
    dk_ref[:early, :] = dkm_ref[...]
    dv_ref[:early, :] = dvm_ref[...]
    for h, c in enumerate(columns):
        ds_l = score_grads(scores[h], weights[h], deltas[h])[0]
        dk_ref[early:, c] = bf((pk_ref[:, c] + dot(ds_l, block[h][0], 0, 0)) * SCALE)
        dv_ref[early:, c] = bf(pv_ref[:, c] + dot(weights[h][1], block[h][1], 0, 0))
    half = turned_ref.shape[0] // 2
    part = dot(turned_ref[...], dk_ref[...], 1, 0)
    sk_ref[...] = bf(part[:half])
    kk_ref[...] = bf(part[half:])
    part = dot(turned_ref[...], dv_ref[...], 1, 0)
    sv_ref[...] = bf(part[:half])
    kv_ref[...] = bf(part[half:])


def rim_attention(
    core, tokens_n, grads_n, w_query, w_key, w_value, w_output, keys, values, part_k, part_v, key_grad, value_grad,
    tokens,
):
    count, width = keys.shape
    column = pl.BlockSpec((width, PAIR), lambda j, c: (0, j))
    row = pl.BlockSpec((PAIR, width), lambda j, c: (j, 0))
    rim = pl.BlockSpec((WIN, PAIR), lambda j, c: (0, j))
    last = pl.BlockSpec((WIN, PAIR), lambda j, c: (count // WIN - 1, j))
    near = pl.BlockSpec((WIN, width), lambda j, c: (0, 0))
    done = pl.BlockSpec((count - WIN, PAIR), lambda j, c: (0, j))
    own = pl.BlockSpec((count, PAIR), lambda j, c: (0, j))
    half = pl.BlockSpec((width // 2, PAIR), lambda j, c: (0, j))
    full = jax.ShapeDtypeStruct((count, width), BF16)
    sums = jax.ShapeDtypeStruct((width // 2, width), BF16)
    return pl.pallas_call(
        rim_kernel,
        grid_spec=pltpu.PrefetchScalarGridSpec(
            num_scalar_prefetch=1,
            grid=(width // PAIR,),
            in_specs=[near, near, column, column, column, row, last, last, rim, rim, done, done]
            + token_specs(count),
            out_specs=[own, own, half, half, half, half],
            scratch_shapes=[pltpu.VMEM((width, count), BF16)],
        ),
        out_shape=[full, full, sums, sums, sums, sums],
        compiler_params=pltpu.CompilerParams(vmem_limit_bytes=VMEM),
        cost_estimate=SMALL,
        name="attention_rim",
    )(
        core, tokens_n, grads_n, w_query, w_key, w_value, w_output, keys, values, part_k, part_v,
        key_grad, value_grad, *[tokens] * 4,
    )


def chip_sum(sends, keeps):
    got = [lax.ppermute(send, "co", [(0, 1), (1, 0)]) for send in sends]
    both = [keep.astype(F32) + extra.astype(F32) for keep, extra in zip(keeps, got)]
    return bf(jnp.concatenate(both, axis=1))


def passed_along(block, distance):
    size = 1
    for axis in SEQ:
        size *= lax.axis_size(axis)
    route = [(i - distance, i) for i in range(size) if 0 <= i - distance < size]
    return lax.ppermute(block, SEQ, route)


def on_device(tokens, out_grad, w_query, w_key, w_value, w_output, grad_accum):
    tokens = tokens[0]
    out_grad = out_grad[0]
    count, width = tokens.shape
    core = lax.axis_index("co")
    which = core.reshape(1)
    tokens_l = passed_along(tokens[count - WIN :], 1)
    queries, keys, values, att_grad = projections(tokens, out_grad, w_query, w_key, w_value, w_output)
    head_x, head_g, tokens_l, keys = lax.optimization_barrier((tokens[:WIN], out_grad[:WIN], tokens_l, keys))
    tokens_n = passed_along(head_x, -1)
    grads_n = passed_along(head_g, -1)
    first = (lax.axis_index("y") + lax.axis_index("z") + lax.axis_index("xl")) == 0
    bias = jnp.where(first, NEG, 0.0).astype(F32).reshape(1)
    query_grad, key_grad, value_grad, part_k, part_v, send_q, keep_q, send_o, keep_o = main_attention(
        which, bias, queries, keys, values, att_grad, out_grad, tokens_l, w_key, w_value, tokens
    )
    send_q, send_o, tokens_n, grads_n = lax.optimization_barrier((send_q, send_o, tokens_n, grads_n))
    both = chip_sum((send_q, send_o), (keep_q, keep_o))
    pieces_qo = lax.all_to_all(both, CHIPS, 0, 0, tiled=True)
    part_k, part_v, _ = lax.optimization_barrier((part_k, part_v, both))
    key_grad, value_grad, send_k, keep_k, send_v, keep_v = rim_attention(
        which, tokens_n, grads_n, w_query, w_key, w_value, w_output,
        keys, values, part_k, part_v, key_grad, value_grad, tokens,
    )
    both = chip_sum((send_k, send_v), (keep_k, keep_v))
    pieces_kv = lax.all_to_all(both, CHIPS, 0, 0, tiled=True)
    in_grad = bf(
        dot(query_grad, w_query, 1, 1) + dot(key_grad, w_key, 1, 1) + dot(value_grad, w_value, 1, 1)
    )
    sum_qo, sum_kv = [
        jnp.sum(pieces.reshape(-1, 8, 2 * width).astype(F32), axis=0) for pieces in (pieces_qo, pieces_kv)
    ]
    total = count
    for axis in AXES:
        total *= lax.axis_size(axis)
    factor = 1.0 / total**0.5
    summed = jnp.concatenate([sum_qo[:, :width], sum_kv, sum_qo[:, width:]], axis=1)
    return in_grad[None], grad_accum + summed * factor


def solution(mesh):
    fine = Mesh(mesh.devices.reshape(2, 2, 4, 4, 2), AXES)
    rows = P(("xh", "co"), SEQ, None)
    accum = P(AXES, None)
    return jax.shard_map(
        on_device,
        mesh=fine,
        in_specs=(rows, rows, P(), P(), P(), P(), accum),
        out_specs=(rows, accum),
        check_vma=False,
    )
```

```python
import jax
import jax.numpy as jnp
from jax import lax
from jax.experimental import pallas as pl
from jax.experimental.pallas import tpu as pltpu
from jax.sharding import Mesh
from jax.sharding import PartitionSpec as P

HD = 128
WIN = 256
LOG2E = 1.4426950408889634
SCALE = 1.0 / HD**0.5
AXES = ("xh", "co", "y", "z", "xl")
SEQ = ("y", "z", "xl")
CHIPS = ("xh", "y", "z", "xl")
F32 = jnp.float32
BF16 = jnp.bfloat16


def dot(a, b, ca, cb):
    return lax.dot_general(a, b, (((ca,), (cb,)), ((), ())), preferred_element_type=F32)


SMALL = pl.CostEstimate(flops=10**8, bytes_accessed=10**5, transcendentals=0)
VMEM = 60 * 2**20
PAIR = 2 * HD
HALF = WIN // 2
NEG = -1e30


def bf(value):
    return value.astype(BF16)


def quads(a, b, c, d):
    return jnp.concatenate([jnp.concatenate([a, b], axis=1), jnp.concatenate([c, d], axis=1)], axis=0)


def upper_triangle():
    rows = lax.broadcasted_iota(jnp.int32, (HALF, HALF), 0)
    cols = lax.broadcasted_iota(jnp.int32, (HALF, HALF), 1)
    return cols > rows


def scores_of(block, bias):
    query, grad, key_l, value_l, key_r, value_r = block
    s_l = dot(query, key_l, 1, 1)
    if bias is not None:
        s_l = s_l + bias
    return s_l, dot(query, key_r, 1, 1), dot(grad, value_l, 1, 1), dot(grad, value_r, 1, 1)


def probs_of(scores, upper):
    s_l, s_r = scores[:2]
    low = slice(0, HALF)
    high = slice(HALF, WIN)
    runs = (
        (jnp.where(upper, s_l[low, low], NEG), s_l[low, high], jnp.where(upper, NEG, s_r[low, low])),
        (jnp.where(upper, s_l[high, high], NEG), s_r[high, low], jnp.where(upper, NEG, s_r[high, high])),
    )
    probs = []
    for run in runs:
        top = jnp.max(jnp.maximum(jnp.maximum(run[0], run[1]), run[2]), axis=1, keepdims=True)
        shift = top * (SCALE * LOG2E)
        e = [jnp.exp2(part * (SCALE * LOG2E) - shift) for part in run]
        inv = 1.0 / jnp.sum(e[0] + e[1] + e[2], axis=1, keepdims=True)
        probs.append([part * inv for part in e])
    zero = jnp.zeros((HALF, HALF), BF16)
    (t0, t1, t2), (b0, b1, b2) = probs
    return probs, quads(bf(t0), bf(t1), zero, bf(b0)), quads(bf(t2), zero, bf(b1), bf(b2))


def delta_of(block, weights):
    grad, value_l, value_r = block[1], block[3], block[5]
    attended = bf(dot(weights[1], value_l, 1, 0) + dot(weights[2], value_r, 1, 0))
    return attended, jnp.sum(grad.astype(F32) * attended.astype(F32), axis=1, keepdims=True)


def score_grads(scores, weights, delta):
    d_l, d_r = scores[2:]
    low = slice(0, HALF)
    high = slice(HALF, WIN)
    (t0, t1, t2), (b0, b1, b2) = weights[0]
    dt = delta[low]
    db = delta[high]
    zero = jnp.zeros((HALF, HALF), BF16)
    left = quads(
        bf(t0 * (d_l[low, low] - dt)), bf(t1 * (d_l[low, high] - dt)), zero, bf(b0 * (d_l[high, high] - db))
    )
    right = quads(
        bf(t2 * (d_r[low, low] - dt)), zero, bf(b1 * (d_r[high, low] - db)), bf(b2 * (d_r[high, high] - db))
    )
    return left, right


def keep_transposed(parts, turned_ref):
    @pl.when(pl.program_id(0) == 0)
    def _():
        for i, part in enumerate(parts):
            turned_ref[i * part.shape[1] : (i + 1) * part.shape[1], :] = part[...].T


def token_specs(count):
    def pick(half, other):
        return pl.BlockSpec((count, PAIR), lambda j, c: (0, 2 * half + (1 - c[0] if other else c[0])))

    return [pick(0, True), pick(1, True), pick(0, False), pick(1, False)]


def lanes():
    return [slice(h * HD, (h + 1) * HD) for h in range(PAIR // HD)]


def front_kernel(
    x_ref, g_ref, wq_ref, wk_ref, wv_ref, wo_ref,
    xh_ref, gh_ref, q0_ref, k0_ref, v0_ref, a0_ref, kz_ref, vz_ref, att_ref, dq_ref, dk_ref, dv_ref,
    pk0_ref, pv0_ref, pkz_ref, pvz_ref, q_ref, k_ref, v_ref, a_ref,
):
    @pl.when(pl.program_id(0) == 0)
    def _():
        xh_ref[...] = x_ref[:WIN, :]
        gh_ref[...] = g_ref[:WIN, :]

    upper = upper_triangle()
    count = x_ref.shape[0]
    blocks = count // WIN
    span = [slice(b * WIN, (b + 1) * WIN) for b in range(blocks)]
    q_ref[...] = bf(dot(x_ref[...], wq_ref[...], 1, 0))
    k_ref[...] = bf(dot(x_ref[...], wk_ref[...], 1, 0))
    v_ref[...] = bf(dot(x_ref[...], wv_ref[...], 1, 0))
    a_ref[...] = bf(dot(g_ref[...], wo_ref[...], 1, 1))
    q0_ref[...] = q_ref[:WIN, :]
    k0_ref[...] = k_ref[:WIN, :]
    v0_ref[...] = v_ref[:WIN, :]
    a0_ref[...] = a_ref[:WIN, :]
    kz_ref[...] = k_ref[count - WIN :, :]
    vz_ref[...] = v_ref[count - WIN :, :]
    for c in lanes():
        block = [
            tuple(
                ref[span[i], c]
                for ref, i in ((q_ref, b), (a_ref, b), (k_ref, b - 1), (v_ref, b - 1), (k_ref, b), (v_ref, b))
            )
            for b in range(1, blocks)
        ]
        scores = [scores_of(entry, None) for entry in block]
        weights = [probs_of(entry, upper) for entry in scores]
        deltas = []
        for i, entry in enumerate(block):
            attended, delta = delta_of(entry, weights[i])
            att_ref[span[i], c] = attended
            deltas.append(delta)
        sgrads = [score_grads(*entry) for entry in zip(scores, weights, deltas)]
        for i, (query, grad, key_l, _, key_r, _) in enumerate(block):
            ds_l, ds_r = sgrads[i]
            _, pb_l, pb_r = weights[i]
            dq_ref[span[i], c] = bf((dot(ds_l, key_l, 1, 0) + dot(ds_r, key_r, 1, 0)) * SCALE)
            dk_l = dot(ds_l, query, 0, 0)
            dv_l = dot(pb_l, grad, 0, 0)
            if i == 0:
                pk0_ref[:, c] = dk_l
                pv0_ref[:, c] = dv_l
            else:
                dk_ref[span[i - 1], c] = bf((dk_open + dk_l) * SCALE)
                dv_ref[span[i - 1], c] = bf(dv_open + dv_l)
            dk_open = dot(ds_r, query, 0, 0)
            dv_open = dot(pb_r, grad, 0, 0)
        pkz_ref[:, c] = dk_open
        pvz_ref[:, c] = dv_open


def front(tokens, out_grad, w_query, w_key, w_value, w_output):
    count, width = tokens.shape
    whole = pl.BlockSpec((count, width), lambda j: (0, 0))
    column = pl.BlockSpec((width, PAIR), lambda j: (0, j))
    row = pl.BlockSpec((PAIR, width), lambda j: (j, 0))

    def out(rows):
        return pl.BlockSpec((rows, PAIR), lambda j: (0, j))

    def like(rows, dtype=BF16):
        return jax.ShapeDtypeStruct((rows, width), dtype)

    rim, late, mid = WIN, count - WIN, count - 2 * WIN
    heights = [rim] * 6 + [late, late, mid, mid]
    return pl.pallas_call(
        front_kernel,
        grid=(width // PAIR,),
        in_specs=[whole, whole, column, column, column, row],
        out_specs=[pl.BlockSpec((WIN, width), lambda j: (0, 0))] * 2 + [out(h) for h in heights] + [out(rim)] * 4,
        out_shape=[like(WIN)] * 2 + [like(h) for h in heights] + [like(rim, F32)] * 4,
        scratch_shapes=[pltpu.VMEM((count, PAIR), BF16)] * 4,
        compiler_params=pltpu.CompilerParams(vmem_limit_bytes=VMEM),
        cost_estimate=SMALL,
        name="front",
    )(tokens, out_grad, w_query, w_key, w_value, w_output)


def first_kernel(
    core_ref, bias_ref, q_ref, k_ref, v_ref, a_ref, pk_ref, pv_ref, att_in, dq_in, g_ref, xl_ref, wk_ref, wv_ref,
    x0, x1, x2, x3, dq_ref, dk_ref, dv_ref, sq_ref, kq_ref, so_ref, ko_ref, turned_ref, att_ref,
):
    keep_transposed((x0, x1, x2, x3), turned_ref)
    upper = upper_triangle()
    keys_l = bf(dot(xl_ref[...], wk_ref[...], 1, 0))
    values_l = bf(dot(xl_ref[...], wv_ref[...], 1, 0))
    block = [
        (q_ref[:, c], a_ref[:, c], keys_l[:, c], values_l[:, c], k_ref[:, c], v_ref[:, c]) for c in lanes()
    ]
    scores = [scores_of(entry, bias_ref[0]) for entry in block]
    weights = [probs_of(entry, upper) for entry in scores]
    deltas = []
    for i, c in enumerate(lanes()):
        attended, delta = delta_of(block[i], weights[i])
        att_ref[:WIN, c] = attended
        deltas.append(delta)
    att_ref[WIN:, :] = att_in[...]
    dq_ref[WIN:, :] = dq_in[...]
    for i, c in enumerate(lanes()):
        query, grad, key_l, _, key_r, _ = block[i]
        ds_l, ds_r = score_grads(scores[i], weights[i], deltas[i])
        dq_ref[:WIN, c] = bf((dot(ds_l, key_l, 1, 0) + dot(ds_r, key_r, 1, 0)) * SCALE)
        dk_ref[:, c] = bf((pk_ref[:, c] + dot(ds_r, query, 0, 0)) * SCALE)
        dv_ref[:, c] = bf(pv_ref[:, c] + dot(weights[i][2], grad, 0, 0))
    part = dot(turned_ref[...], dq_ref[...], 1, 0)
    half = part.shape[0] // 2
    sq_ref[...] = bf(part[:half])
    kq_ref[...] = bf(part[half:])
    part = bf(dot(att_ref[...], g_ref[...], 0, 0))
    own = lax.rem(pl.program_id(0), 2) == core_ref[0]

    @pl.when(own)
    def _():
        ko_ref[...] = part

    @pl.when(jnp.logical_not(own))
    def _():
        so_ref[...] = part


def first_block(core, bias, own, partial, late, out_grad, tokens_l, w_key, w_value, tokens):
    count, width = tokens.shape
    rim = pl.BlockSpec((WIN, PAIR), lambda j, c: (0, j))
    rest = pl.BlockSpec((count - WIN, PAIR), lambda j, c: (0, j))
    full = pl.BlockSpec((count, PAIR), lambda j, c: (0, j))
    left = pl.BlockSpec((WIN, width), lambda j, c: (0, 0))
    whole = pl.BlockSpec((count, width), lambda j, c: (0, 0))
    column = pl.BlockSpec((width, PAIR), lambda j, c: (0, j))
    half = pl.BlockSpec((width // 2, PAIR), lambda j, c: (0, j))
    band = pl.BlockSpec((PAIR, width), lambda j, c: (j // 2, 0))
    sums = jax.ShapeDtypeStruct((width // 2, width), BF16)
    part = jax.ShapeDtypeStruct((WIN, width), BF16)
    return pl.pallas_call(
        first_kernel,
        grid_spec=pltpu.PrefetchScalarGridSpec(
            num_scalar_prefetch=1,
            grid=(width // PAIR,),
            in_specs=[pl.BlockSpec(memory_space=pltpu.SMEM)]
            + [rim] * 6
            + [rest, rest, whole, left, column, column]
            + token_specs(count),
            out_specs=[full, rim, rim, half, half, band, band],
            scratch_shapes=[pltpu.VMEM((width, count), BF16), pltpu.VMEM((count, PAIR), BF16)],
        ),
        out_shape=[jax.ShapeDtypeStruct((count, width), BF16), part, part, sums, sums, sums, sums],
        compiler_params=pltpu.CompilerParams(vmem_limit_bytes=VMEM),
        cost_estimate=SMALL,
        name="first_block",
    )(core, bias, *own, *partial, *late, out_grad, tokens_l, w_key, w_value, *[tokens] * 4)


def last_kernel(
    core_ref, xn_ref, gn_ref, wq_ref, wk_ref, wv_ref, wo_ref, k_ref, v_ref, pk_ref, pv_ref, dk0_ref, dv0_ref,
    dkm_ref, dvm_ref, x0, x1, x2, x3, dk_ref, dv_ref, sk_ref, kk_ref, sv_ref, kv_ref, turned_ref,
):
    keep_transposed((x0, x1, x2, x3), turned_ref)
    upper = upper_triangle()
    tokens = xn_ref[...]
    queries = bf(dot(tokens, wq_ref[...], 1, 0))
    keys = bf(dot(tokens, wk_ref[...], 1, 0))
    values = bf(dot(tokens, wv_ref[...], 1, 0))
    grads = bf(dot(gn_ref[...], wo_ref[...], 1, 1))
    block = [
        (queries[:, c], grads[:, c], k_ref[:, c], v_ref[:, c], keys[:, c], values[:, c]) for c in lanes()
    ]
    scores = [scores_of(entry, None) for entry in block]
    weights = [probs_of(entry, upper) for entry in scores]
    deltas = [delta_of(*entry)[1] for entry in zip(block, weights)]
    end = dk_ref.shape[0] - WIN
    dk_ref[:WIN, :] = dk0_ref[...]
    dv_ref[:WIN, :] = dv0_ref[...]
    dk_ref[WIN:end, :] = dkm_ref[...]
    dv_ref[WIN:end, :] = dvm_ref[...]
    for i, c in enumerate(lanes()):
        ds_l = score_grads(scores[i], weights[i], deltas[i])[0]
        dk_ref[end:, c] = bf((pk_ref[:, c] + dot(ds_l, block[i][0], 0, 0)) * SCALE)
        dv_ref[end:, c] = bf(pv_ref[:, c] + dot(weights[i][1], block[i][1], 0, 0))
    half = turned_ref.shape[0] // 2
    part = dot(turned_ref[...], dk_ref[...], 1, 0)
    sk_ref[...] = bf(part[:half])
    kk_ref[...] = bf(part[half:])
    part = dot(turned_ref[...], dv_ref[...], 1, 0)
    sv_ref[...] = bf(part[:half])
    kv_ref[...] = bf(part[half:])


def last_block(core, tokens_n, grads_n, weights, last, partial, first, middle, tokens):
    count, width = tokens.shape
    column = pl.BlockSpec((width, PAIR), lambda j, c: (0, j))
    row = pl.BlockSpec((PAIR, width), lambda j, c: (j, 0))
    rim = pl.BlockSpec((WIN, PAIR), lambda j, c: (0, j))
    near = pl.BlockSpec((WIN, width), lambda j, c: (0, 0))
    mid = pl.BlockSpec((count - 2 * WIN, PAIR), lambda j, c: (0, j))
    full = pl.BlockSpec((count, PAIR), lambda j, c: (0, j))
    half = pl.BlockSpec((width // 2, PAIR), lambda j, c: (0, j))
    grad = jax.ShapeDtypeStruct((count, width), BF16)
    sums = jax.ShapeDtypeStruct((width // 2, width), BF16)
    return pl.pallas_call(
        last_kernel,
        grid_spec=pltpu.PrefetchScalarGridSpec(
            num_scalar_prefetch=1,
            grid=(width // PAIR,),
            in_specs=[near, near, column, column, column, row] + [rim] * 6 + [mid, mid] + token_specs(count),
            out_specs=[full, full, half, half, half, half],
            scratch_shapes=[pltpu.VMEM((width, count), BF16)],
        ),
        out_shape=[grad, grad, sums, sums, sums, sums],
        compiler_params=pltpu.CompilerParams(vmem_limit_bytes=VMEM),
        cost_estimate=SMALL,
        name="last_block",
    )(core, tokens_n, grads_n, *weights, *last, *partial, *first, *middle, *[tokens] * 4)


def chip_sum(sends, keeps):
    got = [lax.ppermute(send, "co", [(0, 1), (1, 0)]) for send in sends]
    both = [keep.astype(F32) + extra.astype(F32) for keep, extra in zip(keeps, got)]
    return bf(jnp.concatenate(both, axis=1))


def passed_along(block, distance):
    size = 1
    for axis in SEQ:
        size *= lax.axis_size(axis)
    route = [(i - distance, i) for i in range(size) if 0 <= i - distance < size]
    return lax.ppermute(block, SEQ, route)


def on_device(tokens, out_grad, w_query, w_key, w_value, w_output, grad_accum):
    tokens = tokens[0]
    out_grad = out_grad[0]
    count, width = tokens.shape
    core = lax.axis_index("co")
    which = core.reshape(1)
    first = (lax.axis_index("y") + lax.axis_index("z") + lax.axis_index("xl")) == 0
    bias = jnp.where(first, NEG, 0.0).astype(F32).reshape(1)
    tokens_l = passed_along(tokens[count - WIN :], 1)
    weights = (w_query, w_key, w_value, w_output)
    head_x, head_g, *rest = front(tokens, out_grad, *weights)
    own, last, late, middle, partial_0, partial_z = rest[:4], rest[4:6], rest[6:8], rest[8:10], rest[10:12], rest[12:]
    tokens_n = passed_along(head_x, -1)
    grads_n = passed_along(head_g, -1)
    query_grad, key_0, value_0, send_q, keep_q, send_o, keep_o = first_block(
        which, bias, own, partial_0, late, out_grad, tokens_l, w_key, w_value, tokens
    )
    send_q, send_o, tokens_n = lax.optimization_barrier((send_q, send_o, tokens_n))
    both = chip_sum((send_q, send_o), (keep_q, keep_o))
    pieces_qo = lax.all_to_all(both, CHIPS, 0, 0, tiled=True)
    tokens_n, _ = lax.optimization_barrier((tokens_n, both))
    key_grad, value_grad, send_k, keep_k, send_v, keep_v = last_block(
        which, tokens_n, grads_n, weights, last, partial_z, (key_0, value_0), middle, tokens
    )
    both = chip_sum((send_k, send_v), (keep_k, keep_v))
    pieces_kv = lax.all_to_all(both, CHIPS, 0, 0, tiled=True)
    in_grad = bf(
        dot(query_grad, w_query, 1, 1) + dot(key_grad, w_key, 1, 1) + dot(value_grad, w_value, 1, 1)
    )
    sum_qo, sum_kv = [
        jnp.sum(pieces.reshape(-1, 8, 2 * width).astype(F32), axis=0) for pieces in (pieces_qo, pieces_kv)
    ]
    total = count
    for axis in AXES:
        total *= lax.axis_size(axis)
    factor = 1.0 / total**0.5
    summed = jnp.concatenate([sum_qo[:, :width], sum_kv, sum_qo[:, width:]], axis=1)
    return in_grad[None], grad_accum + summed * factor


def solution(mesh):
    fine = Mesh(mesh.devices.reshape(2, 2, 4, 4, 2), AXES)
    rows = P(("xh", "co"), SEQ, None)
    accum = P(AXES, None)
    return jax.shard_map(
        on_device,
        mesh=fine,
        in_specs=(rows, rows, P(), P(), P(), P(), accum),
        out_specs=(rows, accum),
        check_vma=False,
    )
```

```python
import jax
import jax.numpy as jnp
from jax import lax
from jax.experimental import pallas as pl
from jax.experimental.pallas import tpu as pltpu
from jax.sharding import Mesh
from jax.sharding import PartitionSpec as P

HD = 128
WIN = 256
LOG2E = 1.4426950408889634
SCALE = 1.0 / HD**0.5
AXES = ("xh", "co", "y", "z", "xl")
SEQ = ("y", "z", "xl")
CHIPS = ("xh", "y", "z", "xl")
F32 = jnp.float32
BF16 = jnp.bfloat16


def dot(a, b, ca, cb):
    return lax.dot_general(a, b, (((ca,), (cb,)), ((), ())), preferred_element_type=F32)


SMALL = pl.CostEstimate(flops=10**8, bytes_accessed=10**5, transcendentals=0)
VMEM = 60 * 2**20
PAIR = 2 * HD
HALF = WIN // 2
NEG = -1e30


def bf(value):
    return value.astype(BF16)


def quads(a, b, c, d):
    return jnp.concatenate([jnp.concatenate([a, b], axis=1), jnp.concatenate([c, d], axis=1)], axis=0)


def upper_triangle():
    rows = lax.broadcasted_iota(jnp.int32, (HALF, HALF), 0)
    cols = lax.broadcasted_iota(jnp.int32, (HALF, HALF), 1)
    return cols > rows


def scores_of(block, bias):
    query, grad, key_l, value_l, key_r, value_r = block
    s_l = dot(query, key_l, 1, 1)
    if bias is not None:
        s_l = s_l + bias
    return s_l, dot(query, key_r, 1, 1), dot(grad, value_l, 1, 1), dot(grad, value_r, 1, 1)


def probs_of(scores, upper):
    s_l, s_r = scores[:2]
    low = slice(0, HALF)
    high = slice(HALF, WIN)
    runs = (
        (jnp.where(upper, s_l[low, low], NEG), s_l[low, high], jnp.where(upper, NEG, s_r[low, low])),
        (jnp.where(upper, s_l[high, high], NEG), s_r[high, low], jnp.where(upper, NEG, s_r[high, high])),
    )
    probs = []
    for run in runs:
        top = jnp.max(jnp.maximum(jnp.maximum(run[0], run[1]), run[2]), axis=1, keepdims=True)
        shift = top * (SCALE * LOG2E)
        e = [jnp.exp2(part * (SCALE * LOG2E) - shift) for part in run]
        inv = 1.0 / jnp.sum(e[0] + e[1] + e[2], axis=1, keepdims=True)
        probs.append([part * inv for part in e])
    zero = jnp.zeros((HALF, HALF), BF16)
    (t0, t1, t2), (b0, b1, b2) = probs
    return probs, quads(bf(t0), bf(t1), zero, bf(b0)), quads(bf(t2), zero, bf(b1), bf(b2))


def delta_of(block, weights):
    grad, value_l, value_r = block[1], block[3], block[5]
    attended = bf(dot(weights[1], value_l, 1, 0) + dot(weights[2], value_r, 1, 0))
    return attended, jnp.sum(grad.astype(F32) * attended.astype(F32), axis=1, keepdims=True)


def score_grads(scores, weights, delta):
    d_l, d_r = scores[2:]
    low = slice(0, HALF)
    high = slice(HALF, WIN)
    (t0, t1, t2), (b0, b1, b2) = weights[0]
    dt = delta[low]
    db = delta[high]
    zero = jnp.zeros((HALF, HALF), BF16)
    left = quads(
        bf(t0 * (d_l[low, low] - dt)), bf(t1 * (d_l[low, high] - dt)), zero, bf(b0 * (d_l[high, high] - db))
    )
    right = quads(
        bf(t2 * (d_r[low, low] - dt)), zero, bf(b1 * (d_r[high, low] - db)), bf(b2 * (d_r[high, high] - db))
    )
    return left, right


def turned_specs(width, count):
    def pick(half, other):
        return pl.BlockSpec((width // 4, count), lambda j, c: (2 * half + (1 - c[0] if other else c[0]), 0))

    return [pick(0, True), pick(1, True), pick(0, False), pick(1, False)]


def store_product(turned, right, send_refs, keep_ref, start):
    product = bf(dot(jnp.concatenate([part[...] for part in turned], axis=0), right, 1, 0))
    half = product.shape[0] // 2
    columns = pl.ds(pl.multiple_of(start, PAIR), PAIR)
    quarter = half // 2
    for i, send_ref in enumerate(send_refs):
        send_ref[:, columns] = product[i * quarter : (i + 1) * quarter]
    keep_ref[:, columns] = product[half:]


def lanes():
    return [slice(h * HD, (h + 1) * HD) for h in range(PAIR // HD)]


def front_kernel(
    x_ref, g_ref, wq_ref, wk_ref, wv_ref, wo_ref, part_ref,
    turned_ref, q0_ref, k0_ref, v0_ref, a0_ref, kz_ref, vz_ref, att_ref, dq_ref, dk_ref, dv_ref,
    pk0_ref, pv0_ref, pkz_ref, pvz_ref, q_ref, k_ref, v_ref, a_ref,
):
    turned_ref[...] = part_ref[...].T
    upper = upper_triangle()
    count = x_ref.shape[0]
    blocks = count // WIN
    span = [slice(b * WIN, (b + 1) * WIN) for b in range(blocks)]
    q_ref[...] = bf(dot(x_ref[...], wq_ref[...], 1, 0))
    k_ref[...] = bf(dot(x_ref[...], wk_ref[...], 1, 0))
    v_ref[...] = bf(dot(x_ref[...], wv_ref[...], 1, 0))
    a_ref[...] = bf(dot(g_ref[...], wo_ref[...], 1, 1))
    q0_ref[...] = q_ref[:WIN, :]
    k0_ref[...] = k_ref[:WIN, :]
    v0_ref[...] = v_ref[:WIN, :]
    a0_ref[...] = a_ref[:WIN, :]
    kz_ref[...] = k_ref[count - WIN :, :]
    vz_ref[...] = v_ref[count - WIN :, :]
    for c in lanes():
        block = [
            tuple(
                ref[span[i], c]
                for ref, i in ((q_ref, b), (a_ref, b), (k_ref, b - 1), (v_ref, b - 1), (k_ref, b), (v_ref, b))
            )
            for b in range(1, blocks)
        ]
        scores = [scores_of(entry, None) for entry in block]
        weights = [probs_of(entry, upper) for entry in scores]
        deltas = []
        for i, entry in enumerate(block):
            attended, delta = delta_of(entry, weights[i])
            att_ref[span[i], c] = attended
            deltas.append(delta)
        sgrads = [score_grads(*entry) for entry in zip(scores, weights, deltas)]
        for i, (query, grad, key_l, _, key_r, _) in enumerate(block):
            ds_l, ds_r = sgrads[i]
            _, pb_l, pb_r = weights[i]
            dq_ref[span[i], c] = bf((dot(ds_l, key_l, 1, 0) + dot(ds_r, key_r, 1, 0)) * SCALE)
            dk_l = dot(ds_l, query, 0, 0)
            dv_l = dot(pb_l, grad, 0, 0)
            if i == 0:
                pk0_ref[:, c] = dk_l
                pv0_ref[:, c] = dv_l
            else:
                dk_ref[span[i - 1], c] = bf((dk_open + dk_l) * SCALE)
                dv_ref[span[i - 1], c] = bf(dv_open + dv_l)
            dk_open = dot(ds_r, query, 0, 0)
            dv_open = dot(pb_r, grad, 0, 0)
        pkz_ref[:, c] = dk_open
        pvz_ref[:, c] = dv_open


def front(tokens, out_grad, w_query, w_key, w_value, w_output):
    count, width = tokens.shape
    whole = pl.BlockSpec((count, width), lambda j: (0, 0))
    column = pl.BlockSpec((width, PAIR), lambda j: (0, j))
    row = pl.BlockSpec((PAIR, width), lambda j: (j, 0))

    def out(rows):
        return pl.BlockSpec((rows, PAIR), lambda j: (0, j))

    def like(rows, dtype=BF16):
        return jax.ShapeDtypeStruct((rows, width), dtype)

    rim, late, mid = WIN, count - WIN, count - 2 * WIN
    heights = [rim] * 6 + [late, late, mid, mid]
    return pl.pallas_call(
        front_kernel,
        grid=(width // PAIR,),
        in_specs=[whole, whole, column, column, column, row, out(count)],
        out_specs=[row] + [out(h) for h in heights] + [out(rim)] * 4,
        out_shape=[like(width)] + [like(h) for h in heights] + [like(rim, F32)] * 4,
        scratch_shapes=[pltpu.VMEM((count, PAIR), BF16)] * 4,
        compiler_params=pltpu.CompilerParams(vmem_limit_bytes=VMEM),
        cost_estimate=SMALL,
        name="front",
    )(tokens, out_grad, w_query, w_key, w_value, w_output, tokens)


def first_kernel(
    core_ref, bias_ref, q_ref, k_ref, v_ref, a_ref, pk_ref, pv_ref, att_in, dq_in, xl_ref, wk_ref, wv_ref,
    x0, x1, x2, x3, g_hbm, dq_ref, dk_ref, dv_ref, sa_ref, sb_ref, keep_ref, att_ref, g_ref, g_sem,
):
    step = pl.program_id(0)
    fetch = pltpu.make_async_copy(g_hbm, g_ref, g_sem)

    @pl.when(step == 0)
    def _():
        fetch.start()

    side = lax.rem(step, 2)
    att = att_ref.at[side]
    upper = upper_triangle()
    keys_l = bf(dot(xl_ref[...], wk_ref[...], 1, 0))
    values_l = bf(dot(xl_ref[...], wv_ref[...], 1, 0))
    block = [
        (q_ref[:, c], a_ref[:, c], keys_l[:, c], values_l[:, c], k_ref[:, c], v_ref[:, c]) for c in lanes()
    ]
    scores = [scores_of(entry, bias_ref[0]) for entry in block]
    weights = [probs_of(entry, upper) for entry in scores]
    deltas = []
    for i, c in enumerate(lanes()):
        attended, delta = delta_of(block[i], weights[i])
        att[:WIN, c] = attended
        deltas.append(delta)
    att[WIN:, :] = att_in[...]
    dq_ref[WIN:, :] = dq_in[...]
    for i, c in enumerate(lanes()):
        query, grad, key_l, _, key_r, _ = block[i]
        ds_l, ds_r = score_grads(scores[i], weights[i], deltas[i])
        dq_ref[:WIN, c] = bf((dot(ds_l, key_l, 1, 0) + dot(ds_r, key_r, 1, 0)) * SCALE)
        dk_ref[:, c] = bf((pk_ref[:, c] + dot(ds_r, query, 0, 0)) * SCALE)
        dv_ref[:, c] = bf(pv_ref[:, c] + dot(weights[i][2], grad, 0, 0))
    store_product((x0, x1, x2, x3), dq_ref[...], (sa_ref, sb_ref), keep_ref, step * PAIR)

    @pl.when(step == 1)
    def _():
        fetch.wait()

    @pl.when(side == 1)
    def _():
        width = g_ref.shape[1]
        product = bf(dot(jnp.concatenate([att_ref[0], att_ref[1]], axis=1), g_ref[...], 0, 0))
        rows = pl.ds(pl.multiple_of((step // 2) * PAIR, PAIR), PAIR)

        mine = core_ref[0] == 0
        keep_ref[rows, width:] = jnp.where(mine, product[:PAIR], product[PAIR:])
        other = jnp.where(mine, product[PAIR:], product[:PAIR])

        @pl.when(step == 1)
        def _():
            sa_ref[:, width:] = other

        @pl.when(step == 3)
        def _():
            sb_ref[:, width:] = other


def first_block(core, bias, own, partial, late, out_grad, tokens_l, w_key, w_value, turned):
    width, count = turned.shape
    rim = pl.BlockSpec((WIN, PAIR), lambda j, c: (0, j))
    rest = pl.BlockSpec((count - WIN, PAIR), lambda j, c: (0, j))
    full = pl.BlockSpec((count, PAIR), lambda j, c: (0, j))
    left = pl.BlockSpec((WIN, width), lambda j, c: (0, 0))
    column = pl.BlockSpec((width, PAIR), lambda j, c: (0, j))
    sums = pl.BlockSpec((width // 2, 2 * width), lambda j, c: (0, 0))
    both = jax.ShapeDtypeStruct((width // 2, 2 * width), BF16)
    half = pl.BlockSpec((width // 4, 2 * width), lambda j, c: (0, 0))
    part_sum = jax.ShapeDtypeStruct((width // 4, 2 * width), BF16)
    part = jax.ShapeDtypeStruct((WIN, width), BF16)
    return pl.pallas_call(
        first_kernel,
        grid_spec=pltpu.PrefetchScalarGridSpec(
            num_scalar_prefetch=1,
            grid=(width // PAIR,),
            in_specs=[pl.BlockSpec(memory_space=pltpu.SMEM)]
            + [rim] * 6
            + [rest, rest, left, column, column]
            + turned_specs(width, count)
            + [pl.BlockSpec(memory_space=pl.ANY)],
            out_specs=[full, rim, rim, half, half, sums],
            scratch_shapes=[
                pltpu.VMEM((2, count, PAIR), BF16),
                pltpu.VMEM((count, width), BF16),
                pltpu.SemaphoreType.DMA,
            ],
        ),
        out_shape=[jax.ShapeDtypeStruct((count, width), BF16), part, part, part_sum, part_sum, both],
        compiler_params=pltpu.CompilerParams(vmem_limit_bytes=VMEM),
        cost_estimate=SMALL,
        name="first_block",
    )(core, bias, *own, *partial, *late, tokens_l, w_key, w_value, *[turned] * 4, out_grad)


def last_kernel(
    core_ref, xn_ref, gn_ref, wq_ref, wk_ref, wv_ref, wo_ref, k_ref, v_ref, pk_ref, pv_ref, dk0_ref, dv0_ref,
    dkm_ref, dvm_ref, x0, x1, x2, x3, dk_ref, dv_ref, sa_ref, sb_ref, keep_ref,
):
    upper = upper_triangle()
    tokens = xn_ref[...]
    queries = bf(dot(tokens, wq_ref[...], 1, 0))
    keys = bf(dot(tokens, wk_ref[...], 1, 0))
    values = bf(dot(tokens, wv_ref[...], 1, 0))
    grads = bf(dot(gn_ref[...], wo_ref[...], 1, 1))
    block = [
        (queries[:, c], grads[:, c], k_ref[:, c], v_ref[:, c], keys[:, c], values[:, c]) for c in lanes()
    ]
    scores = [scores_of(entry, None) for entry in block]
    weights = [probs_of(entry, upper) for entry in scores]
    deltas = [delta_of(*entry)[1] for entry in zip(block, weights)]
    end = dk_ref.shape[0] - WIN
    dk_ref[:WIN, :] = dk0_ref[...]
    dv_ref[:WIN, :] = dv0_ref[...]
    dk_ref[WIN:end, :] = dkm_ref[...]
    dv_ref[WIN:end, :] = dvm_ref[...]
    for i, c in enumerate(lanes()):
        ds_l = score_grads(scores[i], weights[i], deltas[i])[0]
        dk_ref[end:, c] = bf((pk_ref[:, c] + dot(ds_l, block[i][0], 0, 0)) * SCALE)
        dv_ref[end:, c] = bf(pv_ref[:, c] + dot(weights[i][1], block[i][1], 0, 0))
    start = pl.program_id(0) * PAIR
    store_product((x0, x1, x2, x3), dk_ref[...], (sa_ref, sb_ref), keep_ref, start)
    store_product((x0, x1, x2, x3), dv_ref[...], (sa_ref, sb_ref), keep_ref, start + keep_ref.shape[1] // 2)


def last_block(core, tokens_n, grads_n, weights, last, partial, first, middle, turned):
    width, count = turned.shape
    column = pl.BlockSpec((width, PAIR), lambda j, c: (0, j))
    row = pl.BlockSpec((PAIR, width), lambda j, c: (j, 0))
    rim = pl.BlockSpec((WIN, PAIR), lambda j, c: (0, j))
    near = pl.BlockSpec((WIN, width), lambda j, c: (0, 0))
    mid = pl.BlockSpec((count - 2 * WIN, PAIR), lambda j, c: (0, j))
    full = pl.BlockSpec((count, PAIR), lambda j, c: (0, j))
    sums = pl.BlockSpec((width // 2, 2 * width), lambda j, c: (0, 0))
    grad = jax.ShapeDtypeStruct((count, width), BF16)
    both = jax.ShapeDtypeStruct((width // 2, 2 * width), BF16)
    half = pl.BlockSpec((width // 4, 2 * width), lambda j, c: (0, 0))
    part_sum = jax.ShapeDtypeStruct((width // 4, 2 * width), BF16)
    return pl.pallas_call(
        last_kernel,
        grid_spec=pltpu.PrefetchScalarGridSpec(
            num_scalar_prefetch=1,
            grid=(width // PAIR,),
            in_specs=[near, near, column, column, column, row] + [rim] * 6 + [mid, mid] + turned_specs(width, count),
            out_specs=[full, full, half, half, sums],
        ),
        out_shape=[grad, grad, part_sum, part_sum, both],
        compiler_params=pltpu.CompilerParams(vmem_limit_bytes=VMEM),
        cost_estimate=SMALL,
        name="last_block",
    )(core, tokens_n, grads_n, *weights, *last, *partial, *first, *middle, *[turned] * 4)


def chip_sum(sends, keep):
    got = [lax.ppermute(send, "co", [(0, 1), (1, 0)]) for send in sends]
    return bf(keep.astype(F32) + jnp.concatenate(got, axis=0).astype(F32))


def passed_along(block, distance):
    size = 1
    for axis in SEQ:
        size *= lax.axis_size(axis)
    route = [(i - distance, i) for i in range(size) if 0 <= i - distance < size]
    return lax.ppermute(block, SEQ, route)


def on_device(tokens, out_grad, w_query, w_key, w_value, w_output, grad_accum):
    tokens = tokens[0]
    out_grad = out_grad[0]
    count, width = tokens.shape
    core = lax.axis_index("co")
    which = core.reshape(1)
    first = (lax.axis_index("y") + lax.axis_index("z") + lax.axis_index("xl")) == 0
    bias = jnp.where(first, NEG, 0.0).astype(F32).reshape(1)
    tokens_l = passed_along(tokens[count - WIN :], 1)
    tokens_n = passed_along(tokens[:WIN], -1)
    grads_n = passed_along(out_grad[:WIN], -1)
    weights = (w_query, w_key, w_value, w_output)
    turned, *rest = front(tokens, out_grad, *weights)
    own, last, late, middle, partial_0, partial_z = rest[:4], rest[4:6], rest[6:8], rest[8:10], rest[10:12], rest[12:]
    query_grad, key_0, value_0, send_a, send_b, keep = first_block(
        which, bias, own, partial_0, late, out_grad, tokens_l, w_key, w_value, turned
    )
    send_a, send_b, tokens_n, grads_n = lax.optimization_barrier((send_a, send_b, tokens_n, grads_n))
    both = chip_sum((send_a, send_b), keep)
    pieces_qo = lax.all_to_all(both, CHIPS, 0, 0, tiled=True)
    tokens_n, _ = lax.optimization_barrier((tokens_n, both))
    key_grad, value_grad, send_a, send_b, keep = last_block(
        which, tokens_n, grads_n, weights, last, partial_z, (key_0, value_0), middle, turned
    )
    both = chip_sum((send_a, send_b), keep)
    pieces_kv = lax.all_to_all(both, CHIPS, 0, 0, tiled=True)
    in_grad = bf(
        dot(query_grad, w_query, 1, 1) + dot(key_grad, w_key, 1, 1) + dot(value_grad, w_value, 1, 1)
    )
    sum_qo, sum_kv = [
        jnp.sum(pieces.reshape(-1, 8, 2 * width).astype(F32), axis=0) for pieces in (pieces_qo, pieces_kv)
    ]
    total = count
    for axis in AXES:
        total *= lax.axis_size(axis)
    factor = 1.0 / total**0.5
    summed = jnp.concatenate([sum_qo[:, :width], sum_kv, sum_qo[:, width:]], axis=1)
    return in_grad[None], grad_accum + summed * factor


def solution(mesh):
    fine = Mesh(mesh.devices.reshape(2, 2, 4, 4, 2), AXES)
    rows = P(("xh", "co"), SEQ, None)
    accum = P(AXES, None)
    return jax.shard_map(
        on_device,
        mesh=fine,
        in_specs=(rows, rows, P(), P(), P(), P(), accum),
        out_specs=(rows, accum),
        check_vma=False,
    )
```

```python
import jax
import jax.numpy as jnp
from jax import lax
from jax.experimental import pallas as pl
from jax.experimental.pallas import tpu as pltpu
from jax.sharding import Mesh
from jax.sharding import PartitionSpec as P

HD = 128
WIN = 256
LOG2E = 1.4426950408889634
SCALE = 1.0 / HD**0.5
AXES = ("xh", "co", "y", "z", "xl")
SEQ = ("y", "z", "xl")
CHIPS = ("xh", "y", "z", "xl")
F32 = jnp.float32
BF16 = jnp.bfloat16


def dot(a, b, ca, cb):
    return lax.dot_general(a, b, (((ca,), (cb,)), ((), ())), preferred_element_type=F32)


SMALL = pl.CostEstimate(flops=10**8, bytes_accessed=10**5, transcendentals=0)
VMEM = 60 * 2**20
PAIR = 2 * HD
FOUR = 4 * HD
HALF = WIN // 2
NEG = -1e30


def bf(value):
    return value.astype(BF16)


def quads(a, b, c, d):
    return jnp.concatenate([jnp.concatenate([a, b], axis=1), jnp.concatenate([c, d], axis=1)], axis=0)


def upper_triangle():
    rows = lax.broadcasted_iota(jnp.int32, (HALF, HALF), 0)
    cols = lax.broadcasted_iota(jnp.int32, (HALF, HALF), 1)
    return cols > rows


def scores_of(block, bias):
    query, grad, key_l, value_l, key_r, value_r = block
    s_l = dot(query, key_l, 1, 1)
    if bias is not None:
        s_l = s_l + bias
    return s_l, dot(query, key_r, 1, 1), dot(grad, value_l, 1, 1), dot(grad, value_r, 1, 1)


def probs_of(scores, upper):
    s_l, s_r = scores[:2]
    low = slice(0, HALF)
    high = slice(HALF, WIN)
    runs = (
        (jnp.where(upper, s_l[low, low], NEG), s_l[low, high], jnp.where(upper, NEG, s_r[low, low])),
        (jnp.where(upper, s_l[high, high], NEG), s_r[high, low], jnp.where(upper, NEG, s_r[high, high])),
    )
    probs = []
    for run in runs:
        top = jnp.max(jnp.maximum(jnp.maximum(run[0], run[1]), run[2]), axis=1, keepdims=True)
        shift = top * (SCALE * LOG2E)
        e = [jnp.exp2(part * (SCALE * LOG2E) - shift) for part in run]
        inv = 1.0 / jnp.sum(e[0] + e[1] + e[2], axis=1, keepdims=True)
        probs.append([part * inv for part in e])
    zero = jnp.zeros((HALF, HALF), BF16)
    (t0, t1, t2), (b0, b1, b2) = probs
    return probs, quads(bf(t0), bf(t1), zero, bf(b0)), quads(bf(t2), zero, bf(b1), bf(b2))


def delta_of(block, weights):
    grad, value_l, value_r = block[1], block[3], block[5]
    attended = bf(dot(weights[1], value_l, 1, 0) + dot(weights[2], value_r, 1, 0))
    return attended, jnp.sum(grad.astype(F32) * attended.astype(F32), axis=1, keepdims=True)


def score_grads(scores, weights, delta):
    d_l, d_r = scores[2:]
    low = slice(0, HALF)
    high = slice(HALF, WIN)
    (t0, t1, t2), (b0, b1, b2) = weights[0]
    dt = delta[low]
    db = delta[high]
    zero = jnp.zeros((HALF, HALF), BF16)
    left = quads(
        bf(t0 * (d_l[low, low] - dt)), bf(t1 * (d_l[low, high] - dt)), zero, bf(b0 * (d_l[high, high] - db))
    )
    right = quads(
        bf(t2 * (d_r[low, low] - dt)), zero, bf(b1 * (d_r[high, low] - db)), bf(b2 * (d_r[high, high] - db))
    )
    return left, right


def turned_specs(width, count):
    def pick(half, other):
        return pl.BlockSpec((width // 4, count), lambda j, c: (2 * half + (1 - c[0] if other else c[0]), 0))

    return [pick(0, True), pick(1, True), pick(0, False), pick(1, False)]


def store_product(turned, right, send_refs, keep_ref, start):
    product = bf(dot(jnp.concatenate([part[...] for part in turned], axis=0), right, 1, 0))
    half = product.shape[0] // 2
    columns = pl.ds(pl.multiple_of(start, FOUR), FOUR)
    piece = half // len(send_refs)
    for i, send_ref in enumerate(send_refs):
        send_ref[:, columns] = product[i * piece : (i + 1) * piece]
    keep_ref[:, columns] = product[half:]


def lanes(width):
    return [slice(h * HD, (h + 1) * HD) for h in range(width // HD)]


def front_kernel(
    x_ref, g_ref, wq_ref, wk_ref, wv_ref, wo_ref, part_ref,
    turned_ref, q0_ref, k0_ref, v0_ref, a0_ref, kz_ref, vz_ref, att_ref, dq_ref, dk_ref, dv_ref,
    pk0_ref, pv0_ref, pkz_ref, pvz_ref, q_ref, k_ref, v_ref, a_ref,
):
    turned_ref[...] = part_ref[...].T
    upper = upper_triangle()
    count = x_ref.shape[0]
    blocks = count // WIN
    span = [slice(b * WIN, (b + 1) * WIN) for b in range(blocks)]
    q_ref[...] = bf(dot(x_ref[...], wq_ref[...], 1, 0))
    k_ref[...] = bf(dot(x_ref[...], wk_ref[...], 1, 0))
    v_ref[...] = bf(dot(x_ref[...], wv_ref[...], 1, 0))
    a_ref[...] = bf(dot(g_ref[...], wo_ref[...], 1, 1))
    q0_ref[...] = q_ref[:WIN, :]
    k0_ref[...] = k_ref[:WIN, :]
    v0_ref[...] = v_ref[:WIN, :]
    a0_ref[...] = a_ref[:WIN, :]
    kz_ref[...] = k_ref[count - WIN :, :]
    vz_ref[...] = v_ref[count - WIN :, :]
    entries = [(c, b) for c in lanes(PAIR) for b in range(1, blocks)]
    block = [
        tuple(
            ref[span[i], c]
            for ref, i in ((q_ref, b), (a_ref, b), (k_ref, b - 1), (v_ref, b - 1), (k_ref, b), (v_ref, b))
        )
        for c, b in entries
    ]
    scores = [scores_of(entry, None) for entry in block]
    weights = [probs_of(entry, upper) for entry in scores]
    deltas = []
    for i, (c, b) in enumerate(entries):
        attended, delta = delta_of(block[i], weights[i])
        att_ref[span[b - 1], c] = attended
        deltas.append(delta)
    sgrads = [score_grads(*entry) for entry in zip(scores, weights, deltas)]
    for i, (c, b) in enumerate(entries):
        query, grad, key_l, _, key_r, _ = block[i]
        ds_l, ds_r = sgrads[i]
        _, pb_l, pb_r = weights[i]
        dq_ref[span[b - 1], c] = bf((dot(ds_l, key_l, 1, 0) + dot(ds_r, key_r, 1, 0)) * SCALE)
        dk_l = dot(ds_l, query, 0, 0)
        dv_l = dot(pb_l, grad, 0, 0)
        if b == 1:
            pk0_ref[:, c] = dk_l
            pv0_ref[:, c] = dv_l
        else:
            dk_ref[span[b - 2], c] = bf((dk_open + dk_l) * SCALE)
            dv_ref[span[b - 2], c] = bf(dv_open + dv_l)
        dk_open = dot(ds_r, query, 0, 0)
        dv_open = dot(pb_r, grad, 0, 0)
        if b == blocks - 1:
            pkz_ref[:, c] = dk_open
            pvz_ref[:, c] = dv_open


def front(tokens, out_grad, w_query, w_key, w_value, w_output):
    count, width = tokens.shape
    whole = pl.BlockSpec((count, width), lambda j: (0, 0))
    column = pl.BlockSpec((width, PAIR), lambda j: (0, j))
    row = pl.BlockSpec((PAIR, width), lambda j: (j, 0))

    def out(rows):
        return pl.BlockSpec((rows, PAIR), lambda j: (0, j))

    def like(rows, dtype=BF16):
        return jax.ShapeDtypeStruct((rows, width), dtype)

    rim, late, mid = WIN, count - WIN, count - 2 * WIN
    heights = [rim] * 6 + [late, late, mid, mid]
    return pl.pallas_call(
        front_kernel,
        grid=(width // PAIR,),
        in_specs=[whole, whole, column, column, column, row, out(count)],
        out_specs=[row] + [out(h) for h in heights] + [out(rim)] * 4,
        out_shape=[like(width)] + [like(h) for h in heights] + [like(rim, F32)] * 4,
        scratch_shapes=[pltpu.VMEM((count, PAIR), BF16)] * 4,
        compiler_params=pltpu.CompilerParams(vmem_limit_bytes=VMEM),
        cost_estimate=SMALL,
        name="front",
    )(tokens, out_grad, w_query, w_key, w_value, w_output, tokens)


def first_kernel(
    core_ref, bias_ref, q_ref, k_ref, v_ref, a_ref, pk_ref, pv_ref, att_in, dq_in, xl_ref, wk_ref, wv_ref,
    x0, x1, x2, x3, g_hbm, dq_ref, dk_ref, dv_ref, send_ref, keep_ref, att_ref, g_ref, g_sem,
):
    step = pl.program_id(0)
    fetch = pltpu.make_async_copy(g_hbm, g_ref, g_sem)

    @pl.when(step == 0)
    def _():
        fetch.start()

    upper = upper_triangle()
    keys_l = bf(dot(xl_ref[...], wk_ref[...], 1, 0))
    values_l = bf(dot(xl_ref[...], wv_ref[...], 1, 0))
    block = [
        (q_ref[:, c], a_ref[:, c], keys_l[:, c], values_l[:, c], k_ref[:, c], v_ref[:, c]) for c in lanes(FOUR)
    ]
    scores = [scores_of(entry, bias_ref[0]) for entry in block]
    weights = [probs_of(entry, upper) for entry in scores]
    deltas = []
    for i, c in enumerate(lanes(FOUR)):
        attended, delta = delta_of(block[i], weights[i])
        att_ref[:WIN, c] = attended
        deltas.append(delta)
    att_ref[WIN:, :] = att_in[...]
    dq_ref[WIN:, :] = dq_in[...]
    for i, c in enumerate(lanes(FOUR)):
        query, grad, key_l, _, key_r, _ = block[i]
        ds_l, ds_r = score_grads(scores[i], weights[i], deltas[i])
        dq_ref[:WIN, c] = bf((dot(ds_l, key_l, 1, 0) + dot(ds_r, key_r, 1, 0)) * SCALE)
        dk_ref[:, c] = bf((pk_ref[:, c] + dot(ds_r, query, 0, 0)) * SCALE)
        dv_ref[:, c] = bf(pv_ref[:, c] + dot(weights[i][2], grad, 0, 0))
    store_product((x0, x1, x2, x3), dq_ref[...], (send_ref,), keep_ref, step * FOUR)

    @pl.when(step == 0)
    def _():
        fetch.wait()

    product = bf(dot(att_ref[...], g_ref[...], 0, 0))
    rows = pl.ds(pl.multiple_of(step * PAIR, PAIR), PAIR)
    width = g_ref.shape[1]
    mine = core_ref[0] == 0
    keep_ref[rows, width:] = jnp.where(mine, product[:PAIR], product[PAIR:])
    send_ref[rows, width:] = jnp.where(mine, product[PAIR:], product[:PAIR])


def first_block(core, bias, own, partial, late, out_grad, tokens_l, w_key, w_value, turned):
    width, count = turned.shape
    rim = pl.BlockSpec((WIN, FOUR), lambda j, c: (0, j))
    rest = pl.BlockSpec((count - WIN, FOUR), lambda j, c: (0, j))
    full = pl.BlockSpec((count, FOUR), lambda j, c: (0, j))
    left = pl.BlockSpec((WIN, width), lambda j, c: (0, 0))
    column = pl.BlockSpec((width, FOUR), lambda j, c: (0, j))
    sums = pl.BlockSpec((width // 2, 2 * width), lambda j, c: (0, 0))
    both = jax.ShapeDtypeStruct((width // 2, 2 * width), BF16)
    part = jax.ShapeDtypeStruct((WIN, width), BF16)
    return pl.pallas_call(
        first_kernel,
        grid_spec=pltpu.PrefetchScalarGridSpec(
            num_scalar_prefetch=1,
            grid=(width // FOUR,),
            in_specs=[pl.BlockSpec(memory_space=pltpu.SMEM)]
            + [rim] * 6
            + [rest, rest, left, column, column]
            + turned_specs(width, count)
            + [pl.BlockSpec(memory_space=pl.ANY)],
            out_specs=[full, rim, rim, sums, sums],
            scratch_shapes=[
                pltpu.VMEM((count, FOUR), BF16),
                pltpu.VMEM((count, width), BF16),
                pltpu.SemaphoreType.DMA,
            ],
        ),
        out_shape=[jax.ShapeDtypeStruct((count, width), BF16), part, part, both, both],
        compiler_params=pltpu.CompilerParams(vmem_limit_bytes=VMEM),
        cost_estimate=SMALL,
        name="first_block",
    )(core, bias, *own, *partial, *late, tokens_l, w_key, w_value, *[turned] * 4, out_grad)


def last_kernel(
    core_ref, ahead_ref, wq_ref, wk_ref, wv_ref, wo_ref, k_ref, v_ref, pk_ref, pv_ref, dk0_ref, dv0_ref,
    dkm_ref, dvm_ref, x0, x1, x2, x3, dk_ref, dv_ref, sa_ref, sb_ref, keep_ref,
):
    upper = upper_triangle()
    tokens = ahead_ref[:WIN, :]
    queries = bf(dot(tokens, wq_ref[...], 1, 0))
    keys = bf(dot(tokens, wk_ref[...], 1, 0))
    values = bf(dot(tokens, wv_ref[...], 1, 0))
    grads = bf(dot(ahead_ref[WIN:, :], wo_ref[...], 1, 1))
    block = [
        (queries[:, c], grads[:, c], k_ref[:, c], v_ref[:, c], keys[:, c], values[:, c]) for c in lanes(FOUR)
    ]
    scores = [scores_of(entry, None) for entry in block]
    weights = [probs_of(entry, upper) for entry in scores]
    deltas = [delta_of(*entry)[1] for entry in zip(block, weights)]
    end = dk_ref.shape[0] - WIN
    dk_ref[:WIN, :] = dk0_ref[...]
    dv_ref[:WIN, :] = dv0_ref[...]
    dk_ref[WIN:end, :] = dkm_ref[...]
    dv_ref[WIN:end, :] = dvm_ref[...]
    for i, c in enumerate(lanes(FOUR)):
        ds_l = score_grads(scores[i], weights[i], deltas[i])[0]
        dk_ref[end:, c] = bf((pk_ref[:, c] + dot(ds_l, block[i][0], 0, 0)) * SCALE)
        dv_ref[end:, c] = bf(pv_ref[:, c] + dot(weights[i][1], block[i][1], 0, 0))
    start = pl.program_id(0) * FOUR
    store_product((x0, x1, x2, x3), dk_ref[...], (sa_ref, sb_ref), keep_ref, start)
    store_product((x0, x1, x2, x3), dv_ref[...], (sa_ref, sb_ref), keep_ref, start + keep_ref.shape[1] // 2)


def last_block(core, ahead, weights, last, partial, first, middle, turned):
    width, count = turned.shape
    column = pl.BlockSpec((width, FOUR), lambda j, c: (0, j))
    row = pl.BlockSpec((FOUR, width), lambda j, c: (j, 0))
    rim = pl.BlockSpec((WIN, FOUR), lambda j, c: (0, j))
    near = pl.BlockSpec((2 * WIN, width), lambda j, c: (0, 0))
    mid = pl.BlockSpec((count - 2 * WIN, FOUR), lambda j, c: (0, j))
    full = pl.BlockSpec((count, FOUR), lambda j, c: (0, j))
    sums = pl.BlockSpec((width // 2, 2 * width), lambda j, c: (0, 0))
    grad = jax.ShapeDtypeStruct((count, width), BF16)
    both = jax.ShapeDtypeStruct((width // 2, 2 * width), BF16)
    half = pl.BlockSpec((width // 4, 2 * width), lambda j, c: (0, 0))
    part_sum = jax.ShapeDtypeStruct((width // 4, 2 * width), BF16)
    return pl.pallas_call(
        last_kernel,
        grid_spec=pltpu.PrefetchScalarGridSpec(
            num_scalar_prefetch=1,
            grid=(width // FOUR,),
            in_specs=[near, column, column, column, row] + [rim] * 6 + [mid, mid] + turned_specs(width, count),
            out_specs=[full, full, half, half, sums],
        ),
        out_shape=[grad, grad, part_sum, part_sum, both],
        compiler_params=pltpu.CompilerParams(vmem_limit_bytes=VMEM),
        cost_estimate=SMALL,
        name="last_block",
    )(core, ahead, *weights, *last, *partial, *first, *middle, *[turned] * 4)


def chip_sum(sends, keep):
    got = [lax.ppermute(send, "co", [(0, 1), (1, 0)]) for send in sends]
    return bf(keep.astype(F32) + jnp.concatenate(got, axis=0).astype(F32))


def passed_along(block, distance):
    size = 1
    for axis in SEQ:
        size *= lax.axis_size(axis)
    route = [(i - distance, i) for i in range(size) if 0 <= i - distance < size]
    return lax.ppermute(block, SEQ, route)


def on_device(tokens, out_grad, w_query, w_key, w_value, w_output, grad_accum):
    tokens = tokens[0]
    out_grad = out_grad[0]
    count, width = tokens.shape
    core = lax.axis_index("co")
    which = core.reshape(1)
    first = (lax.axis_index("y") + lax.axis_index("z") + lax.axis_index("xl")) == 0
    bias = jnp.where(first, NEG, 0.0).astype(F32).reshape(1)
    tokens_l = passed_along(tokens[count - WIN :], 1)
    ahead = passed_along(jnp.concatenate([tokens[:WIN], out_grad[:WIN]], axis=0), -1)
    weights = (w_query, w_key, w_value, w_output)
    turned, *rest = front(tokens, out_grad, *weights)
    own, last, late, middle, partial_0, partial_z = rest[:4], rest[4:6], rest[6:8], rest[8:10], rest[10:12], rest[12:]
    query_grad, key_0, value_0, send, keep = first_block(
        which, bias, own, partial_0, late, out_grad, tokens_l, w_key, w_value, turned
    )
    send, ahead = lax.optimization_barrier((send, ahead))
    both = chip_sum((send,), keep)
    pieces_qo = lax.all_to_all(both, CHIPS, 0, 0, tiled=True)
    ahead, _ = lax.optimization_barrier((ahead, both))
    key_grad, value_grad, send_a, send_b, keep = last_block(
        which, ahead, weights, last, partial_z, (key_0, value_0), middle, turned
    )
    both = chip_sum((send_a, send_b), keep)
    pieces_kv = lax.all_to_all(both, CHIPS, 0, 0, tiled=True)
    in_grad = bf(
        dot(query_grad, w_query, 1, 1) + dot(key_grad, w_key, 1, 1) + dot(value_grad, w_value, 1, 1)
    )
    sum_qo, sum_kv = [
        jnp.sum(pieces.reshape(-1, 8, 2 * width).astype(F32), axis=0) for pieces in (pieces_qo, pieces_kv)
    ]
    total = count
    for axis in AXES:
        total *= lax.axis_size(axis)
    factor = 1.0 / total**0.5
    summed = jnp.concatenate([sum_qo[:, :width], sum_kv, sum_qo[:, width:]], axis=1)
    return in_grad[None], grad_accum + summed * factor


def solution(mesh):
    fine = Mesh(mesh.devices.reshape(2, 2, 4, 4, 2), AXES)
    rows = P(("xh", "co"), SEQ, None)
    accum = P(AXES, None)
    return jax.shard_map(
        on_device,
        mesh=fine,
        in_specs=(rows, rows, P(), P(), P(), P(), accum),
        out_specs=(rows, accum),
        check_vma=False,
    )
```

```python
import jax
import jax.numpy as jnp
from jax import lax
from jax.experimental import pallas as pl
from jax.experimental.pallas import tpu as pltpu
from jax.sharding import Mesh
from jax.sharding import PartitionSpec as P

HD = 128
WIN = 256
LOG2E = 1.4426950408889634
SCALE = 1.0 / HD**0.5
AXES = ("xh", "co", "y", "z", "xl")
SEQ = ("y", "z", "xl")
CHIPS = ("xh", "y", "z", "xl")
F32 = jnp.float32
BF16 = jnp.bfloat16


def dot(a, b, ca, cb):
    return lax.dot_general(a, b, (((ca,), (cb,)), ((), ())), preferred_element_type=F32)


SMALL = pl.CostEstimate(flops=10**8, bytes_accessed=10**5, transcendentals=0)
VMEM = 60 * 2**20
PAIR = 2 * HD
FOUR = 4 * HD
HALF = WIN // 2
NEG = -1e30


def bf(value):
    return value.astype(BF16)


def upper_triangle():
    rows = lax.broadcasted_iota(jnp.int32, (HALF, HALF), 0)
    cols = lax.broadcasted_iota(jnp.int32, (HALF, HALF), 1)
    return cols > rows


def scores_of(block, bias):
    query, grad, key, value = block
    scores = dot(query, key, 1, 1)
    if bias is not None:
        scores = jnp.concatenate([scores[:, :WIN] + bias, scores[:, WIN:]], axis=1)
    return scores, dot(grad, value, 1, 1)


def runs_of(array):
    return [
        [array[h * HALF : (h + 1) * HALF, (h + i) * HALF : (h + i + 1) * HALF] for i in range(3)] for h in range(2)
    ]


def whole_of(runs):
    zero = jnp.zeros((HALF, HALF), BF16)
    top, bottom = [[bf(part) for part in run] for run in runs]
    return jnp.concatenate(
        [jnp.concatenate(top + [zero], axis=1), jnp.concatenate([zero] + bottom, axis=1)], axis=0
    )


def probs_of(scores, upper):
    probs = []
    for first, middle, last in runs_of(scores[0]):
        run = [jnp.where(upper, first, NEG), middle, jnp.where(upper, NEG, last)]
        top = jnp.max(jnp.maximum(jnp.maximum(run[0], run[1]), run[2]), axis=1, keepdims=True)
        shift = top * (SCALE * LOG2E)
        e = [jnp.exp2(part * (SCALE * LOG2E) - shift) for part in run]
        inv = 1.0 / jnp.sum(e[0] + e[1] + e[2], axis=1, keepdims=True)
        probs.append([part * inv for part in e])
    return probs, whole_of(probs)


def delta_of(block, weights):
    grad, value = block[1], block[3]
    attended = bf(dot(weights[1], value, 1, 0))
    return attended, jnp.sum(grad.astype(F32) * attended.astype(F32), axis=1, keepdims=True)


def score_grads(scores, weights, delta):
    halves = (delta[:HALF], delta[HALF:])
    return whole_of(
        [
            [p * (d - half) for p, d in zip(probs, prob_grads)]
            for probs, prob_grads, half in zip(weights[0], runs_of(scores[1]), halves)
        ]
    )


def turned_specs(width, count):
    def pick(half, other):
        return pl.BlockSpec((width // 4, count), lambda j, c: (2 * half + (1 - c[0] if other else c[0]), 0))

    return [pick(0, True), pick(1, True), pick(0, False), pick(1, False)]


def store_product(turned, right, send_refs, keep_ref, start):
    product = bf(dot(jnp.concatenate([part[...] for part in turned], axis=0), right, 1, 0))
    half = product.shape[0] // 2
    columns = pl.ds(pl.multiple_of(start, FOUR), FOUR)
    piece = half // len(send_refs)
    for i, send_ref in enumerate(send_refs):
        send_ref[:, columns] = product[i * piece : (i + 1) * piece]
    keep_ref[:, columns] = product[half:]


def lanes(width):
    return [slice(h * HD, (h + 1) * HD) for h in range(width // HD)]


def front_kernel(
    x_ref, g_ref, wq_ref, wk_ref, wv_ref, wo_ref, part_ref,
    turned_ref, xh_ref, gh_ref, q0_ref, k0_ref, v0_ref, a0_ref, kz_ref, vz_ref, att_ref, dq_ref, dk_ref, dv_ref,
    pk0_ref, pv0_ref, pkz_ref, pvz_ref, q_ref, k_ref, v_ref, a_ref,
):
    turned_ref[...] = part_ref[...].T

    @pl.when(pl.program_id(0) == 0)
    def _():
        xh_ref[...] = x_ref[:WIN, :]
        gh_ref[...] = g_ref[:WIN, :]

    upper = upper_triangle()
    count = x_ref.shape[0]
    blocks = count // WIN
    span = [slice(b * WIN, (b + 1) * WIN) for b in range(blocks)]
    q_ref[...] = bf(dot(x_ref[...], wq_ref[...], 1, 0))
    k_ref[...] = bf(dot(x_ref[...], wk_ref[...], 1, 0))
    v_ref[...] = bf(dot(x_ref[...], wv_ref[...], 1, 0))
    a_ref[...] = bf(dot(g_ref[...], wo_ref[...], 1, 1))
    q0_ref[...] = q_ref[:WIN, :]
    k0_ref[...] = k_ref[:WIN, :]
    v0_ref[...] = v_ref[:WIN, :]
    a0_ref[...] = a_ref[:WIN, :]
    kz_ref[...] = k_ref[count - WIN :, :]
    vz_ref[...] = v_ref[count - WIN :, :]
    window = [slice((b - 1) * WIN, (b + 1) * WIN) for b in range(blocks)]
    entries = [(c, b) for c in lanes(PAIR) for b in range(1, blocks)]
    block = [
        tuple(
            ref[rows, c]
            for ref, rows in ((q_ref, span[b]), (a_ref, span[b]), (k_ref, window[b]), (v_ref, window[b]))
        )
        for c, b in entries
    ]
    scores = [scores_of(entry, None) for entry in block]
    weights = [probs_of(entry, upper) for entry in scores]
    deltas = []
    for i, (c, b) in enumerate(entries):
        attended, delta = delta_of(block[i], weights[i])
        att_ref[span[b - 1], c] = attended
        deltas.append(delta)
    sgrads = [score_grads(*entry) for entry in zip(scores, weights, deltas)]
    for i, (c, b) in enumerate(entries):
        query, grad, key, _ = block[i]
        dq_ref[span[b - 1], c] = bf(dot(sgrads[i], key, 1, 0) * SCALE)
        dk = dot(sgrads[i], query, 0, 0)
        dv = dot(weights[i][1], grad, 0, 0)
        dk_l = dk[:WIN]
        dv_l = dv[:WIN]
        if b == 1:
            pk0_ref[:, c] = dk_l
            pv0_ref[:, c] = dv_l
        else:
            dk_ref[span[b - 2], c] = bf((dk_open + dk_l) * SCALE)
            dv_ref[span[b - 2], c] = bf(dv_open + dv_l)
        dk_open = dk[WIN:]
        dv_open = dv[WIN:]
        if b == blocks - 1:
            pkz_ref[:, c] = dk_open
            pvz_ref[:, c] = dv_open


def front(tokens, out_grad, w_query, w_key, w_value, w_output):
    count, width = tokens.shape
    whole = pl.BlockSpec((count, width), lambda j: (0, 0))
    column = pl.BlockSpec((width, PAIR), lambda j: (0, j))
    row = pl.BlockSpec((PAIR, width), lambda j: (j, 0))

    def out(rows):
        return pl.BlockSpec((rows, PAIR), lambda j: (0, j))

    def like(rows, dtype=BF16):
        return jax.ShapeDtypeStruct((rows, width), dtype)

    head = pl.BlockSpec((WIN, width), lambda j: (0, 0))
    rim, late, mid = WIN, count - WIN, count - 2 * WIN
    heights = [rim] * 6 + [late, late, mid, mid]
    return pl.pallas_call(
        front_kernel,
        grid=(width // PAIR,),
        in_specs=[whole, whole, column, column, column, row, out(count)],
        out_specs=[row, head, head] + [out(h) for h in heights] + [out(rim)] * 4,
        out_shape=[like(width), like(rim), like(rim)] + [like(h) for h in heights] + [like(rim, F32)] * 4,
        scratch_shapes=[pltpu.VMEM((count, PAIR), BF16)] * 4,
        compiler_params=pltpu.CompilerParams(vmem_limit_bytes=VMEM),
        cost_estimate=SMALL,
        name="front",
    )(tokens, out_grad, w_query, w_key, w_value, w_output, tokens)


def first_kernel(
    core_ref, bias_ref, q_ref, k_ref, v_ref, a_ref, pk_ref, pv_ref, att_in, dq_in, xl_ref, wk_ref, wv_ref,
    x0, x1, x2, x3, g_hbm, dq_ref, dk_ref, dv_ref, send_ref, keep_ref, att_ref, g_ref, g_sem,
):
    step = pl.program_id(0)
    fetch = pltpu.make_async_copy(g_hbm, g_ref, g_sem)

    @pl.when(step == 0)
    def _():
        fetch.start()

    upper = upper_triangle()
    keys_l = bf(dot(xl_ref[...], wk_ref[...], 1, 0))
    values_l = bf(dot(xl_ref[...], wv_ref[...], 1, 0))
    keys = jnp.concatenate([keys_l, k_ref[...]], axis=0)
    values = jnp.concatenate([values_l, v_ref[...]], axis=0)
    block = [(q_ref[:, c], a_ref[:, c], keys[:, c], values[:, c]) for c in lanes(FOUR)]
    scores = [scores_of(entry, bias_ref[0]) for entry in block]
    weights = [probs_of(entry, upper) for entry in scores]
    deltas = []
    for i, c in enumerate(lanes(FOUR)):
        attended, delta = delta_of(block[i], weights[i])
        att_ref[:WIN, c] = attended
        deltas.append(delta)
    att_ref[WIN:, :] = att_in[...]
    dq_ref[WIN:, :] = dq_in[...]
    for i, c in enumerate(lanes(FOUR)):
        query, grad, key, _ = block[i]
        ds = score_grads(scores[i], weights[i], deltas[i])
        dq_ref[:WIN, c] = bf(dot(ds, key, 1, 0) * SCALE)
        dk_ref[:, c] = bf((pk_ref[:, c] + dot(ds[:, WIN:], query, 0, 0)) * SCALE)
        dv_ref[:, c] = bf(pv_ref[:, c] + dot(weights[i][1][:, WIN:], grad, 0, 0))
    store_product((x0, x1, x2, x3), dq_ref[...], (send_ref,), keep_ref, step * FOUR)

    @pl.when(step == 0)
    def _():
        fetch.wait()

    product = bf(dot(att_ref[...], g_ref[...], 0, 0))
    rows = pl.ds(pl.multiple_of(step * PAIR, PAIR), PAIR)
    width = g_ref.shape[1]
    mine = core_ref[0] == 0
    keep_ref[rows, width:] = jnp.where(mine, product[:PAIR], product[PAIR:])
    send_ref[rows, width:] = jnp.where(mine, product[PAIR:], product[:PAIR])


def first_block(core, bias, own, partial, late, out_grad, tokens_l, w_key, w_value, turned):
    width, count = turned.shape
    rim = pl.BlockSpec((WIN, FOUR), lambda j, c: (0, j))
    rest = pl.BlockSpec((count - WIN, FOUR), lambda j, c: (0, j))
    full = pl.BlockSpec((count, FOUR), lambda j, c: (0, j))
    left = pl.BlockSpec((WIN, width), lambda j, c: (0, 0))
    column = pl.BlockSpec((width, FOUR), lambda j, c: (0, j))
    sums = pl.BlockSpec((width // 2, 2 * width), lambda j, c: (0, 0))
    both = jax.ShapeDtypeStruct((width // 2, 2 * width), BF16)
    part = jax.ShapeDtypeStruct((WIN, width), BF16)
    return pl.pallas_call(
        first_kernel,
        grid_spec=pltpu.PrefetchScalarGridSpec(
            num_scalar_prefetch=1,
            grid=(width // FOUR,),
            in_specs=[pl.BlockSpec(memory_space=pltpu.SMEM)]
            + [rim] * 6
            + [rest, rest, left, column, column]
            + turned_specs(width, count)
            + [pl.BlockSpec(memory_space=pl.ANY)],
            out_specs=[full, rim, rim, sums, sums],
            scratch_shapes=[
                pltpu.VMEM((count, FOUR), BF16),
                pltpu.VMEM((count, width), BF16),
                pltpu.SemaphoreType.DMA,
            ],
        ),
        out_shape=[jax.ShapeDtypeStruct((count, width), BF16), part, part, both, both],
        compiler_params=pltpu.CompilerParams(vmem_limit_bytes=VMEM),
        cost_estimate=SMALL,
        name="first_block",
    )(core, bias, *own, *partial, *late, tokens_l, w_key, w_value, *[turned] * 4, out_grad)


def last_kernel(
    core_ref, xn_ref, gn_ref, wq_ref, wk_ref, wv_ref, wo_ref, k_ref, v_ref, pk_ref, pv_ref, dk0_ref, dv0_ref,
    dkm_ref, dvm_ref, x0, x1, x2, x3, dk_ref, dv_ref, sa_ref, sb_ref, keep_ref,
):
    upper = upper_triangle()
    tokens = xn_ref[...]
    queries = bf(dot(tokens, wq_ref[...], 1, 0))
    keys = jnp.concatenate([k_ref[...], bf(dot(tokens, wk_ref[...], 1, 0))], axis=0)
    values = jnp.concatenate([v_ref[...], bf(dot(tokens, wv_ref[...], 1, 0))], axis=0)
    grads = bf(dot(gn_ref[...], wo_ref[...], 1, 1))
    block = [(queries[:, c], grads[:, c], keys[:, c], values[:, c]) for c in lanes(FOUR)]
    scores = [scores_of(entry, None) for entry in block]
    weights = [probs_of(entry, upper) for entry in scores]
    deltas = [delta_of(*entry)[1] for entry in zip(block, weights)]
    end = dk_ref.shape[0] - WIN
    dk_ref[:WIN, :] = dk0_ref[...]
    dv_ref[:WIN, :] = dv0_ref[...]
    dk_ref[WIN:end, :] = dkm_ref[...]
    dv_ref[WIN:end, :] = dvm_ref[...]
    for i, c in enumerate(lanes(FOUR)):
        ds = score_grads(scores[i], weights[i], deltas[i])
        dk_ref[end:, c] = bf((pk_ref[:, c] + dot(ds[:, :WIN], block[i][0], 0, 0)) * SCALE)
        dv_ref[end:, c] = bf(pv_ref[:, c] + dot(weights[i][1][:, :WIN], block[i][1], 0, 0))
    start = pl.program_id(0) * FOUR
    store_product((x0, x1, x2, x3), dk_ref[...], (sa_ref, sb_ref), keep_ref, start)
    store_product((x0, x1, x2, x3), dv_ref[...], (sa_ref, sb_ref), keep_ref, start + keep_ref.shape[1] // 2)


def last_block(core, tokens_n, grads_n, weights, last, partial, first, middle, turned):
    width, count = turned.shape
    column = pl.BlockSpec((width, FOUR), lambda j, c: (0, j))
    row = pl.BlockSpec((FOUR, width), lambda j, c: (j, 0))
    rim = pl.BlockSpec((WIN, FOUR), lambda j, c: (0, j))
    near = pl.BlockSpec((WIN, width), lambda j, c: (0, 0))
    mid = pl.BlockSpec((count - 2 * WIN, FOUR), lambda j, c: (0, j))
    full = pl.BlockSpec((count, FOUR), lambda j, c: (0, j))
    sums = pl.BlockSpec((width // 2, 2 * width), lambda j, c: (0, 0))
    grad = jax.ShapeDtypeStruct((count, width), BF16)
    both = jax.ShapeDtypeStruct((width // 2, 2 * width), BF16)
    half = pl.BlockSpec((width // 4, 2 * width), lambda j, c: (0, 0))
    part_sum = jax.ShapeDtypeStruct((width // 4, 2 * width), BF16)
    return pl.pallas_call(
        last_kernel,
        grid_spec=pltpu.PrefetchScalarGridSpec(
            num_scalar_prefetch=1,
            grid=(width // FOUR,),
            in_specs=[near, near, column, column, column, row] + [rim] * 6 + [mid, mid] + turned_specs(width, count),
            out_specs=[full, full, half, half, sums],
        ),
        out_shape=[grad, grad, part_sum, part_sum, both],
        compiler_params=pltpu.CompilerParams(vmem_limit_bytes=VMEM),
        cost_estimate=SMALL,
        name="last_block",
    )(core, tokens_n, grads_n, *weights, *last, *partial, *first, *middle, *[turned] * 4)


def chip_sum(sends, keep, meanwhile=None):
    got = [lax.ppermute(send, "co", [(0, 1), (1, 0)]) for send in sends]
    if meanwhile is not None:
        *got, meanwhile = lax.optimization_barrier((*got, meanwhile))
    return bf(keep.astype(F32) + jnp.concatenate(got, axis=0).astype(F32)), meanwhile


def piece_sum(pieces, width):
    return jnp.sum(pieces.reshape(-1, 8, width).astype(F32), axis=0)


def passed_along(block, distance):
    size = 1
    for axis in SEQ:
        size *= lax.axis_size(axis)
    route = [(i - distance, i) for i in range(size) if 0 <= i - distance < size]
    return lax.ppermute(block, SEQ, route)


def on_device(tokens, out_grad, w_query, w_key, w_value, w_output, grad_accum):
    tokens = tokens[0]
    out_grad = out_grad[0]
    count, width = tokens.shape
    core = lax.axis_index("co")
    which = core.reshape(1)
    first = (lax.axis_index("y") + lax.axis_index("z") + lax.axis_index("xl")) == 0
    bias = jnp.where(first, NEG, 0.0).astype(F32).reshape(1)
    tokens_l = passed_along(tokens[count - WIN :], 1)
    weights = (w_query, w_key, w_value, w_output)
    turned, head_x, head_g, *rest = front(tokens, out_grad, *weights)
    tokens_n = passed_along(head_x, -1)
    grads_n = passed_along(head_g, -1)
    own, last, late, middle, partial_0, partial_z = rest[:4], rest[4:6], rest[6:8], rest[8:10], rest[10:12], rest[12:]
    query_grad, key_0, value_0, send, keep = first_block(
        which, bias, own, partial_0, late, out_grad, tokens_l, w_key, w_value, turned
    )
    send, tokens_n = lax.optimization_barrier((send, tokens_n))
    both, _ = chip_sum((send,), keep)
    pieces_qo = lax.all_to_all(both, CHIPS, 0, 0, tiled=True)
    tokens_n, _ = lax.optimization_barrier((tokens_n, both))
    key_grad, value_grad, send_a, send_b, keep = last_block(
        which, tokens_n, grads_n, weights, last, partial_z, (key_0, value_0), middle, turned
    )
    in_grad = bf(
        dot(query_grad, w_query, 1, 1) + dot(key_grad, w_key, 1, 1) + dot(value_grad, w_value, 1, 1)
    )
    both, in_grad = chip_sum((send_a, send_b), keep, in_grad)
    total = count
    for axis in AXES:
        total *= lax.axis_size(axis)
    factor = 1.0 / total**0.5
    sum_qo = piece_sum(pieces_qo, 2 * width) * factor
    new_q = grad_accum[:, :width] + sum_qo[:, :width]
    new_o = grad_accum[:, 3 * width :] + sum_qo[:, width:]
    rest = grad_accum[:, width : 3 * width]
    both, new_q, new_o, rest = lax.optimization_barrier((both, new_q, new_o, rest))
    sum_kv = piece_sum(lax.all_to_all(both, CHIPS, 0, 0, tiled=True), 2 * width) * factor
    return in_grad[None], jnp.concatenate([new_q, rest + sum_kv, new_o], axis=1)


def solution(mesh):
    fine = Mesh(mesh.devices.reshape(2, 2, 4, 4, 2), AXES)
    rows = P(("xh", "co"), SEQ, None)
    accum = P(AXES, None)
    return jax.shard_map(
        on_device,
        mesh=fine,
        in_specs=(rows, rows, P(), P(), P(), P(), accum),
        out_specs=(rows, accum),
        check_vma=False,
    )
```

```python
import jax
import jax.numpy as jnp
from jax import lax
from jax.experimental import pallas as pl
from jax.experimental.pallas import tpu as pltpu
from jax.sharding import Mesh
from jax.sharding import PartitionSpec as P

HD = 128
WIN = 256
LOG2E = 1.4426950408889634
SCALE = 1.0 / HD**0.5
AXES = ("xh", "co", "y", "z", "xl")
SEQ = ("y", "z", "xl")
CHIPS = ("xh", "y", "z", "xl")
F32 = jnp.float32
BF16 = jnp.bfloat16


def dot(a, b, ca, cb):
    return lax.dot_general(a, b, (((ca,), (cb,)), ((), ())), preferred_element_type=F32)


SMALL = pl.CostEstimate(flops=10**8, bytes_accessed=10**5, transcendentals=0)
VMEM = 60 * 2**20
PAIR = 2 * HD
FOUR = 4 * HD
HALF = WIN // 2
NEG = -1e30


def bf(value):
    return value.astype(BF16)


def upper_triangle():
    rows = lax.broadcasted_iota(jnp.int32, (HALF, HALF), 0)
    cols = lax.broadcasted_iota(jnp.int32, (HALF, HALF), 1)
    return cols > rows


def scores_of(block, bias):
    query, grad, key, value = block
    scores = dot(query, key, 1, 1)
    if bias is not None:
        scores = jnp.concatenate([scores[:, :WIN] + bias, scores[:, WIN:]], axis=1)
    return scores, dot(grad, value, 1, 1)


def runs_of(array):
    return [
        [array[h * HALF : (h + 1) * HALF, (h + i) * HALF : (h + i + 1) * HALF] for i in range(3)] for h in range(2)
    ]


def whole_of(runs):
    zero = jnp.zeros((HALF, HALF), BF16)
    top, bottom = [[bf(part) for part in run] for run in runs]
    return jnp.concatenate(
        [jnp.concatenate(top + [zero], axis=1), jnp.concatenate([zero] + bottom, axis=1)], axis=0
    )


def probs_of(scores, upper):
    probs = []
    for first, middle, last in runs_of(scores[0]):
        run = [jnp.where(upper, first, NEG), middle, jnp.where(upper, NEG, last)]
        top = jnp.max(jnp.maximum(jnp.maximum(run[0], run[1]), run[2]), axis=1, keepdims=True)
        shift = top * (SCALE * LOG2E)
        e = [jnp.exp2(part * (SCALE * LOG2E) - shift) for part in run]
        inv = 1.0 / jnp.sum(e[0] + e[1] + e[2], axis=1, keepdims=True)
        probs.append([part * inv for part in e])
    return probs, whole_of(probs)


def delta_of(block, weights):
    grad, value = block[1], block[3]
    attended = bf(dot(weights[1], value, 1, 0))
    return attended, jnp.sum(grad.astype(F32) * attended.astype(F32), axis=1, keepdims=True)


def score_grads(scores, weights, delta):
    halves = (delta[:HALF], delta[HALF:])
    return whole_of(
        [
            [p * (d - half) for p, d in zip(probs, prob_grads)]
            for probs, prob_grads, half in zip(weights[0], runs_of(scores[1]), halves)
        ]
    )


def turned_specs(width, count):
    def pick(half, other):
        return pl.BlockSpec((width // 4, count), lambda j, c: (2 * half + (1 - c[0] if other else c[0]), 0))

    return [pick(0, True), pick(1, True), pick(0, False), pick(1, False)]


def store_product(turned, right, send_refs, keep_ref, start):
    product = bf(dot(jnp.concatenate([part[...] for part in turned], axis=0), right, 1, 0))
    half = product.shape[0] // 2
    columns = pl.ds(pl.multiple_of(start, FOUR), FOUR)
    piece = half // len(send_refs)
    for i, send_ref in enumerate(send_refs):
        send_ref[:, columns] = product[i * piece : (i + 1) * piece]
    keep_ref[:, columns] = product[half:]


def lanes(width):
    return [slice(h * HD, (h + 1) * HD) for h in range(width // HD)]


def front_kernel(
    x_ref, g_ref, wq_ref, wk_ref, wv_ref, wo_ref, part_ref,
    turned_ref, xh_ref, gh_ref, q0_ref, k0_ref, v0_ref, a0_ref, kz_ref, vz_ref, att_ref, dq_ref, dk_ref, dv_ref,
    pk0_ref, pv0_ref, pkz_ref, pvz_ref, q_ref, k_ref, v_ref, a_ref,
):
    turned_ref[...] = part_ref[...].T

    @pl.when(pl.program_id(0) == 0)
    def _():
        xh_ref[...] = x_ref[:WIN, :]
        gh_ref[...] = g_ref[:WIN, :]

    upper = upper_triangle()
    count = x_ref.shape[0]
    blocks = count // WIN
    span = [slice(b * WIN, (b + 1) * WIN) for b in range(blocks)]
    q_ref[...] = bf(dot(x_ref[...], wq_ref[...], 1, 0))
    k_ref[...] = bf(dot(x_ref[...], wk_ref[...], 1, 0))
    v_ref[...] = bf(dot(x_ref[...], wv_ref[...], 1, 0))
    a_ref[...] = bf(dot(g_ref[...], wo_ref[...], 1, 1))
    q0_ref[...] = q_ref[:WIN, :]
    k0_ref[...] = k_ref[:WIN, :]
    v0_ref[...] = v_ref[:WIN, :]
    a0_ref[...] = a_ref[:WIN, :]
    kz_ref[...] = k_ref[count - WIN :, :]
    vz_ref[...] = v_ref[count - WIN :, :]
    window = [slice((b - 1) * WIN, (b + 1) * WIN) for b in range(blocks)]
    entries = [(c, b) for c in lanes(PAIR) for b in range(1, blocks)]
    block = [
        tuple(
            ref[rows, c]
            for ref, rows in ((q_ref, span[b]), (a_ref, span[b]), (k_ref, window[b]), (v_ref, window[b]))
        )
        for c, b in entries
    ]
    scores = [scores_of(entry, None) for entry in block]
    weights = [probs_of(entry, upper) for entry in scores]
    deltas = []
    for i, (c, b) in enumerate(entries):
        attended, delta = delta_of(block[i], weights[i])
        att_ref[span[b - 1], c] = attended
        deltas.append(delta)
    sgrads = [score_grads(*entry) for entry in zip(scores, weights, deltas)]
    for i, (c, b) in enumerate(entries):
        query, grad, key, _ = block[i]
        dq_ref[span[b - 1], c] = bf(dot(sgrads[i], key, 1, 0) * SCALE)
        dk = dot(sgrads[i], query, 0, 0)
        dv = dot(weights[i][1], grad, 0, 0)
        dk_l = dk[:WIN]
        dv_l = dv[:WIN]
        if b == 1:
            pk0_ref[:, c] = dk_l
            pv0_ref[:, c] = dv_l
        else:
            dk_ref[span[b - 2], c] = bf((dk_open + dk_l) * SCALE)
            dv_ref[span[b - 2], c] = bf(dv_open + dv_l)
        dk_open = dk[WIN:]
        dv_open = dv[WIN:]
        if b == blocks - 1:
            pkz_ref[:, c] = dk_open
            pvz_ref[:, c] = dv_open


def front(tokens, out_grad, w_query, w_key, w_value, w_output):
    count, width = tokens.shape
    whole = pl.BlockSpec((count, width), lambda j: (0, 0))
    column = pl.BlockSpec((width, PAIR), lambda j: (0, j))
    row = pl.BlockSpec((PAIR, width), lambda j: (j, 0))

    def out(rows):
        return pl.BlockSpec((rows, PAIR), lambda j: (0, j))

    def like(rows, dtype=BF16):
        return jax.ShapeDtypeStruct((rows, width), dtype)

    head = pl.BlockSpec((WIN, width), lambda j: (0, 0))
    rim, late, mid = WIN, count - WIN, count - 2 * WIN
    heights = [rim] * 6 + [late, late, mid, mid]
    return pl.pallas_call(
        front_kernel,
        grid=(width // PAIR,),
        in_specs=[whole, whole, column, column, column, row, out(count)],
        out_specs=[row, head, head] + [out(h) for h in heights] + [out(rim)] * 4,
        out_shape=[like(width), like(rim), like(rim)] + [like(h) for h in heights] + [like(rim, F32)] * 4,
        scratch_shapes=[pltpu.VMEM((count, PAIR), BF16)] * 4,
        compiler_params=pltpu.CompilerParams(vmem_limit_bytes=VMEM),
        cost_estimate=SMALL,
        name="front",
    )(tokens, out_grad, w_query, w_key, w_value, w_output, tokens)


def first_kernel(
    core_ref, bias_ref, q_ref, k_ref, v_ref, a_ref, pk_ref, pv_ref, att_in, dq_in, xl_ref, wk_ref, wv_ref,
    x0, x1, x2, x3, g_hbm, dq_ref, dk_ref, dv_ref, send_ref, keep_ref, att_ref, g_ref, g_sem,
):
    step = pl.program_id(0)
    fetch = pltpu.make_async_copy(g_hbm, g_ref, g_sem)

    @pl.when(step == 0)
    def _():
        fetch.start()

    upper = upper_triangle()
    keys_l = bf(dot(xl_ref[...], wk_ref[...], 1, 0))
    values_l = bf(dot(xl_ref[...], wv_ref[...], 1, 0))
    keys = jnp.concatenate([keys_l, k_ref[...]], axis=0)
    values = jnp.concatenate([values_l, v_ref[...]], axis=0)
    block = [(q_ref[:, c], a_ref[:, c], keys[:, c], values[:, c]) for c in lanes(FOUR)]
    scores = [scores_of(entry, bias_ref[0]) for entry in block]
    weights = [probs_of(entry, upper) for entry in scores]
    deltas = []
    for i, c in enumerate(lanes(FOUR)):
        attended, delta = delta_of(block[i], weights[i])
        att_ref[:WIN, c] = attended
        deltas.append(delta)
    att_ref[WIN:, :] = att_in[...]
    dq_ref[WIN:, :] = dq_in[...]
    for i, c in enumerate(lanes(FOUR)):
        query, grad, key, _ = block[i]
        ds = score_grads(scores[i], weights[i], deltas[i])
        dq_ref[:WIN, c] = bf(dot(ds, key, 1, 0) * SCALE)
        dk_ref[:, c] = bf((pk_ref[:, c] + dot(ds[:, WIN:], query, 0, 0)) * SCALE)
        dv_ref[:, c] = bf(pv_ref[:, c] + dot(weights[i][1][:, WIN:], grad, 0, 0))
    store_product((x0, x1, x2, x3), dq_ref[...], (send_ref,), keep_ref, step * FOUR)

    @pl.when(step == 0)
    def _():
        fetch.wait()

    product = bf(dot(att_ref[...], g_ref[...], 0, 0))
    rows = pl.ds(pl.multiple_of(step * PAIR, PAIR), PAIR)
    width = g_ref.shape[1]
    mine = core_ref[0] == 0
    keep_ref[rows, width:] = jnp.where(mine, product[:PAIR], product[PAIR:])
    send_ref[rows, width:] = jnp.where(mine, product[PAIR:], product[:PAIR])


def first_block(core, bias, own, partial, late, out_grad, tokens_l, w_key, w_value, turned):
    width, count = turned.shape
    rim = pl.BlockSpec((WIN, FOUR), lambda j, c: (0, j))
    rest = pl.BlockSpec((count - WIN, FOUR), lambda j, c: (0, j))
    full = pl.BlockSpec((count, FOUR), lambda j, c: (0, j))
    left = pl.BlockSpec((WIN, width), lambda j, c: (0, 0))
    column = pl.BlockSpec((width, FOUR), lambda j, c: (0, j))
    sums = pl.BlockSpec((width // 2, 2 * width), lambda j, c: (0, 0))
    both = jax.ShapeDtypeStruct((width // 2, 2 * width), BF16)
    part = jax.ShapeDtypeStruct((WIN, width), BF16)
    return pl.pallas_call(
        first_kernel,
        grid_spec=pltpu.PrefetchScalarGridSpec(
            num_scalar_prefetch=1,
            grid=(width // FOUR,),
            in_specs=[pl.BlockSpec(memory_space=pltpu.SMEM)]
            + [rim] * 6
            + [rest, rest, left, column, column]
            + turned_specs(width, count)
            + [pl.BlockSpec(memory_space=pl.ANY)],
            out_specs=[full, rim, rim, sums, sums],
            scratch_shapes=[
                pltpu.VMEM((count, FOUR), BF16),
                pltpu.VMEM((count, width), BF16),
                pltpu.SemaphoreType.DMA,
            ],
        ),
        out_shape=[jax.ShapeDtypeStruct((count, width), BF16), part, part, both, both],
        compiler_params=pltpu.CompilerParams(vmem_limit_bytes=VMEM),
        cost_estimate=SMALL,
        name="first_block",
    )(core, bias, *own, *partial, *late, tokens_l, w_key, w_value, *[turned] * 4, out_grad)


def last_kernel(
    core_ref, xn_ref, gn_ref, wq_ref, wk_ref, wv_ref, wo_ref, k_ref, v_ref, pk_ref, pv_ref, dk0_ref, dv0_ref,
    dkm_ref, dvm_ref, x0, x1, x2, x3, dk_ref, dv_ref, sa_ref, sb_ref, keep_ref,
):
    upper = upper_triangle()
    tokens = xn_ref[...]
    queries = bf(dot(tokens, wq_ref[...], 1, 0))
    keys = jnp.concatenate([k_ref[...], bf(dot(tokens, wk_ref[...], 1, 0))], axis=0)
    values = jnp.concatenate([v_ref[...], bf(dot(tokens, wv_ref[...], 1, 0))], axis=0)
    grads = bf(dot(gn_ref[...], wo_ref[...], 1, 1))
    block = [(queries[:, c], grads[:, c], keys[:, c], values[:, c]) for c in lanes(FOUR)]
    scores = [scores_of(entry, None) for entry in block]
    weights = [probs_of(entry, upper) for entry in scores]
    deltas = [delta_of(*entry)[1] for entry in zip(block, weights)]
    end = dk_ref.shape[0] - WIN
    dk_ref[:WIN, :] = dk0_ref[...]
    dv_ref[:WIN, :] = dv0_ref[...]
    dk_ref[WIN:end, :] = dkm_ref[...]
    dv_ref[WIN:end, :] = dvm_ref[...]
    for i, c in enumerate(lanes(FOUR)):
        ds = score_grads(scores[i], weights[i], deltas[i])
        dk_ref[end:, c] = bf((pk_ref[:, c] + dot(ds[:, :WIN], block[i][0], 0, 0)) * SCALE)
        dv_ref[end:, c] = bf(pv_ref[:, c] + dot(weights[i][1][:, :WIN], block[i][1], 0, 0))
    start = pl.program_id(0) * FOUR
    store_product((x0, x1, x2, x3), dk_ref[...], (sa_ref, sb_ref), keep_ref, start)
    store_product((x0, x1, x2, x3), dv_ref[...], (sa_ref, sb_ref), keep_ref, start + keep_ref.shape[1] // 2)


def last_block(core, tokens_n, grads_n, weights, last, partial, first, middle, turned):
    width, count = turned.shape
    column = pl.BlockSpec((width, FOUR), lambda j, c: (0, j))
    row = pl.BlockSpec((FOUR, width), lambda j, c: (j, 0))
    rim = pl.BlockSpec((WIN, FOUR), lambda j, c: (0, j))
    near = pl.BlockSpec((WIN, width), lambda j, c: (0, 0))
    mid = pl.BlockSpec((count - 2 * WIN, FOUR), lambda j, c: (0, j))
    full = pl.BlockSpec((count, FOUR), lambda j, c: (0, j))
    sums = pl.BlockSpec((width // 2, 2 * width), lambda j, c: (0, 0))
    grad = jax.ShapeDtypeStruct((count, width), BF16)
    both = jax.ShapeDtypeStruct((width // 2, 2 * width), BF16)
    half = pl.BlockSpec((width // 4, 2 * width), lambda j, c: (0, 0))
    part_sum = jax.ShapeDtypeStruct((width // 4, 2 * width), BF16)
    return pl.pallas_call(
        last_kernel,
        grid_spec=pltpu.PrefetchScalarGridSpec(
            num_scalar_prefetch=1,
            grid=(width // FOUR,),
            in_specs=[near, near, column, column, column, row] + [rim] * 6 + [mid, mid] + turned_specs(width, count),
            out_specs=[full, full, half, half, sums],
        ),
        out_shape=[grad, grad, part_sum, part_sum, both],
        compiler_params=pltpu.CompilerParams(vmem_limit_bytes=VMEM),
        cost_estimate=SMALL,
        name="last_block",
    )(core, tokens_n, grads_n, *weights, *last, *partial, *first, *middle, *[turned] * 4)


def chip_sum(sends, keep, meanwhile=None):
    got = [lax.ppermute(send, "co", [(0, 1), (1, 0)]) for send in sends]
    if meanwhile is not None:
        *got, meanwhile = lax.optimization_barrier((*got, meanwhile))
    return bf(keep.astype(F32) + jnp.concatenate(got, axis=0).astype(F32)), meanwhile


def piece_sum(pieces, width):
    return jnp.sum(pieces.reshape(-1, 8, width).astype(F32), axis=0)


def passed_along(block, distance):
    size = 1
    for axis in SEQ:
        size *= lax.axis_size(axis)
    route = [(i - distance, i) for i in range(size) if 0 <= i - distance < size]
    return lax.ppermute(block, SEQ, route)


def on_device(tokens, out_grad, w_query, w_key, w_value, w_output, grad_accum):
    tokens = tokens[0]
    out_grad = out_grad[0]
    count, width = tokens.shape
    core = lax.axis_index("co")
    which = core.reshape(1)
    first = (lax.axis_index("y") + lax.axis_index("z") + lax.axis_index("xl")) == 0
    bias = jnp.where(first, NEG, 0.0).astype(F32).reshape(1)
    tokens_l = passed_along(tokens[count - WIN :], 1)
    weights = (w_query, w_key, w_value, w_output)
    turned, head_x, head_g, *rest = front(tokens, out_grad, *weights)
    tokens_n = passed_along(head_x, -1)
    grads_n = passed_along(head_g, -1)
    own, last, late, middle, partial_0, partial_z = rest[:4], rest[4:6], rest[6:8], rest[8:10], rest[10:12], rest[12:]
    query_grad, key_0, value_0, send, keep = first_block(
        which, bias, own, partial_0, late, out_grad, tokens_l, w_key, w_value, turned
    )
    send, tokens_n = lax.optimization_barrier((send, tokens_n))
    both, _ = chip_sum((send,), keep)
    pieces_qo = lax.all_to_all(both, CHIPS, 0, 0, tiled=True)
    tokens_n, _ = lax.optimization_barrier((tokens_n, both))
    key_grad, value_grad, send_a, send_b, keep = last_block(
        which, tokens_n, grads_n, weights, last, partial_z, (key_0, value_0), middle, turned
    )
    send_a, send_b, query_grad = lax.optimization_barrier((send_a, send_b, query_grad))
    both, in_query = chip_sum((send_a, send_b), keep, dot(query_grad, w_query, 1, 1))
    pieces_kv = lax.all_to_all(both, CHIPS, 0, 0, tiled=True)
    in_grad = bf(in_query + dot(key_grad, w_key, 1, 1) + dot(value_grad, w_value, 1, 1))
    total = count
    for axis in AXES:
        total *= lax.axis_size(axis)
    factor = 1.0 / total**0.5
    sum_qo = piece_sum(pieces_qo, 2 * width)
    sum_kv = piece_sum(pieces_kv, 2 * width)
    summed = jnp.concatenate([sum_qo[:, :width], sum_kv, sum_qo[:, width:]], axis=1)
    return in_grad[None], grad_accum + summed * factor


def solution(mesh):
    fine = Mesh(mesh.devices.reshape(2, 2, 4, 4, 2), AXES)
    rows = P(("xh", "co"), SEQ, None)
    accum = P(AXES, None)
    return jax.shard_map(
        on_device,
        mesh=fine,
        in_specs=(rows, rows, P(), P(), P(), P(), accum),
        out_specs=(rows, accum),
        check_vma=False,
    )
```

```python
import jax
import jax.numpy as jnp
from jax import lax
from jax.experimental import pallas as pl
from jax.experimental.pallas import tpu as pltpu
from jax.sharding import Mesh
from jax.sharding import PartitionSpec as P

HD = 128
WIN = 256
LOG2E = 1.4426950408889634
SCALE = 1.0 / HD**0.5
AXES = ("xh", "co", "y", "z", "xl")
SEQ = ("y", "z", "xl")
CHIPS = ("xh", "y", "z", "xl")
F32 = jnp.float32
BF16 = jnp.bfloat16


def dot(a, b, ca, cb):
    return lax.dot_general(a, b, (((ca,), (cb,)), ((), ())), preferred_element_type=F32)


SMALL = pl.CostEstimate(flops=10**8, bytes_accessed=10**5, transcendentals=0)
VMEM = 60 * 2**20
ROOM = 57 * 2**20
PAIR = 2 * HD
FOUR = 4 * HD
HALF = WIN // 2
NEG = -1e30


def bf(value):
    return value.astype(BF16)


def upper_triangle():
    rows = lax.broadcasted_iota(jnp.int32, (HALF, HALF), 0)
    cols = lax.broadcasted_iota(jnp.int32, (HALF, HALF), 1)
    return cols > rows


def scores_of(block, bias):
    query, grad, key, value = block
    scores = dot(query, key, 1, 1)
    if bias is not None:
        scores = jnp.concatenate([scores[:, :WIN] + bias, scores[:, WIN:]], axis=1)
    return scores, dot(grad, value, 1, 1)


def runs_of(array):
    return [
        [array[h * HALF : (h + 1) * HALF, (h + i) * HALF : (h + i + 1) * HALF] for i in range(3)] for h in range(2)
    ]


def whole_of(runs):
    zero = jnp.zeros((HALF, HALF), BF16)
    top, bottom = [[bf(part) for part in run] for run in runs]
    return jnp.concatenate(
        [jnp.concatenate(top + [zero], axis=1), jnp.concatenate([zero] + bottom, axis=1)], axis=0
    )


def probs_of(scores, upper):
    probs = []
    for first, middle, last in runs_of(scores[0]):
        run = [jnp.where(upper, first, NEG), middle, jnp.where(upper, NEG, last)]
        top = jnp.max(jnp.maximum(jnp.maximum(run[0], run[1]), run[2]), axis=1, keepdims=True)
        shift = top * (SCALE * LOG2E)
        e = [jnp.exp2(part * (SCALE * LOG2E) - shift) for part in run]
        inv = 1.0 / jnp.sum(e[0] + e[1] + e[2], axis=1, keepdims=True)
        probs.append([part * inv for part in e])
    return probs, whole_of(probs)


def delta_of(block, weights):
    grad, value = block[1], block[3]
    attended = bf(dot(weights[1], value, 1, 0))
    return attended, jnp.sum(grad.astype(F32) * attended.astype(F32), axis=1, keepdims=True)


def score_grads(scores, weights, delta):
    halves = (delta[:HALF], delta[HALF:])
    return whole_of(
        [
            [p * (d - half) for p, d in zip(probs, prob_grads)]
            for probs, prob_grads, half in zip(weights[0], runs_of(scores[1]), halves)
        ]
    )


def turned_specs(width, count):
    def pick(half, other):
        return pl.BlockSpec((width // 4, count), lambda j, c: (2 * half + (1 - c[0] if other else c[0]), 0))

    return [pick(0, True), pick(1, True), pick(0, False), pick(1, False)]


def store_product(turned, right, send_refs, keep_ref, start):
    product = bf(dot(jnp.concatenate([part[...] for part in turned], axis=0), right, 1, 0))
    half = product.shape[0] // 2
    columns = pl.ds(pl.multiple_of(start, FOUR), FOUR)
    piece = half // len(send_refs)
    for i, send_ref in enumerate(send_refs):
        send_ref[:, columns] = product[i * piece : (i + 1) * piece]
    keep_ref[:, columns] = product[half:]


def lanes(width):
    return [slice(h * HD, (h + 1) * HD) for h in range(width // HD)]


def front_kernel(
    x_ref, g_ref, wq_ref, wk_ref, wv_ref, wo_ref, part_ref,
    turned_ref, xh_ref, gh_ref, q0_ref, k0_ref, v0_ref, a0_ref, kz_ref, vz_ref, att_ref, dq_ref, dk_ref, dv_ref,
    pk0_ref, pv0_ref, pkz_ref, pvz_ref, q_ref, k_ref, v_ref, a_ref,
):
    turned_ref[...] = part_ref[...].T

    @pl.when(pl.program_id(0) == 0)
    def _():
        xh_ref[...] = x_ref[:WIN, :]
        gh_ref[...] = g_ref[:WIN, :]

    upper = upper_triangle()
    count = x_ref.shape[0]
    blocks = count // WIN
    span = [slice(b * WIN, (b + 1) * WIN) for b in range(blocks)]
    q_ref[...] = bf(dot(x_ref[...], wq_ref[...], 1, 0))
    k_ref[...] = bf(dot(x_ref[...], wk_ref[...], 1, 0))
    v_ref[...] = bf(dot(x_ref[...], wv_ref[...], 1, 0))
    a_ref[...] = bf(dot(g_ref[...], wo_ref[...], 1, 1))
    q0_ref[...] = q_ref[:WIN, :]
    k0_ref[...] = k_ref[:WIN, :]
    v0_ref[...] = v_ref[:WIN, :]
    a0_ref[...] = a_ref[:WIN, :]
    kz_ref[...] = k_ref[count - WIN :, :]
    vz_ref[...] = v_ref[count - WIN :, :]
    window = [slice((b - 1) * WIN, (b + 1) * WIN) for b in range(blocks)]
    entries = [(c, b) for c in lanes(PAIR) for b in range(1, blocks)]
    block = [
        tuple(
            ref[rows, c]
            for ref, rows in ((q_ref, span[b]), (a_ref, span[b]), (k_ref, window[b]), (v_ref, window[b]))
        )
        for c, b in entries
    ]
    scores = [scores_of(entry, None) for entry in block]
    weights = [probs_of(entry, upper) for entry in scores]
    deltas = []
    for i, (c, b) in enumerate(entries):
        attended, delta = delta_of(block[i], weights[i])
        att_ref[span[b - 1], c] = attended
        deltas.append(delta)
    sgrads = [score_grads(*entry) for entry in zip(scores, weights, deltas)]
    for i, (c, b) in enumerate(entries):
        query, grad, key, _ = block[i]
        dq_ref[span[b - 1], c] = bf(dot(sgrads[i], key, 1, 0) * SCALE)
        dk = dot(sgrads[i], query, 0, 0)
        dv = dot(weights[i][1], grad, 0, 0)
        dk_l = dk[:WIN]
        dv_l = dv[:WIN]
        if b == 1:
            pk0_ref[:, c] = dk_l
            pv0_ref[:, c] = dv_l
        else:
            dk_ref[span[b - 2], c] = bf((dk_open + dk_l) * SCALE)
            dv_ref[span[b - 2], c] = bf(dv_open + dv_l)
        dk_open = dk[WIN:]
        dv_open = dv[WIN:]
        if b == blocks - 1:
            pkz_ref[:, c] = dk_open
            pvz_ref[:, c] = dv_open


def front(tokens, out_grad, w_query, w_key, w_value, w_output):
    count, width = tokens.shape
    whole = pl.BlockSpec((count, width), lambda j: (0, 0))
    column = pl.BlockSpec((width, PAIR), lambda j: (0, j))
    row = pl.BlockSpec((PAIR, width), lambda j: (j, 0))

    def out(rows):
        return pl.BlockSpec((rows, PAIR), lambda j: (0, j))

    def like(rows, dtype=BF16):
        return jax.ShapeDtypeStruct((rows, width), dtype)

    head = pl.BlockSpec((WIN, width), lambda j: (0, 0))
    rim, late, mid = WIN, count - WIN, count - 2 * WIN
    heights = [rim] * 6 + [late, late, mid, mid]
    return pl.pallas_call(
        front_kernel,
        grid=(width // PAIR,),
        in_specs=[whole, whole, column, column, column, row, out(count)],
        out_specs=[row, head, head] + [out(h) for h in heights] + [out(rim)] * 4,
        out_shape=[like(width), like(rim), like(rim)] + [like(h) for h in heights] + [like(rim, F32)] * 4,
        scratch_shapes=[pltpu.VMEM((count, PAIR), BF16)] * 4,
        compiler_params=pltpu.CompilerParams(vmem_limit_bytes=VMEM),
        cost_estimate=SMALL,
        name="front",
    )(tokens, out_grad, w_query, w_key, w_value, w_output, tokens)


def first_kernel(
    core_ref, bias_ref, q_ref, k_ref, v_ref, a_ref, pk_ref, pv_ref, att_in, dq_in, xl_ref, wk_ref, wv_ref,
    x0, x1, x2, x3, g_hbm, dq_ref, dk_ref, dv_ref, send_ref, keep_ref, att_ref, g_ref, g_sem,
):
    step = pl.program_id(0)
    fetch = pltpu.make_async_copy(g_hbm, g_ref, g_sem)

    @pl.when(step == 0)
    def _():
        fetch.start()

    upper = upper_triangle()
    keys_l = bf(dot(xl_ref[...], wk_ref[...], 1, 0))
    values_l = bf(dot(xl_ref[...], wv_ref[...], 1, 0))
    keys = jnp.concatenate([keys_l, k_ref[...]], axis=0)
    values = jnp.concatenate([values_l, v_ref[...]], axis=0)
    block = [(q_ref[:, c], a_ref[:, c], keys[:, c], values[:, c]) for c in lanes(FOUR)]
    scores = [scores_of(entry, bias_ref[0]) for entry in block]
    weights = [probs_of(entry, upper) for entry in scores]
    deltas = []
    for i, c in enumerate(lanes(FOUR)):
        attended, delta = delta_of(block[i], weights[i])
        att_ref[:WIN, c] = attended
        deltas.append(delta)
    att_ref[WIN:, :] = att_in[...]
    dq_ref[WIN:, :] = dq_in[...]
    for i, c in enumerate(lanes(FOUR)):
        query, grad, key, _ = block[i]
        ds = score_grads(scores[i], weights[i], deltas[i])
        dq_ref[:WIN, c] = bf(dot(ds, key, 1, 0) * SCALE)
        dk_ref[:, c] = bf((pk_ref[:, c] + dot(ds[:, WIN:], query, 0, 0)) * SCALE)
        dv_ref[:, c] = bf(pv_ref[:, c] + dot(weights[i][1][:, WIN:], grad, 0, 0))
    store_product((x0, x1, x2, x3), dq_ref[...], (send_ref,), keep_ref, step * FOUR)

    @pl.when(step == 0)
    def _():
        fetch.wait()

    product = bf(dot(att_ref[...], g_ref[...], 0, 0))
    rows = pl.ds(pl.multiple_of(step * PAIR, PAIR), PAIR)
    width = g_ref.shape[1]
    mine = core_ref[0] == 0
    keep_ref[rows, width:] = jnp.where(mine, product[:PAIR], product[PAIR:])
    send_ref[rows, width:] = jnp.where(mine, product[PAIR:], product[:PAIR])


def first_block(core, bias, own, partial, late, out_grad, tokens_l, w_key, w_value, turned):
    width, count = turned.shape
    rim = pl.BlockSpec((WIN, FOUR), lambda j, c: (0, j))
    rest = pl.BlockSpec((count - WIN, FOUR), lambda j, c: (0, j))
    full = pl.BlockSpec((count, FOUR), lambda j, c: (0, j))
    left = pl.BlockSpec((WIN, width), lambda j, c: (0, 0))
    column = pl.BlockSpec((width, FOUR), lambda j, c: (0, j))
    sums = pl.BlockSpec(memory_space=pltpu.VMEM)
    both = pltpu.VMEM((width // 2, 2 * width), BF16)
    part = jax.ShapeDtypeStruct((WIN, width), BF16)
    return pl.pallas_call(
        first_kernel,
        grid_spec=pltpu.PrefetchScalarGridSpec(
            num_scalar_prefetch=1,
            grid=(width // FOUR,),
            in_specs=[pl.BlockSpec(memory_space=pltpu.SMEM)]
            + [rim] * 6
            + [rest, rest, left, column, column]
            + turned_specs(width, count)
            + [pl.BlockSpec(memory_space=pl.ANY)],
            out_specs=[full, rim, rim, sums, sums],
            scratch_shapes=[
                pltpu.VMEM((count, FOUR), BF16),
                pltpu.VMEM((count, width), BF16),
                pltpu.SemaphoreType.DMA,
            ],
        ),
        out_shape=[jax.ShapeDtypeStruct((count, width), BF16), part, part, both, both],
        compiler_params=pltpu.CompilerParams(vmem_limit_bytes=ROOM),
        cost_estimate=SMALL,
        name="first_block",
    )(core, bias, *own, *partial, *late, tokens_l, w_key, w_value, *[turned] * 4, out_grad)


def last_kernel(
    core_ref, xn_ref, gn_ref, wq_ref, wk_ref, wv_ref, wo_ref, k_ref, v_ref, pk_ref, pv_ref, dk0_ref, dv0_ref,
    dkm_ref, dvm_ref, x0, x1, x2, x3, dk_ref, dv_ref, sa_ref, sb_ref, keep_ref,
):
    upper = upper_triangle()
    tokens = xn_ref[...]
    queries = bf(dot(tokens, wq_ref[...], 1, 0))
    keys = jnp.concatenate([k_ref[...], bf(dot(tokens, wk_ref[...], 1, 0))], axis=0)
    values = jnp.concatenate([v_ref[...], bf(dot(tokens, wv_ref[...], 1, 0))], axis=0)
    grads = bf(dot(gn_ref[...], wo_ref[...], 1, 1))
    block = [(queries[:, c], grads[:, c], keys[:, c], values[:, c]) for c in lanes(FOUR)]
    scores = [scores_of(entry, None) for entry in block]
    weights = [probs_of(entry, upper) for entry in scores]
    deltas = [delta_of(*entry)[1] for entry in zip(block, weights)]
    end = dk_ref.shape[0] - WIN
    dk_ref[:WIN, :] = dk0_ref[...]
    dv_ref[:WIN, :] = dv0_ref[...]
    dk_ref[WIN:end, :] = dkm_ref[...]
    dv_ref[WIN:end, :] = dvm_ref[...]
    for i, c in enumerate(lanes(FOUR)):
        ds = score_grads(scores[i], weights[i], deltas[i])
        dk_ref[end:, c] = bf((pk_ref[:, c] + dot(ds[:, :WIN], block[i][0], 0, 0)) * SCALE)
        dv_ref[end:, c] = bf(pv_ref[:, c] + dot(weights[i][1][:, :WIN], block[i][1], 0, 0))
    start = pl.program_id(0) * FOUR
    store_product((x0, x1, x2, x3), dk_ref[...], (sa_ref, sb_ref), keep_ref, start)
    store_product((x0, x1, x2, x3), dv_ref[...], (sa_ref, sb_ref), keep_ref, start + keep_ref.shape[1] // 2)


def last_block(core, tokens_n, grads_n, weights, last, partial, first, middle, turned):
    width, count = turned.shape
    column = pl.BlockSpec((width, FOUR), lambda j, c: (0, j))
    row = pl.BlockSpec((FOUR, width), lambda j, c: (j, 0))
    rim = pl.BlockSpec((WIN, FOUR), lambda j, c: (0, j))
    near = pl.BlockSpec((WIN, width), lambda j, c: (0, 0))
    mid = pl.BlockSpec((count - 2 * WIN, FOUR), lambda j, c: (0, j))
    full = pl.BlockSpec((count, FOUR), lambda j, c: (0, j))
    sums = pl.BlockSpec(memory_space=pltpu.VMEM)
    grad = jax.ShapeDtypeStruct((count, width), BF16)
    both = pltpu.VMEM((width // 2, 2 * width), BF16)
    half = pl.BlockSpec(memory_space=pltpu.VMEM)
    part_sum = pltpu.VMEM((width // 4, 2 * width), BF16)
    return pl.pallas_call(
        last_kernel,
        grid_spec=pltpu.PrefetchScalarGridSpec(
            num_scalar_prefetch=1,
            grid=(width // FOUR,),
            in_specs=[near, near, column, column, column, row] + [rim] * 6 + [mid, mid] + turned_specs(width, count),
            out_specs=[full, full, half, half, sums],
        ),
        out_shape=[grad, grad, part_sum, part_sum, both],
        compiler_params=pltpu.CompilerParams(vmem_limit_bytes=ROOM),
        cost_estimate=SMALL,
        name="last_block",
    )(core, tokens_n, grads_n, *weights, *last, *partial, *first, *middle, *[turned] * 4)


def chip_sum(sends, keep, meanwhile=None):
    got = [lax.ppermute(send, "co", [(0, 1), (1, 0)]) for send in sends]
    if meanwhile is not None:
        *got, meanwhile = lax.optimization_barrier((*got, meanwhile))
    return bf(keep.astype(F32) + jnp.concatenate(got, axis=0).astype(F32)), meanwhile


def piece_sum(pieces, width):
    return jnp.sum(pieces.reshape(-1, 8, width).astype(F32), axis=0)


def passed_along(block, distance):
    size = 1
    for axis in SEQ:
        size *= lax.axis_size(axis)
    route = [(i - distance, i) for i in range(size) if 0 <= i - distance < size]
    return lax.ppermute(block, SEQ, route)


def on_device(tokens, out_grad, w_query, w_key, w_value, w_output, grad_accum):
    tokens = tokens[0]
    out_grad = out_grad[0]
    count, width = tokens.shape
    core = lax.axis_index("co")
    which = core.reshape(1)
    first = (lax.axis_index("y") + lax.axis_index("z") + lax.axis_index("xl")) == 0
    bias = jnp.where(first, NEG, 0.0).astype(F32).reshape(1)
    tokens_l = passed_along(tokens[count - WIN :], 1)
    weights = (w_query, w_key, w_value, w_output)
    turned, head_x, head_g, *rest = front(tokens, out_grad, *weights)
    tokens_n = passed_along(head_x, -1)
    grads_n = passed_along(head_g, -1)
    own, last, late, middle, partial_0, partial_z = rest[:4], rest[4:6], rest[6:8], rest[8:10], rest[10:12], rest[12:]
    query_grad, key_0, value_0, send, keep = first_block(
        which, bias, own, partial_0, late, out_grad, tokens_l, w_key, w_value, turned
    )
    send, tokens_n = lax.optimization_barrier((send, tokens_n))
    both, _ = chip_sum((send,), keep)
    pieces_qo = lax.all_to_all(both, CHIPS, 0, 0, tiled=True)
    tokens_n, _ = lax.optimization_barrier((tokens_n, both))
    key_grad, value_grad, send_a, send_b, keep = last_block(
        which, tokens_n, grads_n, weights, last, partial_z, (key_0, value_0), middle, turned
    )
    send_a, send_b, query_grad = lax.optimization_barrier((send_a, send_b, query_grad))
    both, in_query = chip_sum((send_a, send_b), keep, dot(query_grad, w_query, 1, 1))
    pieces_kv = lax.all_to_all(both, CHIPS, 0, 0, tiled=True)
    in_grad = bf(in_query + dot(key_grad, w_key, 1, 1) + dot(value_grad, w_value, 1, 1))
    total = count
    for axis in AXES:
        total *= lax.axis_size(axis)
    factor = 1.0 / total**0.5
    sum_qo = piece_sum(pieces_qo, 2 * width)
    sum_kv = piece_sum(pieces_kv, 2 * width)
    summed = jnp.concatenate([sum_qo[:, :width], sum_kv, sum_qo[:, width:]], axis=1)
    return in_grad[None], grad_accum + summed * factor


def solution(mesh):
    fine = Mesh(mesh.devices.reshape(2, 2, 4, 4, 2), AXES)
    rows = P(("xh", "co"), SEQ, None)
    accum = P(AXES, None)
    return jax.shard_map(
        on_device,
        mesh=fine,
        in_specs=(rows, rows, P(), P(), P(), P(), accum),
        out_specs=(rows, accum),
        check_vma=False,
    )
```

```python
import jax
import jax.numpy as jnp
from jax import lax
from jax.experimental import pallas as pl
from jax.experimental.pallas import tpu as pltpu
from jax.sharding import Mesh
from jax.sharding import PartitionSpec as P

HD = 128
WIN = 256
LOG2E = 1.4426950408889634
SCALE = 1.0 / HD**0.5
AXES = ("xh", "co", "y", "z", "xl")
SEQ = ("y", "z", "xl")
CHIPS = ("xh", "y", "z", "xl")
F32 = jnp.float32
BF16 = jnp.bfloat16


def dot(a, b, ca, cb):
    return lax.dot_general(a, b, (((ca,), (cb,)), ((), ())), preferred_element_type=F32)


SMALL = pl.CostEstimate(flops=10**8, bytes_accessed=10**5, transcendentals=0)
VMEM = 60 * 2**20
ROOM = 57 * 2**20
PAIR = 2 * HD
FOUR = 4 * HD
HALF = WIN // 2
NEG = -1e30


def bf(value):
    return value.astype(BF16)


def upper_triangle():
    rows = lax.broadcasted_iota(jnp.int32, (HALF, HALF), 0)
    cols = lax.broadcasted_iota(jnp.int32, (HALF, HALF), 1)
    return cols > rows


def scores_of(block, bias):
    query, grad, key, value = block
    scores = dot(query, key, 1, 1)
    if bias is not None:
        scores = jnp.concatenate([scores[:, :WIN] + bias, scores[:, WIN:]], axis=1)
    return scores, dot(grad, value, 1, 1)


def runs_of(array):
    return [
        [array[h * HALF : (h + 1) * HALF, (h + i) * HALF : (h + i + 1) * HALF] for i in range(3)] for h in range(2)
    ]


def whole_of(runs):
    zero = jnp.zeros((HALF, HALF), BF16)
    top, bottom = [[bf(part) for part in run] for run in runs]
    return jnp.concatenate(
        [jnp.concatenate(top + [zero], axis=1), jnp.concatenate([zero] + bottom, axis=1)], axis=0
    )


def probs_of(scores, upper):
    probs = []
    for first, middle, last in runs_of(scores[0]):
        run = [jnp.where(upper, first, NEG), middle, jnp.where(upper, NEG, last)]
        top = jnp.max(jnp.maximum(jnp.maximum(run[0], run[1]), run[2]), axis=1, keepdims=True)
        shift = top * (SCALE * LOG2E)
        e = [jnp.exp2(part * (SCALE * LOG2E) - shift) for part in run]
        inv = 1.0 / jnp.sum(e[0] + e[1] + e[2], axis=1, keepdims=True)
        probs.append([part * inv for part in e])
    return probs, whole_of(probs)


def delta_of(block, weights):
    grad, value = block[1], block[3]
    attended = bf(dot(weights[1], value, 1, 0))
    return attended, jnp.sum(grad.astype(F32) * attended.astype(F32), axis=1, keepdims=True)


def score_grads(scores, weights, delta):
    halves = (delta[:HALF], delta[HALF:])
    return whole_of(
        [
            [p * (d - half) for p, d in zip(probs, prob_grads)]
            for probs, prob_grads, half in zip(weights[0], runs_of(scores[1]), halves)
        ]
    )


def turned_specs(width, count):
    def pick(half, other):
        return pl.BlockSpec((width // 4, count), lambda j, c: (2 * half + (1 - c[0] if other else c[0]), 0))

    return [pick(0, True), pick(1, True), pick(0, False), pick(1, False)]


def store_product(turned, right, send_refs, keep_ref, start):
    product = bf(dot(jnp.concatenate([part[...] for part in turned], axis=0), right, 1, 0))
    half = product.shape[0] // 2
    columns = pl.ds(pl.multiple_of(start, FOUR), FOUR)
    piece = half // len(send_refs)
    for i, send_ref in enumerate(send_refs):
        send_ref[:, columns] = product[i * piece : (i + 1) * piece]
    keep_ref[:, columns] = product[half:]


def lanes(width):
    return [slice(h * HD, (h + 1) * HD) for h in range(width // HD)]


def front_kernel(
    x_ref, g_ref, wq_ref, wk_ref, wv_ref, wo_ref, part_ref,
    turned_ref, xh_ref, gh_ref, q0_ref, k0_ref, v0_ref, a0_ref, kz_ref, vz_ref, att_ref, dq_ref, dk_ref, dv_ref,
    pk0_ref, pv0_ref, pkz_ref, pvz_ref, q_ref, k_ref, v_ref, a_ref,
):
    turned_ref[...] = part_ref[...].T

    @pl.when(pl.program_id(0) == 0)
    def _():
        xh_ref[...] = x_ref[:WIN, :]
        gh_ref[...] = g_ref[:WIN, :]

    upper = upper_triangle()
    count = x_ref.shape[0]
    blocks = count // WIN
    span = [slice(b * WIN, (b + 1) * WIN) for b in range(blocks)]
    q_ref[...] = bf(dot(x_ref[...], wq_ref[...], 1, 0))
    k_ref[...] = bf(dot(x_ref[...], wk_ref[...], 1, 0))
    v_ref[...] = bf(dot(x_ref[...], wv_ref[...], 1, 0))
    a_ref[...] = bf(dot(g_ref[...], wo_ref[...], 1, 1))
    q0_ref[...] = q_ref[:WIN, :]
    k0_ref[...] = k_ref[:WIN, :]
    v0_ref[...] = v_ref[:WIN, :]
    a0_ref[...] = a_ref[:WIN, :]
    kz_ref[...] = k_ref[count - WIN :, :]
    vz_ref[...] = v_ref[count - WIN :, :]
    window = [slice((b - 1) * WIN, (b + 1) * WIN) for b in range(blocks)]
    entries = [(c, b) for c in lanes(PAIR) for b in range(1, blocks)]
    block = [
        tuple(
            ref[rows, c]
            for ref, rows in ((q_ref, span[b]), (a_ref, span[b]), (k_ref, window[b]), (v_ref, window[b]))
        )
        for c, b in entries
    ]
    scores = [scores_of(entry, None) for entry in block]
    weights = [probs_of(entry, upper) for entry in scores]
    deltas = []
    for i, (c, b) in enumerate(entries):
        attended, delta = delta_of(block[i], weights[i])
        att_ref[span[b - 1], c] = attended
        deltas.append(delta)
    sgrads = [score_grads(*entry) for entry in zip(scores, weights, deltas)]
    for i, (c, b) in enumerate(entries):
        query, grad, key, _ = block[i]
        dq_ref[span[b - 1], c] = bf(dot(sgrads[i], key, 1, 0) * SCALE)
        dk = dot(sgrads[i], query, 0, 0)
        dv = dot(weights[i][1], grad, 0, 0)
        dk_l = dk[:WIN]
        dv_l = dv[:WIN]
        if b == 1:
            pk0_ref[:, c] = dk_l
            pv0_ref[:, c] = dv_l
        else:
            dk_ref[span[b - 2], c] = bf((dk_open + dk_l) * SCALE)
            dv_ref[span[b - 2], c] = bf(dv_open + dv_l)
        dk_open = dk[WIN:]
        dv_open = dv[WIN:]
        if b == blocks - 1:
            pkz_ref[:, c] = dk_open
            pvz_ref[:, c] = dv_open


def front(tokens, out_grad, w_query, w_key, w_value, w_output):
    count, width = tokens.shape
    whole = pl.BlockSpec((count, width), lambda j: (0, 0))
    column = pl.BlockSpec((width, PAIR), lambda j: (0, j))
    row = pl.BlockSpec((PAIR, width), lambda j: (j, 0))

    def out(rows):
        return pl.BlockSpec((rows, PAIR), lambda j: (0, j))

    def like(rows, dtype=BF16):
        return jax.ShapeDtypeStruct((rows, width), dtype)

    head = pl.BlockSpec((WIN, width), lambda j: (0, 0))
    rim, late, mid = WIN, count - WIN, count - 2 * WIN
    heights = [rim] * 6 + [late, late, mid, mid]
    return pl.pallas_call(
        front_kernel,
        grid=(width // PAIR,),
        in_specs=[whole, whole, column, column, column, row, out(count)],
        out_specs=[row, head, head] + [out(h) for h in heights] + [out(rim)] * 4,
        out_shape=[like(width), like(rim), like(rim)] + [like(h) for h in heights] + [like(rim, F32)] * 4,
        scratch_shapes=[pltpu.VMEM((count, PAIR), BF16)] * 4,
        compiler_params=pltpu.CompilerParams(vmem_limit_bytes=VMEM),
        cost_estimate=SMALL,
        name="front",
    )(tokens, out_grad, w_query, w_key, w_value, w_output, tokens)


def first_kernel(
    core_ref, bias_ref, q_ref, k_ref, v_ref, a_ref, pk_ref, pv_ref, att_in, dq_in, xl_ref, wk_ref, wv_ref,
    x0, x1, x2, x3, g_hbm, dq_ref, dk_ref, dv_ref, send_ref, keep_ref, att_ref, g_ref, g_sem,
):
    step = pl.program_id(0)
    fetch = pltpu.make_async_copy(g_hbm, g_ref, g_sem)

    @pl.when(step == 0)
    def _():
        fetch.start()

    upper = upper_triangle()
    keys_l = bf(dot(xl_ref[...], wk_ref[...], 1, 0))
    values_l = bf(dot(xl_ref[...], wv_ref[...], 1, 0))
    keys = jnp.concatenate([keys_l, k_ref[...]], axis=0)
    values = jnp.concatenate([values_l, v_ref[...]], axis=0)
    block = [(q_ref[:, c], a_ref[:, c], keys[:, c], values[:, c]) for c in lanes(FOUR)]
    scores = [scores_of(entry, bias_ref[0]) for entry in block]
    weights = [probs_of(entry, upper) for entry in scores]
    deltas = []
    for i, c in enumerate(lanes(FOUR)):
        attended, delta = delta_of(block[i], weights[i])
        att_ref[:WIN, c] = attended
        deltas.append(delta)
    att_ref[WIN:, :] = att_in[...]
    dq_ref[WIN:, :] = dq_in[...]
    for i, c in enumerate(lanes(FOUR)):
        query, grad, key, _ = block[i]
        ds = score_grads(scores[i], weights[i], deltas[i])
        dq_ref[:WIN, c] = bf(dot(ds, key, 1, 0) * SCALE)
        dk_ref[:, c] = bf((pk_ref[:, c] + dot(ds[:, WIN:], query, 0, 0)) * SCALE)
        dv_ref[:, c] = bf(pv_ref[:, c] + dot(weights[i][1][:, WIN:], grad, 0, 0))
    store_product((x0, x1, x2, x3), dq_ref[...], (send_ref,), keep_ref, step * FOUR)

    @pl.when(step == 0)
    def _():
        fetch.wait()

    product = bf(dot(att_ref[...], g_ref[...], 0, 0))
    rows = pl.ds(pl.multiple_of(step * PAIR, PAIR), PAIR)
    width = g_ref.shape[1]
    mine = core_ref[0] == 0
    keep_ref[rows, width:] = jnp.where(mine, product[:PAIR], product[PAIR:])
    send_ref[rows, width:] = jnp.where(mine, product[PAIR:], product[:PAIR])


def first_block(core, bias, own, partial, late, out_grad, tokens_l, w_key, w_value, turned):
    width, count = turned.shape
    rim = pl.BlockSpec((WIN, FOUR), lambda j, c: (0, j))
    rest = pl.BlockSpec((count - WIN, FOUR), lambda j, c: (0, j))
    full = pl.BlockSpec((count, FOUR), lambda j, c: (0, j))
    left = pl.BlockSpec((WIN, width), lambda j, c: (0, 0))
    column = pl.BlockSpec((width, FOUR), lambda j, c: (0, j))
    sums = pl.BlockSpec(memory_space=pltpu.VMEM)
    both = pltpu.VMEM((width // 2, 2 * width), BF16)
    part = jax.ShapeDtypeStruct((WIN, width), BF16)
    return pl.pallas_call(
        first_kernel,
        grid_spec=pltpu.PrefetchScalarGridSpec(
            num_scalar_prefetch=1,
            grid=(width // FOUR,),
            in_specs=[pl.BlockSpec(memory_space=pltpu.SMEM)]
            + [rim] * 6
            + [rest, rest, left, column, column]
            + turned_specs(width, count)
            + [pl.BlockSpec(memory_space=pl.ANY)],
            out_specs=[full, rim, rim, sums, sums],
            scratch_shapes=[
                pltpu.VMEM((count, FOUR), BF16),
                pltpu.VMEM((count, width), BF16),
                pltpu.SemaphoreType.DMA,
            ],
        ),
        out_shape=[jax.ShapeDtypeStruct((count, width), BF16), part, part, both, both],
        compiler_params=pltpu.CompilerParams(vmem_limit_bytes=ROOM),
        cost_estimate=SMALL,
        name="first_block",
    )(core, bias, *own, *partial, *late, tokens_l, w_key, w_value, *[turned] * 4, out_grad)


def last_kernel(
    core_ref, xn_ref, gn_ref, wq_ref, wk_ref, wv_ref, wo_ref, k_ref, v_ref, pk_ref, pv_ref, dk0_ref, dv0_ref,
    dkm_ref, dvm_ref, x0, x1, x2, x3, dk_ref, dv_ref, sa_ref, sb_ref, keep_ref,
):
    upper = upper_triangle()
    tokens = xn_ref[...]
    queries = bf(dot(tokens, wq_ref[...], 1, 0))
    keys = jnp.concatenate([k_ref[...], bf(dot(tokens, wk_ref[...], 1, 0))], axis=0)
    values = jnp.concatenate([v_ref[...], bf(dot(tokens, wv_ref[...], 1, 0))], axis=0)
    grads = bf(dot(gn_ref[...], wo_ref[...], 1, 1))
    block = [(queries[:, c], grads[:, c], keys[:, c], values[:, c]) for c in lanes(FOUR)]
    scores = [scores_of(entry, None) for entry in block]
    weights = [probs_of(entry, upper) for entry in scores]
    deltas = [delta_of(*entry)[1] for entry in zip(block, weights)]
    end = dk_ref.shape[0] - WIN
    dk_ref[:WIN, :] = dk0_ref[...]
    dv_ref[:WIN, :] = dv0_ref[...]
    dk_ref[WIN:end, :] = dkm_ref[...]
    dv_ref[WIN:end, :] = dvm_ref[...]
    for i, c in enumerate(lanes(FOUR)):
        ds = score_grads(scores[i], weights[i], deltas[i])
        dk_ref[end:, c] = bf((pk_ref[:, c] + dot(ds[:, :WIN], block[i][0], 0, 0)) * SCALE)
        dv_ref[end:, c] = bf(pv_ref[:, c] + dot(weights[i][1][:, :WIN], block[i][1], 0, 0))
    start = pl.program_id(0) * FOUR
    store_product((x0, x1, x2, x3), dk_ref[...], (sa_ref, sb_ref), keep_ref, start)
    store_product((x0, x1, x2, x3), dv_ref[...], (sa_ref, sb_ref), keep_ref, start + keep_ref.shape[1] // 2)


def last_block(core, tokens_n, grads_n, weights, last, partial, first, middle, turned):
    width, count = turned.shape
    column = pl.BlockSpec((width, FOUR), lambda j, c: (0, j))
    row = pl.BlockSpec((FOUR, width), lambda j, c: (j, 0))
    rim = pl.BlockSpec((WIN, FOUR), lambda j, c: (0, j))
    near = pl.BlockSpec((WIN, width), lambda j, c: (0, 0))
    mid = pl.BlockSpec((count - 2 * WIN, FOUR), lambda j, c: (0, j))
    full = pl.BlockSpec((count, FOUR), lambda j, c: (0, j))
    sums = pl.BlockSpec(memory_space=pltpu.VMEM)
    grad = jax.ShapeDtypeStruct((count, width), BF16)
    both = pltpu.VMEM((width // 2, 2 * width), BF16)
    half = pl.BlockSpec(memory_space=pltpu.VMEM)
    part_sum = pltpu.VMEM((width // 4, 2 * width), BF16)
    return pl.pallas_call(
        last_kernel,
        grid_spec=pltpu.PrefetchScalarGridSpec(
            num_scalar_prefetch=1,
            grid=(width // FOUR,),
            in_specs=[near, near, column, column, column, row] + [rim] * 6 + [mid, mid] + turned_specs(width, count),
            out_specs=[full, full, half, half, sums],
        ),
        out_shape=[grad, grad, part_sum, part_sum, both],
        compiler_params=pltpu.CompilerParams(vmem_limit_bytes=ROOM),
        cost_estimate=SMALL,
        name="last_block",
    )(core, tokens_n, grads_n, *weights, *last, *partial, *first, *middle, *[turned] * 4)


def chip_sum(sends, keep):
    got = [lax.ppermute(send, "co", [(0, 1), (1, 0)]) for send in sends]
    return bf(keep.astype(F32) + jnp.concatenate(got, axis=0).astype(F32))


def piece_sum(pieces, width):
    return jnp.sum(pieces.reshape(-1, 8, width).astype(F32), axis=0)


def passed_along(block, distance):
    size = 1
    for axis in SEQ:
        size *= lax.axis_size(axis)
    route = [(i - distance, i) for i in range(size) if 0 <= i - distance < size]
    return lax.ppermute(block, SEQ, route)


def on_device(tokens, out_grad, w_query, w_key, w_value, w_output, grad_accum):
    tokens = tokens[0]
    out_grad = out_grad[0]
    count, width = tokens.shape
    core = lax.axis_index("co")
    which = core.reshape(1)
    first = (lax.axis_index("y") + lax.axis_index("z") + lax.axis_index("xl")) == 0
    bias = jnp.where(first, NEG, 0.0).astype(F32).reshape(1)
    tokens_l = passed_along(tokens[count - WIN :], 1)
    weights = (w_query, w_key, w_value, w_output)
    turned, head_x, head_g, *rest = front(tokens, out_grad, *weights)
    tokens_n = passed_along(head_x, -1)
    grads_n = passed_along(head_g, -1)
    own, last, late, middle, partial_0, partial_z = rest[:4], rest[4:6], rest[6:8], rest[8:10], rest[10:12], rest[12:]
    query_grad, key_0, value_0, send, keep = first_block(
        which, bias, own, partial_0, late, out_grad, tokens_l, w_key, w_value, turned
    )
    send, tokens_n = lax.optimization_barrier((send, tokens_n))
    both = chip_sum((send,), keep)
    pieces_qo = lax.all_to_all(both, CHIPS, 0, 0, tiled=True)
    tokens_n, _ = lax.optimization_barrier((tokens_n, both))
    key_grad, value_grad, send_a, send_b, keep = last_block(
        which, tokens_n, grads_n, weights, last, partial_z, (key_0, value_0), middle, turned
    )
    both = chip_sum((send_a, send_b), keep)
    sum_qo = piece_sum(pieces_qo, 2 * width)
    query_grad, both, sum_qo = lax.optimization_barrier((query_grad, both, sum_qo))
    pieces_kv = lax.all_to_all(both, CHIPS, 0, 0, tiled=True)
    in_grad = bf(
        dot(query_grad, w_query, 1, 1) + dot(key_grad, w_key, 1, 1) + dot(value_grad, w_value, 1, 1)
    )
    total = count
    for axis in AXES:
        total *= lax.axis_size(axis)
    factor = 1.0 / total**0.5
    sum_kv = piece_sum(pieces_kv, 2 * width)
    summed = jnp.concatenate([sum_qo[:, :width], sum_kv, sum_qo[:, width:]], axis=1)
    return in_grad[None], grad_accum + summed * factor


def solution(mesh):
    fine = Mesh(mesh.devices.reshape(2, 2, 4, 4, 2), AXES)
    rows = P(("xh", "co"), SEQ, None)
    accum = P(AXES, None)
    return jax.shard_map(
        on_device,
        mesh=fine,
        in_specs=(rows, rows, P(), P(), P(), P(), accum),
        out_specs=(rows, accum),
        check_vma=False,
    )
```

```python
import jax
import jax.numpy as jnp
from jax import lax
from jax.experimental import pallas as pl
from jax.experimental.pallas import tpu as pltpu
from jax.sharding import Mesh
from jax.sharding import PartitionSpec as P

HD = 128
WIN = 256
LOG2E = 1.4426950408889634
SCALE = 1.0 / HD**0.5
AXES = ("xh", "co", "y", "z", "xl")
SEQ = ("y", "z", "xl")
CHIPS = ("xh", "y", "z", "xl")
F32 = jnp.float32
BF16 = jnp.bfloat16


def dot(a, b, ca, cb):
    return lax.dot_general(a, b, (((ca,), (cb,)), ((), ())), preferred_element_type=F32)


SMALL = pl.CostEstimate(flops=10**8, bytes_accessed=10**5, transcendentals=0)
VMEM = 60 * 2**20
FULL = 127 * 2**19
ROOM = 57 * 2**20
PAIR = 2 * HD
FOUR = 4 * HD
HALF = WIN // 2
NEG = -1e30


def bf(value):
    return value.astype(BF16)


def upper_triangle():
    rows = lax.broadcasted_iota(jnp.int32, (HALF, HALF), 0)
    cols = lax.broadcasted_iota(jnp.int32, (HALF, HALF), 1)
    return cols > rows


def scores_of(block, bias):
    query, grad, key, value = block
    scores = dot(query, key, 1, 1)
    if bias is not None:
        scores = jnp.concatenate([scores[:, :WIN] + bias, scores[:, WIN:]], axis=1)
    return scores, dot(grad, value, 1, 1)


def runs_of(array):
    return [
        [array[h * HALF : (h + 1) * HALF, (h + i) * HALF : (h + i + 1) * HALF] for i in range(3)] for h in range(2)
    ]


def whole_of(runs):
    zero = jnp.zeros((HALF, HALF), BF16)
    top, bottom = [[bf(part) for part in run] for run in runs]
    return jnp.concatenate(
        [jnp.concatenate(top + [zero], axis=1), jnp.concatenate([zero] + bottom, axis=1)], axis=0
    )


def probs_of(scores, upper):
    probs = []
    for first, middle, last in runs_of(scores[0]):
        run = [jnp.where(upper, first, NEG), middle, jnp.where(upper, NEG, last)]
        top = jnp.max(jnp.maximum(jnp.maximum(run[0], run[1]), run[2]), axis=1, keepdims=True)
        shift = top * (SCALE * LOG2E)
        e = [jnp.exp2(part * (SCALE * LOG2E) - shift) for part in run]
        inv = 1.0 / jnp.sum(e[0] + e[1] + e[2], axis=1, keepdims=True)
        probs.append([part * inv for part in e])
    return probs, whole_of(probs)


def delta_of(block, weights):
    grad, value = block[1], block[3]
    attended = bf(dot(weights[1], value, 1, 0))
    return attended, jnp.sum(grad.astype(F32) * attended.astype(F32), axis=1, keepdims=True)


def score_grads(scores, weights, delta):
    halves = (delta[:HALF], delta[HALF:])
    return whole_of(
        [
            [p * (d - half) for p, d in zip(probs, prob_grads)]
            for probs, prob_grads, half in zip(weights[0], runs_of(scores[1]), halves)
        ]
    )


def turned_specs(width, count):
    def pick(half, other):
        return pl.BlockSpec((width // 4, count), lambda j, c: (2 * half + (1 - c[0] if other else c[0]), 0))

    return [pick(0, True), pick(1, True), pick(0, False), pick(1, False)]


def store_product(turned, right, send_refs, keep_ref, start):
    product = bf(dot(jnp.concatenate([part[...] for part in turned], axis=0), right, 1, 0))
    half = product.shape[0] // 2
    columns = pl.ds(pl.multiple_of(start, FOUR), FOUR)
    piece = half // len(send_refs)
    for i, send_ref in enumerate(send_refs):
        send_ref[:, columns] = product[i * piece : (i + 1) * piece]
    keep_ref[:, columns] = product[half:]


def lanes(width):
    return [slice(h * HD, (h + 1) * HD) for h in range(width // HD)]


def front_kernel(
    x_ref, g_ref, wq_ref, wk_ref, wv_ref, wo_ref, part_ref,
    turned_ref, xh_ref, gh_ref, q0_ref, k0_ref, v0_ref, a0_ref, kz_ref, vz_ref, att_ref, dq_ref, dk_ref, dv_ref,
    pk0_ref, pv0_ref, pkz_ref, pvz_ref, q_ref, k_ref, v_ref, a_ref,
):
    turned_ref[...] = part_ref[...].T

    @pl.when(pl.program_id(0) == 0)
    def _():
        xh_ref[...] = x_ref[:WIN, :]
        gh_ref[...] = g_ref[:WIN, :]

    upper = upper_triangle()
    count = x_ref.shape[0]
    blocks = count // WIN
    span = [slice(b * WIN, (b + 1) * WIN) for b in range(blocks)]
    q_ref[...] = bf(dot(x_ref[...], wq_ref[...], 1, 0))
    k_ref[...] = bf(dot(x_ref[...], wk_ref[...], 1, 0))
    v_ref[...] = bf(dot(x_ref[...], wv_ref[...], 1, 0))
    a_ref[...] = bf(dot(g_ref[...], wo_ref[...], 1, 1))
    q0_ref[...] = q_ref[:WIN, :]
    k0_ref[...] = k_ref[:WIN, :]
    v0_ref[...] = v_ref[:WIN, :]
    a0_ref[...] = a_ref[:WIN, :]
    kz_ref[...] = k_ref[count - WIN :, :]
    vz_ref[...] = v_ref[count - WIN :, :]
    window = [slice((b - 1) * WIN, (b + 1) * WIN) for b in range(blocks)]
    entries = [(c, b) for c in lanes(PAIR) for b in range(1, blocks)]
    block = [
        tuple(
            ref[rows, c]
            for ref, rows in ((q_ref, span[b]), (a_ref, span[b]), (k_ref, window[b]), (v_ref, window[b]))
        )
        for c, b in entries
    ]
    scores = [scores_of(entry, None) for entry in block]
    weights = [probs_of(entry, upper) for entry in scores]
    deltas = []
    for i, (c, b) in enumerate(entries):
        attended, delta = delta_of(block[i], weights[i])
        att_ref[span[b - 1], c] = attended
        deltas.append(delta)
    sgrads = [score_grads(*entry) for entry in zip(scores, weights, deltas)]
    for i, (c, b) in enumerate(entries):
        query, grad, key, _ = block[i]
        dq_ref[span[b - 1], c] = bf(dot(sgrads[i], key, 1, 0) * SCALE)
        dk = dot(sgrads[i], query, 0, 0)
        dv = dot(weights[i][1], grad, 0, 0)
        dk_l = dk[:WIN]
        dv_l = dv[:WIN]
        if b == 1:
            pk0_ref[:, c] = dk_l
            pv0_ref[:, c] = dv_l
        else:
            dk_ref[span[b - 2], c] = bf((dk_open + dk_l) * SCALE)
            dv_ref[span[b - 2], c] = bf(dv_open + dv_l)
        dk_open = dk[WIN:]
        dv_open = dv[WIN:]
        if b == blocks - 1:
            pkz_ref[:, c] = dk_open
            pvz_ref[:, c] = dv_open


def front(tokens, out_grad, w_query, w_key, w_value, w_output):
    count, width = tokens.shape
    whole = pl.BlockSpec((count, width), lambda j: (0, 0))
    column = pl.BlockSpec((width, PAIR), lambda j: (0, j))
    row = pl.BlockSpec((PAIR, width), lambda j: (j, 0))

    def out(rows):
        return pl.BlockSpec((rows, PAIR), lambda j: (0, j))

    def like(rows, dtype=BF16):
        return jax.ShapeDtypeStruct((rows, width), dtype)

    head = pl.BlockSpec((WIN, width), lambda j: (0, 0))
    rim, late, mid = WIN, count - WIN, count - 2 * WIN
    heights = [rim] * 6 + [late, late, mid, mid]
    return pl.pallas_call(
        front_kernel,
        grid=(width // PAIR,),
        in_specs=[whole, whole, column, column, column, row, out(count)],
        out_specs=[row, head, head] + [out(h) for h in heights] + [out(rim)] * 4,
        out_shape=[like(width), like(rim), like(rim)] + [like(h) for h in heights] + [like(rim, F32)] * 4,
        scratch_shapes=[pltpu.VMEM((count, PAIR), BF16)] * 4,
        compiler_params=pltpu.CompilerParams(vmem_limit_bytes=FULL),
        cost_estimate=SMALL,
        name="front",
    )(tokens, out_grad, w_query, w_key, w_value, w_output, tokens)


def first_kernel(
    core_ref, bias_ref, q_ref, k_ref, v_ref, a_ref, pk_ref, pv_ref, att_in, dq_in, xl_ref, wk_ref, wv_ref,
    x0, x1, x2, x3, g_hbm, dq_ref, dk_ref, dv_ref, send_ref, keep_ref, att_ref, g_ref, g_sem,
):
    step = pl.program_id(0)
    fetch = pltpu.make_async_copy(g_hbm, g_ref, g_sem)

    @pl.when(step == 0)
    def _():
        fetch.start()

    upper = upper_triangle()
    keys_l = bf(dot(xl_ref[...], wk_ref[...], 1, 0))
    values_l = bf(dot(xl_ref[...], wv_ref[...], 1, 0))
    keys = jnp.concatenate([keys_l, k_ref[...]], axis=0)
    values = jnp.concatenate([values_l, v_ref[...]], axis=0)
    block = [(q_ref[:, c], a_ref[:, c], keys[:, c], values[:, c]) for c in lanes(FOUR)]
    scores = [scores_of(entry, bias_ref[0]) for entry in block]
    weights = [probs_of(entry, upper) for entry in scores]
    deltas = []
    for i, c in enumerate(lanes(FOUR)):
        attended, delta = delta_of(block[i], weights[i])
        att_ref[:WIN, c] = attended
        deltas.append(delta)
    att_ref[WIN:, :] = att_in[...]
    dq_ref[WIN:, :] = dq_in[...]
    for i, c in enumerate(lanes(FOUR)):
        query, grad, key, _ = block[i]
        ds = score_grads(scores[i], weights[i], deltas[i])
        dq_ref[:WIN, c] = bf(dot(ds, key, 1, 0) * SCALE)
        dk_ref[:, c] = bf((pk_ref[:, c] + dot(ds[:, WIN:], query, 0, 0)) * SCALE)
        dv_ref[:, c] = bf(pv_ref[:, c] + dot(weights[i][1][:, WIN:], grad, 0, 0))
    store_product((x0, x1, x2, x3), dq_ref[...], (send_ref,), keep_ref, step * FOUR)

    @pl.when(step == 0)
    def _():
        fetch.wait()

    product = bf(dot(att_ref[...], g_ref[...], 0, 0))
    rows = pl.ds(pl.multiple_of(step * PAIR, PAIR), PAIR)
    width = g_ref.shape[1]
    mine = core_ref[0] == 0
    keep_ref[rows, width:] = jnp.where(mine, product[:PAIR], product[PAIR:])
    send_ref[rows, width:] = jnp.where(mine, product[PAIR:], product[:PAIR])


def first_block(core, bias, own, partial, late, out_grad, tokens_l, w_key, w_value, turned):
    width, count = turned.shape
    rim = pl.BlockSpec((WIN, FOUR), lambda j, c: (0, j))
    rest = pl.BlockSpec((count - WIN, FOUR), lambda j, c: (0, j))
    full = pl.BlockSpec((count, FOUR), lambda j, c: (0, j))
    left = pl.BlockSpec((WIN, width), lambda j, c: (0, 0))
    column = pl.BlockSpec((width, FOUR), lambda j, c: (0, j))
    sums = pl.BlockSpec(memory_space=pltpu.VMEM)
    both = pltpu.VMEM((width // 2, 2 * width), BF16)
    part = jax.ShapeDtypeStruct((WIN, width), BF16)
    return pl.pallas_call(
        first_kernel,
        grid_spec=pltpu.PrefetchScalarGridSpec(
            num_scalar_prefetch=1,
            grid=(width // FOUR,),
            in_specs=[pl.BlockSpec(memory_space=pltpu.SMEM)]
            + [rim] * 6
            + [rest, rest, left, column, column]
            + turned_specs(width, count)
            + [pl.BlockSpec(memory_space=pl.ANY)],
            out_specs=[full, rim, rim, sums, sums],
            scratch_shapes=[
                pltpu.VMEM((count, FOUR), BF16),
                pltpu.VMEM((count, width), BF16),
                pltpu.SemaphoreType.DMA,
            ],
        ),
        out_shape=[jax.ShapeDtypeStruct((count, width), BF16), part, part, both, both],
        compiler_params=pltpu.CompilerParams(vmem_limit_bytes=ROOM),
        cost_estimate=SMALL,
        name="first_block",
    )(core, bias, *own, *partial, *late, tokens_l, w_key, w_value, *[turned] * 4, out_grad)


def last_kernel(
    core_ref, xn_ref, gn_ref, wq_ref, wk_ref, wv_ref, wo_ref, k_ref, v_ref, pk_ref, pv_ref, dk0_ref, dv0_ref,
    dkm_ref, dvm_ref, x0, x1, x2, x3, dk_ref, dv_ref, sa_ref, sb_ref, keep_ref,
):
    upper = upper_triangle()
    tokens = xn_ref[...]
    queries = bf(dot(tokens, wq_ref[...], 1, 0))
    keys = jnp.concatenate([k_ref[...], bf(dot(tokens, wk_ref[...], 1, 0))], axis=0)
    values = jnp.concatenate([v_ref[...], bf(dot(tokens, wv_ref[...], 1, 0))], axis=0)
    grads = bf(dot(gn_ref[...], wo_ref[...], 1, 1))
    block = [(queries[:, c], grads[:, c], keys[:, c], values[:, c]) for c in lanes(FOUR)]
    scores = [scores_of(entry, None) for entry in block]
    weights = [probs_of(entry, upper) for entry in scores]
    deltas = [delta_of(*entry)[1] for entry in zip(block, weights)]
    end = dk_ref.shape[0] - WIN
    dk_ref[:WIN, :] = dk0_ref[...]
    dv_ref[:WIN, :] = dv0_ref[...]
    dk_ref[WIN:end, :] = dkm_ref[...]
    dv_ref[WIN:end, :] = dvm_ref[...]
    for i, c in enumerate(lanes(FOUR)):
        ds = score_grads(scores[i], weights[i], deltas[i])
        dk_ref[end:, c] = bf((pk_ref[:, c] + dot(ds[:, :WIN], block[i][0], 0, 0)) * SCALE)
        dv_ref[end:, c] = bf(pv_ref[:, c] + dot(weights[i][1][:, :WIN], block[i][1], 0, 0))
    start = pl.program_id(0) * FOUR
    store_product((x0, x1, x2, x3), dk_ref[...], (sa_ref, sb_ref), keep_ref, start)
    store_product((x0, x1, x2, x3), dv_ref[...], (sa_ref, sb_ref), keep_ref, start + keep_ref.shape[1] // 2)


def last_block(core, tokens_n, grads_n, weights, last, partial, first, middle, turned):
    width, count = turned.shape
    column = pl.BlockSpec((width, FOUR), lambda j, c: (0, j))
    row = pl.BlockSpec((FOUR, width), lambda j, c: (j, 0))
    rim = pl.BlockSpec((WIN, FOUR), lambda j, c: (0, j))
    near = pl.BlockSpec((WIN, width), lambda j, c: (0, 0))
    mid = pl.BlockSpec((count - 2 * WIN, FOUR), lambda j, c: (0, j))
    full = pl.BlockSpec((count, FOUR), lambda j, c: (0, j))
    sums = pl.BlockSpec(memory_space=pltpu.VMEM)
    grad = jax.ShapeDtypeStruct((count, width), BF16)
    both = pltpu.VMEM((width // 2, 2 * width), BF16)
    half = pl.BlockSpec(memory_space=pltpu.VMEM)
    part_sum = pltpu.VMEM((width // 4, 2 * width), BF16)
    return pl.pallas_call(
        last_kernel,
        grid_spec=pltpu.PrefetchScalarGridSpec(
            num_scalar_prefetch=1,
            grid=(width // FOUR,),
            in_specs=[near, near, column, column, column, row] + [rim] * 6 + [mid, mid] + turned_specs(width, count),
            out_specs=[full, full, half, half, sums],
        ),
        out_shape=[grad, grad, part_sum, part_sum, both],
        compiler_params=pltpu.CompilerParams(vmem_limit_bytes=ROOM),
        cost_estimate=SMALL,
        name="last_block",
    )(core, tokens_n, grads_n, *weights, *last, *partial, *first, *middle, *[turned] * 4)


def chip_sum(sends, keep):
    got = [lax.ppermute(send, "co", [(0, 1), (1, 0)]) for send in sends]
    return bf(keep.astype(F32) + jnp.concatenate(got, axis=0).astype(F32))


def piece_sum(pieces, width):
    return jnp.sum(pieces.reshape(-1, 8, width).astype(F32), axis=0)


def passed_along(block, distance):
    size = 1
    for axis in SEQ:
        size *= lax.axis_size(axis)
    route = [(i - distance, i) for i in range(size) if 0 <= i - distance < size]
    return lax.ppermute(block, SEQ, route)


def on_device(tokens, out_grad, w_query, w_key, w_value, w_output, grad_accum):
    tokens = tokens[0]
    out_grad = out_grad[0]
    count, width = tokens.shape
    core = lax.axis_index("co")
    which = core.reshape(1)
    first = (lax.axis_index("y") + lax.axis_index("z") + lax.axis_index("xl")) == 0
    bias = jnp.where(first, NEG, 0.0).astype(F32).reshape(1)
    tokens_l = passed_along(tokens[count - WIN :], 1)
    weights = (w_query, w_key, w_value, w_output)
    turned, head_x, head_g, *rest = front(tokens, out_grad, *weights)
    tokens_n = passed_along(head_x, -1)
    grads_n = passed_along(head_g, -1)
    own, last, late, middle, partial_0, partial_z = rest[:4], rest[4:6], rest[6:8], rest[8:10], rest[10:12], rest[12:]
    query_grad, key_0, value_0, send, keep = first_block(
        which, bias, own, partial_0, late, out_grad, tokens_l, w_key, w_value, turned
    )
    send, tokens_n = lax.optimization_barrier((send, tokens_n))
    both = chip_sum((send,), keep)
    pieces_qo = lax.all_to_all(both, CHIPS, 0, 0, tiled=True)
    tokens_n, _ = lax.optimization_barrier((tokens_n, both))
    key_grad, value_grad, send_a, send_b, keep = last_block(
        which, tokens_n, grads_n, weights, last, partial_z, (key_0, value_0), middle, turned
    )
    both = chip_sum((send_a, send_b), keep)
    sum_qo = piece_sum(pieces_qo, 2 * width)
    query_grad, both, sum_qo = lax.optimization_barrier((query_grad, both, sum_qo))
    pieces_kv = lax.all_to_all(both, CHIPS, 0, 0, tiled=True)
    in_grad = bf(
        dot(query_grad, w_query, 1, 1) + dot(key_grad, w_key, 1, 1) + dot(value_grad, w_value, 1, 1)
    )
    total = count
    for axis in AXES:
        total *= lax.axis_size(axis)
    factor = 1.0 / total**0.5
    sum_kv = piece_sum(pieces_kv, 2 * width)
    summed = jnp.concatenate([sum_qo[:, :width], sum_kv, sum_qo[:, width:]], axis=1)
    return in_grad[None], grad_accum + summed * factor


def solution(mesh):
    fine = Mesh(mesh.devices.reshape(2, 2, 4, 4, 2), AXES)
    rows = P(("xh", "co"), SEQ, None)
    accum = P(AXES, None)
    return jax.shard_map(
        on_device,
        mesh=fine,
        in_specs=(rows, rows, P(), P(), P(), P(), accum),
        out_specs=(rows, accum),
        check_vma=False,
    )
```
